128 devices in a mesh: band: 4 (over z_hi, core), mem: 32 (over y, x, z_lo).
Axes of the slice: x: 4, y: 4, z: 4 (z_hi: 2, z_lo: 2; z = z_hi * 2 + z_lo), core: 2. Of those that a mesh axis runs over, the one named last changes fastest.
Arguments:
- members: bfloat16 [64, 16, 32768], P('band', None, 'mem'), may hold values from -6 to 6
- eigvecs: bfloat16 [112, 16, 32768], P('band', None, 'mem'), may hold values from -6 to 6
- control: float32 [112, 64], replicated, may hold values from -6 to 6
- columns: int32 [2048, 16], P('mem'), may hold values from 0 to 1023
- interpolation: bfloat16 [2048, 256, 512], P('mem'), may hold values from -0.375 to 0.375
- owners: int32 [2048], replicated, may hold values from 0 to 31, as said below
- innovation: float32 [32, 256, 512], P('mem'), may hold values from -6 to 6
- obs_weight: float32 [32, 256, 512], P('mem'), may hold values from 0.25 to 4
Outputs:
- gradient: float32 [112, 64], P(None, 'band')
- departures: float32 [32, 256, 512], P('mem', None, 'band')
The draws below stay inside these ranges and needn't reach their ends.
Inputs may be any that keep to these rules, and one draw needn't show every extreme that they name: `owners`: one tile sends at most 8 of its blocks to one owner, and some owner holds exactly 8 blocks from every tile.
All inputs are finite; a program needn't handle non-finite values.
Results may differ from the reference program's by a relative error of at most 0.0032.
Values may be sent and summed in bfloat16 or wider, within the bound.
No kernel may reach another device: no remote copies, remote signals or barrier semaphores. Data moves between devices by JAX's collectives and lax.ppermute only.
A program may use at most 64 MiB of HBM per device.

```python
import math
import jax
import jax.numpy as jnp
from jax import lax

MEMBERS = 64
MODES = 112
LEVELS = 16
PATCH = 16
OBS_BLOCK = 512
TILE_COLS = 1024
BLOCKS = 64
TILES = 32
GRID = 32768
CAPACITY = 8
SLOTS = 256


def draw_owners(key, part):
    base_key = jax.random.fold_in(key, 11)
    hot_key, shift_key, order_key = jax.random.split(base_key, 3)
    hottest = jax.random.randint(hot_key, (), 0, TILES)
    shifts = jax.random.randint(shift_key, (TILES,), 0, TILES - 1)
    places = jnp.arange(BLOCKS, dtype=jnp.int32)
    others = (places[None, :] - CAPACITY + shifts[:, None]) % (TILES - 1)
    chosen = jnp.where(places[None, :] < CAPACITY, hottest, (hottest + 1 + others) % TILES)
    tile_keys = jax.random.split(order_key, TILES)
    orders = jax.vmap(lambda k: jax.random.permutation(k, BLOCKS))(tile_keys)
    shuffled = jnp.take_along_axis(chosen, orders, axis=1)
    return shuffled.reshape(-1).astype(jnp.int32)


def plant(values, key, smallest, largest):
    place = [jax.random.randint(jax.random.fold_in(key, axis), (), 0, length) for axis, length in enumerate(values.shape)]
    main_axis = values.shape.index(max(values.shape))
    beside = place[:main_axis] + [(place[main_axis] + 1) % values.shape[main_axis]] + place[main_axis + 1:]
    return values.at[tuple(place)].set(smallest).at[tuple(beside)].set(largest)


def levels(key, dims, shards, least, top_value):
    def one(dim, blocks):
        heights = jax.random.uniform(jax.random.fold_in(jax.random.fold_in(key, 6), dim), (blocks,), jnp.float32, least / len(shards), top_value / len(shards))
        return jnp.repeat(jnp.exp(heights), dims[dim] // blocks).reshape((-1,) + (1,) * (len(dims) - dim - 1))

    level = one(*shards[0])
    for cut in shards[1:]:
        level = level * one(*cut)
    return level


def scatter_about(own_key, dims, deviation, reach, cuts=(), kind=jnp.bfloat16):
    loudness = levels(own_key, dims, cuts, -0.22, 0.18) if cuts else 1.0
    values = jax.random.normal(own_key, dims, jnp.float32) * deviation * loudness
    return jnp.minimum(jnp.maximum(values, -reach), reach).astype(kind)


def setup_inputs(seed: int = 0) -> dict:
    seeds = jax.random.split(jax.random.key(seed), 9)
    members = scatter_about(seeds[0], (MEMBERS, LEVELS, GRID), 1.0, 6.0, ((0, 4), (2, 32)))
    eigvecs = scatter_about(seeds[1], (MODES, LEVELS, GRID), 1.0, 6.0, ((0, 4), (2, 32)))
    control = scatter_about(seeds[2], (MODES, MEMBERS), 1.0, 6.0, (), jnp.float32)
    columns = plant(jax.random.randint(seeds[3], (TILES * BLOCKS, PATCH), 0, TILE_COLS), jax.random.fold_in(seeds[3], 1), 0, TILE_COLS - 1).astype(jnp.int32)
    interpolation = scatter_about(seeds[4], (TILES * BLOCKS, LEVELS * PATCH, OBS_BLOCK), (LEVELS * PATCH) ** -0.5, 0.375, ((0, 32),))
    owners = draw_owners(jax.random.fold_in(seeds[8], 71), 0)
    innovation = scatter_about(seeds[6], (TILES, SLOTS, OBS_BLOCK), 1.0, 6.0, ((0, 32),), jnp.float32)
    obs_weight = jnp.clip(jnp.exp(math.log(4.0) - 2.7725887 * jax.random.uniform(seeds[7], (TILES, SLOTS, OBS_BLOCK), jnp.float32) ** levels(seeds[7], (TILES, SLOTS, OBS_BLOCK), ((0, 32),), -0.2, 0.2)), 0.25, 4.0)
    return dict(members=members, eigvecs=eigvecs, control=control, columns=columns, interpolation=interpolation, owners=owners, innovation=innovation, obs_weight=obs_weight)


def tile_image(args):
    field, cols, blocks = args
    picked = field[:, cols.reshape(-1)].reshape(LEVELS, BLOCKS, PATCH)
    picked = jnp.transpose(picked, (1, 0, 2)).reshape(BLOCKS, LEVELS * PATCH)
    return jnp.einsum('jr,jro->jo', picked.astype(jnp.float32), blocks.astype(jnp.float32))

def tile_adjoint(args):
    cols, blocks, back = args
    spread = jnp.einsum('jro,jo->jr', blocks.astype(jnp.float32), back.astype(jnp.float32))
    spread = jnp.transpose(spread.reshape(BLOCKS, LEVELS, PATCH), (1, 0, 2)).reshape(LEVELS, BLOCKS * PATCH)
    return jnp.zeros((LEVELS, TILE_COLS), jnp.float32).at[:, cols.reshape(-1)].add(spread)

def reference(members, eigvecs, control, columns, interpolation, owners, innovation, obs_weight):
    scale = 1.0 / math.sqrt(MODES * MEMBERS)
    control_b = control.astype(jnp.bfloat16)
    mixed = jnp.dot(control_b.T, eigvecs.reshape(MODES, -1), preferred_element_type=jnp.float32)
    increment = scale * lax.optimization_barrier(jnp.sum(members.reshape(MEMBERS, -1).astype(jnp.float32) * mixed, axis=0))
    increment_b = increment.astype(jnp.bfloat16).reshape(LEVELS, TILES, TILE_COLS)
    col_tiles = columns.reshape(TILES, BLOCKS, PATCH)
    block_tiles = interpolation.reshape(TILES, BLOCKS, LEVELS * PATCH, OBS_BLOCK)
    image = lax.map(tile_image, (jnp.transpose(increment_b, (1, 0, 2)), col_tiles, block_tiles))
    own = owners.reshape(TILES, BLOCKS)
    order = jnp.arange(BLOCKS, dtype=jnp.int32)
    earlier = order[None, :] < order[:, None]
    same = own[:, :, None] == own[:, None, :]
    rank = lax.optimization_barrier(jnp.sum(jnp.logical_and(same, earlier[None]), axis=2)).astype(jnp.int32)
    slot = (jnp.arange(TILES, dtype=jnp.int32)[:, None] * CAPACITY + rank).astype(jnp.int32)
    slot_image = jnp.zeros((TILES, SLOTS, OBS_BLOCK), jnp.float32).at[own, slot].set(image)
    live = jnp.zeros((TILES, SLOTS), jnp.float32).at[own, slot].set(1.0)
    departures = live[:, :, None] * obs_weight * (innovation - slot_image)
    departures_b = departures.astype(jnp.bfloat16)
    back = departures_b[own, slot]
    adjoint = lax.map(tile_adjoint, (col_tiles, block_tiles, back))
    adjoint = jnp.transpose(adjoint, (1, 0, 2)).reshape(-1)
    weighted = (members.reshape(MEMBERS, -1).astype(jnp.float32) * adjoint).astype(jnp.bfloat16)
    total = jnp.dot(eigvecs.reshape(MODES, -1), weighted.T, preferred_element_type=jnp.float32)
    gradient = control - scale * total
    return (gradient, departures)
```

```python
import math

import jax
import jax.numpy as jnp
from jax import lax
from jax.experimental import pallas as pl
from jax.experimental.pallas import tpu as pltpu
from jax.sharding import PartitionSpec as P

BF = jnp.bfloat16
F32 = jnp.float32
NN = (((1,), (0,)), ((), ()))
NT = (((1,), (1,)), ((), ()))
TN = (((0,), (0,)), ((), ()))
MIB = 1024 * 1024


def dot(a, b, dims=NN):
    return lax.dot_general(a, b, dims, preferred_element_type=F32)


def parts3(x):
    hi = x.astype(BF)
    rest = x - hi.astype(F32)
    mid = rest.astype(BF)
    lo = (rest - mid.astype(F32)).astype(BF)
    return hi, mid, lo


def iota(shape, dim):
    return lax.broadcasted_iota(jnp.int32, shape, dim)


def call(body, outs, n_smem, n_vmem, flops, nbytes, scratch=(), vmem=16):
    return pl.pallas_call(
        body,
        out_shape=outs,
        in_specs=[pl.BlockSpec(memory_space=pltpu.SMEM)] * n_smem
        + [pl.BlockSpec(memory_space=pltpu.VMEM)] * n_vmem,
        out_specs=jax.tree.map(lambda _: pl.BlockSpec(memory_space=pltpu.VMEM), outs),
        scratch_shapes=list(scratch),
        compiler_params=pltpu.CompilerParams(vmem_limit_bytes=vmem * MIB),
        cost_estimate=pl.CostEstimate(flops=flops, bytes_accessed=nbytes, transcendentals=0),
    )


def shape(dims, dtype):
    return jax.ShapeDtypeStruct(dims, dtype)


def prep_body(meta, control, columns, owners, kron, onehot, place):
    band = meta[0]
    tile = meta[1]
    row = iota((448, 112), 0)
    second = (row >= 224).astype(jnp.int32)
    mode = (band ^ second) * 28 + ((row - 224 * second) >> 3)
    pick_rows = (mode == iota((448, 112), 1)).astype(F32).astype(BF)
    col = iota((64, 512), 1)
    member = (band ^ (col >> 7)) * 16 + ((col & 127) >> 3)
    pick_cols = (member == iota((64, 512), 0)).astype(F32).astype(BF)
    rows = dot(pick_rows, control[...].astype(BF)).astype(BF)
    full = dot(rows, pick_cols)
    same = (iota((448, 512), 0) & 7) == (iota((448, 512), 1) & 7)
    kron[...] = jnp.where(same, full, 0.0).astype(BF)
    t = iota((64, 1024), 1)
    cols = columns[...]
    for c in range(16):
        onehot[c * 64:(c + 1) * 64, :] = (cols[:, c:c + 1] == t).astype(F32).astype(BF)
    own_row = jnp.broadcast_to(owners[pl.ds(tile, 1), :].astype(F32), (64, 64))
    own_col = own_row.T
    earlier = iota((64, 64), 1) < iota((64, 64), 0)
    rank = jnp.sum(jnp.where((own_row == own_col) & earlier, 1.0, 0.0), axis=1, keepdims=True)
    target = (own_col[:, :1] * 8.0 + rank).astype(jnp.int32)
    place[...] = (target == iota((64, 256), 1)).astype(F32).astype(BF)


def select_body(place, got, innov, weight):
    x = got[...]
    sel = place[...]
    for out, a in ((innov, x[:, :8].reshape(256, 128)), (weight, x[:, 8:].reshape(256, 128))):
        hi, mid, lo = parts3(a)
        out[...] = dot(sel, hi) + dot(sel, mid) + dot(sel, lo)


def increment_body(scale, kron, m0, m1, m2, m3, e0, e1, out):
    for g in range(0, 1024, 256):
        cut = slice(g, g + 256)
        mixed = None
        for p, m in enumerate((m0, m1, m2, m3)):
            term = dot(kron[:, p * 128:(p + 1) * 128], m[:, cut])
            mixed = term if mixed is None else mixed + term
        total = jnp.sum((mixed[:224] * e0[:, cut].astype(F32)).reshape(28, 8, 256), axis=0)
        total = total + jnp.sum((mixed[224:] * e1[:, cut].astype(F32)).reshape(28, 8, 256), axis=0)
        out[:, cut] = total * scale


def obs_body(meta, inc_my, inc_mt, onehot, place, innov, weight, interp, adj_my, adj_mt, slots, picked, depb, spread):
    first = (meta[0] & 1) == 0
    mine = inc_my[...].astype(F32)
    mate = inc_mt[...].astype(F32)
    inc = jnp.concatenate([jnp.where(first, mine, mate), jnp.where(first, mate, mine)], axis=0).astype(BF)
    picks = dot(onehot[...], inc, NT)
    by_col = jnp.concatenate([picks[c * 64:(c + 1) * 64] for c in range(16)], axis=1).astype(BF)
    r0 = iota((256, 256), 0)
    r1 = iota((256, 256), 1)
    swap = (((r0 & 15) * 16 + (r0 >> 4)) == r1).astype(F32).astype(BF)
    picked[...] = dot(by_col, swap).astype(BF)
    rows = iota((16, 128), 0)
    rows2 = iota((16, 256), 0)
    image = []
    for b in range(4):
        lhs = picked[b * 16:(b + 1) * 16, :]
        acc = jnp.zeros((16, 128), F32)
        for i in range(16):
            acc = jnp.where(rows == i, dot(lhs, interp[b * 16 + i]), acc)
        image.append(acc)
    image = jnp.concatenate(image, axis=0)
    dep = weight[...] * (innov[...] - image)
    depb[...] = dep.astype(BF)
    for b in range(4):
        lhs = depb[b * 16:(b + 1) * 16, :]
        acc = jnp.zeros((16, 256), F32)
        for i in range(16):
            acc = jnp.where(rows2 == i, dot(lhs, interp[b * 16 + i], NT), acc)
        spread[b * 16:(b + 1) * 16, :] = acc
    x = spread[...]
    hi = x.astype(BF)
    lo = (x - hi.astype(F32)).astype(BF)
    terms = []
    for part in (hi, lo):
        turned = dot(swap, part, NT)
        terms.append(jnp.concatenate([turned[c * 16:(c + 1) * 16] for c in range(16)], axis=1))
    both = dot(jnp.concatenate(terms, axis=0).astype(BF), onehot[...])
    adj = both[:16] + both[16:]
    adj_my[...] = jnp.where(first, adj[:8], adj[8:])
    adj_mt[...] = jnp.where(first, adj[8:], adj[:8])
    sel = place[...]
    hi, mid, lo = parts3(dep)
    slots[...] = dot(sel, hi, TN) + dot(sel, mid, TN) + dot(sel, lo, TN)


def gradient_body(a0, a1, m0, m1, m2, m3, e0, e1, out_my, out_mt):
    adj = a0[...] + a1[...]
    wide = jnp.broadcast_to(adj[None], (16, 8, 1024)).reshape(128, 1024)
    same = (iota((224, 128), 0) & 7) == (iota((224, 128), 1) & 7)
    tops, lows = [], []
    for m in (m0, m1, m2, m3):
        weighted = (m[...].astype(F32) * wide).astype(BF)
        for e, side in ((e0, tops), (e1, lows)):
            full = jnp.where(same, dot(e[...], weighted, NT), 0.0)
            side.append(jnp.sum(full.reshape(28, 8, 128), axis=1))
    sel = ((iota((256, 32), 0) >> 3) == iota((256, 32), 1)).astype(F32).astype(BF)
    for out, p, q in ((out_my, 0, 2), (out_mt, 1, 3)):
        x = jnp.concatenate([
            jnp.concatenate([tops[p], tops[q]], axis=1),
            jnp.concatenate([lows[p], lows[q]], axis=1),
        ], axis=0)
        hi, mid, lo = parts3(x)
        out[...] = dot(hi, sel) + dot(mid, sel) + dot(lo, sel)


def pack_body(keep, came, slots, out):
    full = jnp.concatenate([keep[...], came[...]], axis=0)
    flat = jnp.concatenate(
        [full[i * 16:(i + 1) * 16] for i in range(7)] + [jnp.zeros((16, 16), F32)], axis=1
    )
    out[:, :8, :] = slots[...].reshape(32, 8, 128)
    out[:, 8:, :] = jnp.broadcast_to(flat[None], (32, 16, 128))


def final_body(scale, meta, got, control, gradient, departures):
    band = meta[0]
    departures[...] = got[:, :8, :].reshape(1, 256, 128)
    flat = jnp.sum(got[:, 8:, :], axis=0)
    total = jnp.concatenate([flat[:, i * 16:(i + 1) * 16] for i in range(7)], axis=0)
    r = iota((112, 112), 0)
    block = (r >= 28).astype(jnp.int32) + (r >= 56).astype(jnp.int32) + (r >= 84).astype(jnp.int32)
    source = (band ^ block) * 28 + (r - 28 * block)
    order = (source == iota((112, 112), 1)).astype(F32).astype(BF)
    hi, mid, lo = parts3(total)
    total = dot(order, hi) + dot(order, mid) + dot(order, lo)
    own = (iota((64, 16), 0) == band * 16 + iota((64, 16), 1)).astype(F32).astype(BF)
    hi, mid, lo = parts3(control[...])
    mine = dot(hi, own) + dot(mid, own) + dot(lo, own)
    gradient[...] = mine - scale * total


def per_device(members, eigvecs, control, columns, interpolation, owners, innovation, obs_weight):
    band = lax.axis_index("band")
    tile = lax.axis_index("mem")
    core = band & 1
    scale = 1.0 / math.sqrt(112 * 64)
    meta = jnp.stack([band, tile]).astype(jnp.int32)

    def over(x, bit):
        return lax.ppermute(x, "band", [(i, i ^ bit) for i in range(4)])

    def half(x, which):
        return lax.dynamic_slice_in_dim(x, which * 8, 8, 1).reshape(-1, 1024)

    m_mt = half(members, 1 - core)
    m_my = half(members, core)
    m3 = over(m_mt, 3)
    m2 = over(m_my, 2)
    e_mt = half(eigvecs, 1 - core)
    m1 = over(m_mt, 1)
    e1 = over(e_mt, 1)
    e0 = half(eigvecs, core)

    quarter = lambda x, d: lax.dynamic_slice_in_dim(x, band * 128, 128, d)
    sent = jnp.concatenate(
        [quarter(innovation[0], 1).reshape(32, 8, 128), quarter(obs_weight[0], 1).reshape(32, 8, 128)], axis=1
    )
    got = lax.all_to_all(sent, "mem", split_axis=0, concat_axis=0, tiled=True)
    interp = quarter(interpolation, 2)

    kron, onehot, place = call(
        prep_body,
        (shape((448, 512), BF), shape((1024, 1024), BF), shape((64, 256), BF)),
        1, 3, 10 ** 8, 3 * 10 ** 6,
    )(meta, control, columns, owners.reshape(32, 64))
    innov, weight = call(
        select_body, (shape((64, 128), F32), shape((64, 128), F32)), 0, 2, 10 ** 7, 4 * 10 ** 5
    )(place, got)

    part = call(
        lambda *refs: increment_body(scale, *refs), shape((8, 1024), F32), 0, 7, 5 * 10 ** 8, 2 * 10 ** 6
    )(kron, m_my, m1, m2, m3, e0, e1)
    inc_my = (part + over(part, 2)).astype(BF)
    inc_mt = over(inc_my, 1)

    adj_my, adj_mt, slots = call(
        obs_body,
        (shape((8, 1024), F32), shape((8, 1024), F32), shape((256, 128), F32)),
        1, 7, 10 ** 9, 8 * 10 ** 6,
        scratch=(pltpu.VMEM((64, 256), BF), pltpu.VMEM((64, 128), BF), pltpu.VMEM((64, 256), F32)),
    )(meta, inc_my, inc_mt, onehot, place, innov, weight, interp)
    adj = adj_my + over(adj_mt, 1)

    g_my, g_mt = call(
        gradient_body, (shape((56, 32), F32), shape((56, 32), F32)), 0, 8, 5 * 10 ** 8, 2 * 10 ** 6
    )(adj, over(adj, 2), m_my, m1, m2, m3, e0, e1)
    came = over(g_mt, 1)
    both = g_my + jnp.concatenate([came[28:], came[:28]], axis=0)
    other = over(both[:, 16:], 2)

    payload = call(pack_body, shape((32, 24, 128), F32), 0, 3, 10 ** 5, 6 * 10 ** 5)(both[:, :16], other, slots)
    arrived = lax.all_to_all(payload, "mem", split_axis=0, concat_axis=0, tiled=True)
    gradient, departures = call(
        lambda *refs: final_body(scale, *refs), (shape((112, 16), F32), shape((1, 256, 128), F32)),
        1, 2, 10 ** 6, 6 * 10 ** 5,
    )(meta, arrived, control)
    return (gradient, departures)


def solution(mesh):
    return jax.shard_map(
        per_device,
        mesh=mesh,
        in_specs=(
            P("band", None, "mem"),
            P("band", None, "mem"),
            P(),
            P("mem", None),
            P("mem", None, None),
            P(),
            P("mem", None, None),
            P("mem", None, None),
        ),
        out_specs=(P(None, "band"), P("mem", None, "band")),
        check_vma=False,
    )
```

```python
import math

import jax
import jax.numpy as jnp
from jax import lax
from jax.experimental import pallas as pl
from jax.experimental.pallas import tpu as pltpu
from jax.sharding import PartitionSpec as P

BF = jnp.bfloat16
F32 = jnp.float32
NN = (((1,), (0,)), ((), ()))
NT = (((1,), (1,)), ((), ()))
TN = (((0,), (0,)), ((), ()))
MIB = 1024 * 1024
VM = pl.BlockSpec(memory_space=pltpu.VMEM)
ANY = pl.BlockSpec(memory_space=pl.ANY)


def dot(a, b, dims=NN):
    return lax.dot_general(a, b, dims, preferred_element_type=F32)


def parts3(x):
    hi = x.astype(BF)
    rest = x - hi.astype(F32)
    mid = rest.astype(BF)
    lo = (rest - mid.astype(F32)).astype(BF)
    return hi, mid, lo


def iota(dims, dim):
    return lax.broadcasted_iota(jnp.int32, dims, dim)


def ones_where(cond):
    return cond.astype(F32).astype(BF)


def shape(dims, dtype):
    return jax.ShapeDtypeStruct(dims, dtype)


def call(body, ins, outs, flops, nbytes, scratch=(), vmem=16):
    return pl.pallas_call(
        body,
        out_shape=tuple(o for o, _ in outs),
        in_specs=list(ins),
        out_specs=tuple(s for _, s in outs),
        scratch_shapes=list(scratch),
        compiler_params=pltpu.CompilerParams(vmem_limit_bytes=vmem * MIB),
        cost_estimate=pl.CostEstimate(flops=flops, bytes_accessed=nbytes, transcendentals=0),
    )


def start_all(copies):
    for c in copies:
        c.start()
    return copies


def wait_all(copies):
    for c in copies:
        c.wait()


def halves_copies(src, mine, mate, sem, at):
    core = lax.axis_index("band") & 1
    lo = pl.multiple_of(core * 8, 8)
    hi = pl.multiple_of(8 - core * 8, 8)
    return [
        pltpu.make_async_copy(src.at[:, pl.ds(hi, 8), :], mate, sem.at[at]),
        pltpu.make_async_copy(src.at[:, pl.ds(lo, 8), :], mine, sem.at[at + 1]),
    ]


def split_body(src, mine, mate, sem):
    wait_all(start_all(halves_copies(src, mine, mate, sem, 0)))


def quarter_at(side):
    core = lax.axis_index("band") & 1
    return pl.ds(pl.multiple_of((core + 2 * side) * 128, 128), 128)


def load_body(eig, innovation, obs_weight, owners, mine, mate, payload, innov_own, live_own, iv, sem):
    copies = []
    for n, a in enumerate((innovation, obs_weight)):
        for side in range(2):
            copies.append(pltpu.make_async_copy(
                a.at[0, :, quarter_at(side)], iv.at[n, :, side * 128:(side + 1) * 128], sem.at[2 + 2 * n + side]))
    slices = halves_copies(eig, mine, mate, sem, 0)
    start_all(slices)
    start_all(copies)
    tile = lax.axis_index("mem")
    own = owners[...].astype(F32)
    wait_all(copies)
    for n in range(2):
        payload[:, n * 8:(n + 1) * 8, :] = iv[n].reshape(32, 8, 256).astype(BF)
    hit = jnp.where(own == tile.astype(F32), 1.0, 0.0)
    r = iota((256, 16), 0)
    pair = ones_where((r >> 4) == iota((256, 16), 1))
    both = dot(pair, hit.astype(BF))
    odd = (iota((256, 128), 0) >> 3) & 1
    side = jnp.where((iota((256, 128), 1) >> 6) == odd, both, 0.0)
    count = jnp.sum(side, axis=1, keepdims=True)
    live = jnp.where((iota((256, 1), 0) & 7).astype(F32) < count, 1.0, 0.0)
    high = (lax.axis_index("band") >> 1) == 1
    innov_own[...] = jnp.where(high, iv[0, :, 128:], iv[0, :, :128])
    live_own[...] = live * jnp.where(high, iv[1, :, 128:], iv[1, :, :128])
    wait_all(slices)


def prep_body(control_t, columns_t, owners, interpolation, kron, onehot, place, interp, sem):
    copies = start_all([
        pltpu.make_async_copy(
            interpolation.at[:, :, quarter_at(side)], interp.at[:, :, side * 128:(side + 1) * 128], sem.at[side])
        for side in range(2)
    ])
    band = lax.axis_index("band")
    tile = lax.axis_index("mem")
    row = iota((448, 112), 0)
    second = (row >= 224).astype(jnp.int32)
    mode = (band ^ second) * 28 + ((row - 224 * second) >> 3)
    pick_rows = ones_where(mode == iota((448, 112), 1))
    col = iota((64, 512), 1)
    member = (band ^ (col >> 7)) * 16 + ((col & 127) >> 3)
    pick_cols = ones_where(member == iota((64, 512), 0))
    rows = dot(pick_rows, control_t[...].astype(BF), NT).astype(BF)
    full = dot(rows, pick_cols)
    same = (iota((448, 512), 0) & 7) == (iota((448, 512), 1) & 7)
    kron[...] = jnp.where(same, full, 0.0).astype(BF)
    t = iota((64, 1024), 1)
    cols = columns_t[...].astype(F32).T.astype(jnp.int32)
    for c in range(16):
        onehot[c * 64:(c + 1) * 64, :] = ones_where(cols[:, c:c + 1] == t)
    pair = owners[pl.ds(tile >> 1, 1), :].astype(F32)
    own = jnp.where((tile & 1) == 1, pair[:, 64:], pair[:, :64])
    own_row = jnp.broadcast_to(own, (64, 64))
    own_col = own_row.T
    earlier = iota((64, 64), 1) < iota((64, 64), 0)
    rank = jnp.sum(jnp.where((own_row == own_col) & earlier, 1.0, 0.0), axis=1, keepdims=True)
    target = (own_col[:, :1] * 8.0 + rank).astype(jnp.int32)
    place[...] = ones_where(target == iota((64, 256), 1))
    wait_all(copies)


def select_body(place, got, innov, weight):
    x = got[...].astype(F32)
    sel = place[...]
    innov[...] = dot(sel, x[:, :8].reshape(256, 256).astype(BF))
    weight[...] = dot(sel, x[:, 8:].reshape(256, 256).astype(BF))


def increment_body(scale, kron, m0, m1, m2, m3, e0, e1, _, out):
    for g in range(0, 1024, 256):
        cut = slice(g, g + 256)
        mixed = None
        for p, m in enumerate((m0, m1, m2, m3)):
            term = dot(kron[:, p * 128:(p + 1) * 128], m[:, cut])
            mixed = term if mixed is None else mixed + term
        total = jnp.sum((mixed[:224] * e0[:, cut].astype(F32)).reshape(28, 8, 256), axis=0)
        total = total + jnp.sum((mixed[224:] * e1[:, cut].astype(F32)).reshape(28, 8, 256), axis=0)
        out[:, cut] = total * scale


def obs_body(p0, p1, p2, p3, onehot, place, innov, weight, interp, adj_my, adj_mt, slots, picked, depb, spread):
    band = lax.axis_index("band")
    first = (band & 1) == 0
    mine = p0[...] + p2[...]
    mate = p1[...] + p3[...]
    inc = jnp.concatenate([jnp.where(first, mine, mate), jnp.where(first, mate, mine)], axis=0).astype(BF)
    picks = dot(onehot[...], inc, NT)
    by_col = jnp.concatenate([picks[c * 64:(c + 1) * 64] for c in range(16)], axis=1).astype(BF)
    r0 = iota((256, 256), 0)
    r1 = iota((256, 256), 1)
    swap = ones_where(((r0 & 15) * 16 + (r0 >> 4)) == r1)
    picked[...] = dot(by_col, swap).astype(BF)
    rows = iota((16, 256), 0)
    image = []
    for b in range(4):
        lhs = picked[b * 16:(b + 1) * 16, :]
        acc = jnp.zeros((16, 256), F32)
        for i in range(16):
            acc = jnp.where(rows == i, dot(lhs, interp[b * 16 + i]), acc)
        image.append(acc)
    image = jnp.concatenate(image, axis=0)
    depb[...] = (weight[...] * (innov[...] - image)).astype(BF)
    for b in range(4):
        lhs = depb[b * 16:(b + 1) * 16, :]
        acc = jnp.zeros((16, 256), F32)
        for i in range(16):
            acc = jnp.where(rows == i, dot(lhs, interp[b * 16 + i], NT), acc)
        spread[b * 16:(b + 1) * 16, :] = acc
    x = spread[...]
    hi = x.astype(BF)
    lo = (x - hi.astype(F32)).astype(BF)
    terms = []
    for part in (hi, lo):
        turned = dot(swap, part, NT)
        terms.append(jnp.concatenate([turned[c * 16:(c + 1) * 16] for c in range(16)], axis=1))
    both = dot(jnp.concatenate(terms, axis=0).astype(BF), onehot[...])
    adj = both[:16] + both[16:]
    adj_my[...] = jnp.where(first, adj[:8], adj[8:])
    adj_mt[...] = jnp.where(first, adj[8:], adj[:8])
    sel = place[...]
    hi, mid, lo = parts3(jnp.where((band >> 1) == 0, image[:, :128], image[:, 128:]))
    slots[...] = dot(sel, hi, TN) + dot(sel, mid, TN) + dot(sel, lo, TN)


def gradient_body(a0, a1, m0, m1, m2, m3, e0, e1, g0, g1, g2, g3):
    band = lax.axis_index("band")
    adj = a0[...] + a1[...]
    wide = jnp.broadcast_to(adj[None], (16, 8, 1024)).reshape(128, 1024)
    same = (iota((128, 224), 0) & 7) == (iota((128, 224), 1) & 7)
    mode = iota((224, 128), 0) >> 3
    lane = iota((224, 128), 1)
    sel0 = ones_where(mode + band * 28 == lane)
    sel1 = ones_where(mode + (band ^ 1) * 28 == lane)
    for m, g in ((m3, g3), (m2, g2), (m1, g1), (m0, g0)):
        weighted = (m[...].astype(F32) * wide).astype(BF)
        total = None
        for e, sel in ((e0, sel0), (e1, sel1)):
            full = jnp.where(same, dot(weighted, e[...], NT), 0.0)
            hi, mid, lo = parts3(jnp.sum(full.reshape(16, 8, 224), axis=1))
            term = dot(hi, sel) + dot(mid, sel) + dot(lo, sel)
            total = term if total is None else total + term
        g[...] = total


def pack_body(g0, g1, g2, g3, slots, out):
    total = (g0[...] + g1[...]) + (g2[...] + g3[...])
    out[:, :8, :] = slots[...].reshape(32, 8, 128)
    out[:, 8:, :] = jnp.broadcast_to(total[None], (32, 16, 128))


def final_body(scale, got, control_t, innov, live, gradient_t, departures):
    band = lax.axis_index("band")
    image = got[:, :8, :].reshape(256, 128)
    departures[...] = (live[...] * (innov[...] - image)).reshape(1, 256, 128)
    total = jnp.sum(got[:, 8:, :], axis=0)[:, :112]
    own = ones_where(iota((16, 64), 1) == band * 16 + iota((16, 64), 0))
    hi, mid, lo = parts3(control_t[...])
    gradient_t[...] = dot(own, hi) + dot(own, mid) + dot(own, lo) - scale * total


def per_device(members, eigvecs, control, columns, interpolation, owners, innovation, obs_weight):
    scale = 1.0 / math.sqrt(112 * 64)
    owners = owners.reshape(16, 128)

    def over(x, bit):
        return lax.ppermute(x, "band", [(i, i ^ bit) for i in range(4)])

    dma = pltpu.SemaphoreType.DMA
    m_my, m_mt = call(
        split_body, [ANY], [(shape((16, 8, 1024), BF), ANY)] * 2, 0, 10 ** 6, [dma((2,))]
    )(members)
    m_my, m_mt = m_my.reshape(128, 1024), m_mt.reshape(128, 1024)
    m3 = over(m_mt, 3)
    m2 = over(m_my, 2)
    m1 = over(m_mt, 1)

    e_my, e_mt, payload, innov_own, live_own = call(
        load_body,
        [ANY, ANY, ANY, VM],
        [(shape((28, 8, 1024), BF), ANY)] * 2 + [(shape((32, 16, 256), BF), VM)] + [(shape((256, 128), F32), VM)] * 2,
        10 ** 6, 5 * 10 ** 6,
        [pltpu.VMEM((2, 256, 256), F32), dma((6,))],
    )(eigvecs, innovation, obs_weight, owners)
    e0, e_mt = e_my.reshape(224, 1024), e_mt.reshape(224, 1024)
    e1 = over(e_mt, 1)
    got = lax.all_to_all(payload, "mem", split_axis=0, concat_axis=0, tiled=True)

    kron, onehot, place, interp = call(
        prep_body,
        [VM, VM, VM, ANY],
        [(shape((448, 512), BF), VM), (shape((1024, 1024), BF), VM), (shape((64, 256), BF), VM),
         (shape((64, 256, 256), BF), VM)],
        10 ** 8, 20 * 10 ** 6, [dma((2,))],
    )(control.T, columns.T, owners, interpolation)
    innov, weight = call(
        select_body, [VM] * 2, [(shape((64, 256), F32), VM)] * 2, 10 ** 7, 4 * 10 ** 5
    )(place, got)

    (part,) = call(
        lambda *refs: increment_body(scale, *refs), [VM] * 7 + [ANY], [(shape((8, 1024), F32), VM)],
        5 * 10 ** 8, 2 * 10 ** 6,
    )(kron, m_my, m1, m2, m3, e0, e1, innov)
    p3 = over(part, 3)
    p2 = over(part, 2)
    p1 = over(part, 1)

    adj_my, adj_mt, slots = call(
        obs_body, [VM] * 9,
        [(shape((8, 1024), F32), VM)] * 2 + [(shape((256, 128), F32), VM)],
        10 ** 9, 12 * 10 ** 6,
        [pltpu.VMEM((64, 256), BF), pltpu.VMEM((64, 256), BF), pltpu.VMEM((64, 256), F32)],
    )(part, p1, p2, p3, onehot, place, innov, weight, interp)

    g0, g1, g2, g3 = call(
        gradient_body, [VM] * 8, [(shape((16, 128), F32), VM)] * 4, 5 * 10 ** 8, 2 * 10 ** 6
    )(adj_my, over(adj_mt, 1), m_my, m1, m2, m3, e0, e1)
    r3 = over(g3, 3)
    r2 = over(g2, 2)
    r1 = over(g1, 1)

    (sent,) = call(
        pack_body, [VM] * 5, [(shape((32, 24, 128), F32), VM)], 10 ** 5, 6 * 10 ** 5
    )(g0, r1, r2, r3, slots)
    arrived = lax.all_to_all(sent, "mem", split_axis=0, concat_axis=0, tiled=True)
    gradient_t, departures = call(
        lambda *refs: final_body(scale, *refs), [VM] * 4,
        [(shape((16, 112), F32), VM), (shape((1, 256, 128), F32), VM)], 10 ** 6, 6 * 10 ** 5,
    )(arrived, control.T, innov_own, live_own)
    return (gradient_t.T, departures)


def solution(mesh):
    return jax.shard_map(
        per_device,
        mesh=mesh,
        in_specs=(
            P("band", None, "mem"),
            P("band", None, "mem"),
            P(),
            P("mem", None),
            P("mem", None, None),
            P(),
            P("mem", None, None),
            P("mem", None, None),
        ),
        out_specs=(P(None, "band"), P("mem", None, "band")),
        check_vma=False,
    )
```

```python
import math

import jax
import jax.numpy as jnp
from jax import lax
from jax.experimental import pallas as pl
from jax.experimental.pallas import tpu as pltpu
from jax.sharding import PartitionSpec as P

BF = jnp.bfloat16
F32 = jnp.float32
NN = (((1,), (0,)), ((), ()))
NT = (((1,), (1,)), ((), ()))
TN = (((0,), (0,)), ((), ()))
MIB = 1024 * 1024
VM = pl.BlockSpec(memory_space=pltpu.VMEM)
ANY = pl.BlockSpec(memory_space=pl.ANY)
HB = pl.BlockSpec(memory_space=pltpu.HBM)


def dot(a, b, dims=NN):
    return lax.dot_general(a, b, dims, preferred_element_type=F32)


def parts3(x):
    hi = x.astype(BF)
    rest = x - hi.astype(F32)
    mid = rest.astype(BF)
    lo = (rest - mid.astype(F32)).astype(BF)
    return hi, mid, lo


def iota(dims, dim):
    return lax.broadcasted_iota(jnp.int32, dims, dim)


def ones_where(cond):
    return cond.astype(F32).astype(BF)


def shape(dims, dtype):
    return jax.ShapeDtypeStruct(dims, dtype)


def in_hbm(x):
    return pltpu.with_memory_space_constraint(x, pltpu.HBM)


def in_vmem(x):
    return pltpu.with_memory_space_constraint(x, pltpu.VMEM)


def call(body, ins, outs, flops, nbytes, scratch=(), vmem=16):
    return pl.pallas_call(
        body,
        out_shape=tuple(o for o, _ in outs),
        in_specs=list(ins),
        out_specs=tuple(s for _, s in outs),
        scratch_shapes=list(scratch),
        compiler_params=pltpu.CompilerParams(vmem_limit_bytes=vmem * MIB),
        cost_estimate=pl.CostEstimate(flops=flops, bytes_accessed=nbytes, transcendentals=0),
    )


def start_all(copies):
    for c in copies:
        c.start()
    return copies


def wait_all(copies):
    for c in copies:
        c.wait()


def halves_copies(src, mine, mate, sem, at):
    core = lax.axis_index("band") & 1
    lo = pl.multiple_of(core * 8, 8)
    hi = pl.multiple_of(8 - core * 8, 8)
    return [
        pltpu.make_async_copy(src.at[:, pl.ds(hi, 8), :], mate, sem.at[at]),
        pltpu.make_async_copy(src.at[:, pl.ds(lo, 8), :], mine, sem.at[at + 1]),
    ]


def quarter_at(side):
    core = lax.axis_index("band") & 1
    return pl.ds(pl.multiple_of((core + 2 * side) * 128, 128), 128)


def load_body(mem, eig, innovation, obs_weight, m_mine, m_mate, e_mine, e_mate, payload, iv, sem):
    slices = start_all(halves_copies(mem, m_mine, m_mate, sem, 0))
    copies = start_all([
        pltpu.make_async_copy(
            a.at[0, :, quarter_at(side)], iv.at[n, :, side * 128:(side + 1) * 128], sem.at[4 + 2 * n + side])
        for n, a in enumerate((innovation, obs_weight)) for side in range(2)
    ])
    slices += start_all(halves_copies(eig, e_mine, e_mate, sem, 2))
    wait_all(copies)
    for n in range(2):
        payload[:, n * 8:(n + 1) * 8, :] = iv[n].reshape(32, 8, 256).astype(BF)
    wait_all(slices)


def increment_of(scale, kron, members, eig, cut):
    mixed = dot(kron, members[:, cut])
    return scale * jnp.sum((mixed * eig[:, cut].astype(F32)).reshape(56, 8, 256), axis=0)


def increment_own(scale, control_t, ma, mb, ea, eb, out, kron, ct, members, eig, sem):
    get = start_all([
        pltpu.make_async_copy(a, b, sem.at[n]) for n, (a, b) in enumerate((
            (control_t, ct), (ma, members.at[:128]), (mb, members.at[128:]), (ea, eig.at[:224]), (eb, eig.at[224:])))
    ])
    band = lax.axis_index("band")
    row = iota((448, 112), 0)
    second = (row >= 224).astype(jnp.int32)
    mode = (band ^ second) * 28 + ((row - 224 * second) >> 3)
    pick_rows = ones_where(mode == iota((448, 112), 1))
    col = iota((64, 512), 1)
    member = (band ^ (col >> 7)) * 16 + ((col & 127) >> 3)
    pick_cols = ones_where(member == iota((64, 512), 0))
    same = (iota((448, 512), 0) & 7) == (iota((448, 512), 1) & 7)
    get[0].wait()
    rows = dot(pick_rows, ct[...].astype(BF), NT).astype(BF)
    full = jnp.where(same, dot(rows, pick_cols), 0.0).astype(BF)
    kron[...] = full[:, 256:]
    wait_all(get[1:])
    for g in range(0, 1024, 256):
        cut = slice(g, g + 256)
        out[:, cut] = increment_of(scale, full[:, :256], members, eig, cut)


def increment_other(scale, kron_in, before_in, m0, m1, m2, m3, ea, eb, _, out, eig, members, kron, before, sem):
    first = start_all([pltpu.make_async_copy(kron_in, kron, sem.at[0]), pltpu.make_async_copy(before_in, before, sem.at[1])])
    chunks = [slice(g, g + 256) for g in range(0, 1024, 256)]
    later = [
        start_all([
            pltpu.make_async_copy(a.at[:, cut], b.at[rows, cut], sem.at[2 + 4 * n + i]) for i, (a, b, rows) in enumerate((
                (m2, members, slice(256, 384)), (m3, members, slice(384, 512)),
                (ea, eig, slice(0, 224)), (eb, eig, slice(224, 448))))
        ]) for n, cut in enumerate(chunks)
    ]
    last = start_all([
        pltpu.make_async_copy(m0, members.at[:128], sem.at[18]), pltpu.make_async_copy(m1, members.at[128:256], sem.at[19])])
    wait_all(first)
    for cut, get in zip(chunks, later):
        wait_all(get)
        out[:, cut] = before[:, cut] + increment_of(scale, kron[...], members.at[256:], eig, cut)
    wait_all(last)


def prep_body(columns_t, owners_in, interpolation, got_in, innovation, obs_weight, _,
              onehot, place, interp, innov, weight, innov_own, live_own,
              cols_s, own_s, got, sem):
    band = lax.axis_index("band")
    tile = lax.axis_index("mem")
    quarter = pl.ds(pl.multiple_of(band * 128, 128), 128)
    small = [(columns_t, cols_s), (owners_in, own_s), (got_in, got)]
    mid = [(innovation.at[0, :, quarter], innov_own), (obs_weight.at[0, :, quarter], live_own)]
    big = [(interpolation.at[:, :, quarter_at(side)], interp.at[:, :, side * 128:(side + 1) * 128]) for side in range(2)]
    copies = start_all([pltpu.make_async_copy(a, b, sem.at[n]) for n, (a, b) in enumerate(small + mid + big)])
    wait_all(copies[:3])
    t = iota((64, 1024), 1)
    cols = cols_s[...].astype(F32).T.astype(jnp.int32)
    for c in range(16):
        onehot[c * 64:(c + 1) * 64, :] = ones_where(cols[:, c:c + 1] == t)
    pair = own_s[pl.ds(tile >> 1, 1), :].astype(F32)
    own = jnp.where((tile & 1) == 1, pair[:, 64:], pair[:, :64])
    own_row = jnp.broadcast_to(own, (64, 64))
    own_col = own_row.T
    earlier = iota((64, 64), 1) < iota((64, 64), 0)
    rank = jnp.sum(jnp.where((own_row == own_col) & earlier, 1.0, 0.0), axis=1, keepdims=True)
    target = (own_col[:, :1] * 8.0 + rank).astype(jnp.int32)
    sel = ones_where(target == iota((64, 256), 1))
    place[...] = sel
    x = got[...].astype(F32)
    innov[...] = dot(sel, x[:, :8].reshape(256, 256).astype(BF))
    weight[...] = dot(sel, x[:, 8:].reshape(256, 256).astype(BF))
    hit = ones_where(own_s[...] == tile)
    pair = ones_where((iota((256, 16), 0) >> 4) == iota((256, 16), 1))
    odd = (iota((256, 128), 0) >> 3) & 1
    side = jnp.where((iota((256, 128), 1) >> 6) == odd, dot(pair, hit), 0.0)
    count = jnp.sum(side, axis=1, keepdims=True)
    live = jnp.where((iota((256, 1), 0) & 7).astype(F32) < count, 1.0, 0.0)
    wait_all(copies[3:5])
    live_own[...] = live * live_own[...]
    wait_all(copies[5:])


def add_body(a, b, _, out):
    out[...] = (a[...] + b[...]).astype(BF)


def obs_body(inc_my, inc_mt, onehot, place, innov, weight, interp, adj_my, adj_mt, slots, picked, depb, spread):
    band = lax.axis_index("band")
    first = (band & 1) == 0
    mine = inc_my[...].astype(F32)
    mate = inc_mt[...].astype(F32)
    inc = jnp.concatenate([jnp.where(first, mine, mate), jnp.where(first, mate, mine)], axis=0).astype(BF)
    picks = dot(onehot[...], inc, NT)
    by_col = jnp.concatenate([picks[c * 64:(c + 1) * 64] for c in range(16)], axis=1).astype(BF)
    r0 = iota((256, 256), 0)
    r1 = iota((256, 256), 1)
    swap = ones_where(((r0 & 15) * 16 + (r0 >> 4)) == r1)
    picked[...] = dot(by_col, swap).astype(BF)
    rows = iota((16, 256), 0)
    image = []
    for b in range(4):
        lhs = picked[b * 16:(b + 1) * 16, :]
        acc = jnp.zeros((16, 256), F32)
        for i in range(16):
            acc = jnp.where(rows == i, dot(lhs, interp[b * 16 + i]), acc)
        image.append(acc)
    image = jnp.concatenate(image, axis=0)
    depb[...] = (weight[...] * (innov[...] - image)).astype(BF)
    for b in range(4):
        lhs = depb[b * 16:(b + 1) * 16, :]
        acc = jnp.zeros((16, 256), F32)
        for i in range(16):
            acc = jnp.where(rows == i, dot(lhs, interp[b * 16 + i], NT), acc)
        spread[b * 16:(b + 1) * 16, :] = acc
    x = spread[...]
    hi = x.astype(BF)
    lo = (x - hi.astype(F32)).astype(BF)
    terms = []
    for part in (hi, lo):
        turned = dot(swap, part, NT)
        terms.append(jnp.concatenate([turned[c * 16:(c + 1) * 16] for c in range(16)], axis=1))
    both = dot(jnp.concatenate(terms, axis=0).astype(BF), onehot[...])
    adj = both[:16] + both[16:]
    adj_my[...] = jnp.where(first, adj[:8], adj[8:])
    adj_mt[...] = jnp.where(first, adj[8:], adj[:8])
    sel = place[...]
    hi, mid, lo = parts3(jnp.where((band >> 1) == 0, image[:, :128], image[:, 128:]))
    slots[...] = dot(sel, hi, TN) + dot(sel, mid, TN) + dot(sel, lo, TN)


def gradient_body(a0, a1, eig, members, mate, mine):
    first = (lax.axis_index("band") & 1) == 0
    adj = a0[...] + a1[...]
    wide = jnp.broadcast_to(adj[None], (16, 8, 1024)).reshape(128, 1024)
    same = (iota((448, 256), 0) & 7) == (iota((448, 256), 1) & 7)
    sel = ones_where((iota((32, 256), 1) >> 3) == iota((32, 256), 0))
    for a, b, g in ((1, 3, mate), (0, 2, mine)):
        weighted = jnp.concatenate(
            [(members[p * 128:(p + 1) * 128].astype(F32) * wide).astype(BF) for p in (a, b)], axis=0)
        full = jnp.where(same, dot(eig[...], weighted, NT), 0.0)
        own = jnp.sum(full.reshape(56, 8, 256), axis=1)
        own = jnp.where(first, own, jnp.concatenate([own[28:], own[:28]], axis=0))
        hi, mid, lo = parts3(own)
        g[...] = dot(sel, hi, NT) + dot(sel, mid, NT) + dot(sel, lo, NT)


def pack_body(mine, came, slots, out):
    total = mine[...] + came[...]
    gap = jnp.zeros((8, 8), F32)
    flat = [
        jnp.concatenate([total[r:r + 8], gap, total[r + 8:r + 16], gap], axis=1) for r in (0, 16)
    ]
    high = (lax.axis_index("band") >> 1) == 1
    image = slots[...].reshape(32, 8, 128)
    for side in range(2):
        here = high if side else jnp.logical_not(high)
        rows = slice(side * 32, side * 32 + 32)
        out[rows, :8, :] = image
        out[rows, 8:, :] = jnp.broadcast_to(jnp.where(here, flat[0], flat[1])[None], (32, 8, 128))


def final_body(scale, got, control_t, innov, live, gradient_t, departures):
    band = lax.axis_index("band")
    image = got[pl.ds((band >> 1) * 32, 32), :8, :].reshape(256, 128)
    departures[...] = (live[...] * (innov[...] - image)).reshape(1, 256, 128)
    low = jnp.sum(got[:32, 8:, :], axis=0)
    top = jnp.sum(got[32:, 8:, :], axis=0)
    total = jnp.concatenate([
        jnp.concatenate([low[:, :56], top[:, :56]], axis=1),
        jnp.concatenate([low[:, 64:120], top[:, 64:120]], axis=1),
    ], axis=0)
    own = ones_where(iota((16, 64), 1) == band * 16 + iota((16, 64), 0))
    hi, mid, lo = parts3(control_t[...])
    gradient_t[...] = dot(own, hi) + dot(own, mid) + dot(own, lo) - scale * total


def per_device(members, eigvecs, control, columns, interpolation, owners, innovation, obs_weight):
    scale = 1.0 / math.sqrt(112 * 64)
    owners = owners.reshape(16, 128)

    def over(x, bit):
        return lax.ppermute(x, "band", [(i, i ^ bit) for i in range(4)])

    dma = pltpu.SemaphoreType.DMA
    m_my, m_mt, e_my, e_mt, payload = call(
        load_body,
        [HB] * 4,
        [(pltpu.HBM((16, 8, 1024), BF), HB)] * 2 + [(pltpu.HBM((28, 8, 1024), BF), HB)] * 2
        + [(pltpu.HBM((32, 16, 256), BF), VM)],
        10 ** 6, 5 * 10 ** 6,
        [pltpu.VMEM((2, 256, 256), F32), dma((8,))],
    )(in_hbm(members), in_hbm(eigvecs), in_hbm(innovation), in_hbm(obs_weight))
    m_my, m_mt, e0, e_mt = [in_hbm(a.reshape(-1, 1024)) for a in (m_my, m_mt, e_my, e_mt)]
    m3 = over(m_mt, 3)
    m2 = over(m_my, 2)
    m1 = over(m_mt, 1)
    got = lax.all_to_all(payload, "mem", split_axis=0, concat_axis=0, tiled=True)
    e1 = over(e_mt, 1)
    m1, m2, m3, e1 = [in_vmem(a) for a in (m1, m2, m3, e1)]

    part, kron = call(
        lambda *refs: increment_own(scale, *refs), [HB, HB, VM, HB, VM],
        [(pltpu.HBM((8, 1024), F32), VM), (pltpu.HBM((448, 256), BF), VM)],
        25 * 10 ** 7, 2 * 10 ** 6,
        [pltpu.VMEM((64, 112), F32), pltpu.VMEM((256, 1024), BF), pltpu.VMEM((448, 1024), BF), dma((5,))],
    )(in_hbm(control.T), m_my, m1, e0, e1)
    part, eig, ensemble = call(
        lambda *refs: increment_other(scale, *refs), [HB] * 3 + [VM] * 3 + [HB, VM, ANY],
        [(shape((8, 1024), F32), VM), (pltpu.VMEM((448, 1024), BF), VM), (pltpu.VMEM((512, 1024), BF), VM)],
        25 * 10 ** 7, 2 * 10 ** 6,
        [pltpu.VMEM((448, 256), BF), pltpu.VMEM((8, 1024), F32), dma((20,))],
    )(in_hbm(kron), in_hbm(part), m_my, m1, m2, m3, e0, e1, got)
    eig, ensemble = in_vmem(eig), in_vmem(ensemble)

    kept = call(
        prep_body,
        [HB] * 3 + [ANY] + [HB] * 2 + [ANY],
        [(pltpu.VMEM(d, t), VM) for d, t in (
            ((1024, 1024), BF), ((64, 256), BF), ((64, 256, 256), BF), ((64, 256), F32), ((64, 256), F32),
            ((256, 128), F32), ((256, 128), F32))],
        10 ** 8, 12 * 10 ** 6,
        [pltpu.VMEM((16, 64), jnp.int32), pltpu.VMEM((16, 128), jnp.int32), pltpu.VMEM((32, 16, 256), BF), dma((7,))],
    )(in_hbm(columns.T), in_hbm(owners), in_hbm(interpolation), got, in_hbm(innovation), in_hbm(obs_weight), part)
    onehot, place, interp, innov, weight, innov_own, live_own = [in_vmem(a) for a in kept]

    (inc_my,) = call(
        add_body, [VM, VM, ANY], [(shape((8, 1024), BF), VM)], 10 ** 4, 10 ** 5
    )(part, over(part, 2), place)
    inc_mt = over(inc_my, 1)
    adj_my, adj_mt, slots = call(
        obs_body, [VM] * 7,
        [(shape((8, 1024), F32), VM)] * 2 + [(pltpu.VMEM((256, 128), F32), VM)],
        10 ** 9, 12 * 10 ** 6,
        [pltpu.VMEM((64, 256), BF), pltpu.VMEM((64, 256), BF), pltpu.VMEM((64, 256), F32)],
    )(inc_my, inc_mt, onehot, place, innov, weight, interp)

    g_mt, g_my = call(
        gradient_body, [VM] * 4, [(shape((32, 56), F32), VM)] * 2, 5 * 10 ** 8, 2 * 10 ** 6
    )(adj_my, over(adj_mt, 1), eig, ensemble)

    (sent,) = call(
        pack_body, [VM] * 3, [(shape((64, 16, 128), F32), VM)], 10 ** 5, 6 * 10 ** 5
    )(g_my, over(g_mt, 1), in_vmem(slots))
    groups = [[(2 * z + core) * 32 + t for z in range(2) for t in range(32)] for core in range(2)]
    arrived = lax.all_to_all(
        sent, ("band", "mem"), split_axis=0, concat_axis=0, axis_index_groups=groups, tiled=True)
    gradient_t, departures = call(
        lambda *refs: final_body(scale, *refs), [VM] * 4,
        [(shape((16, 112), F32), VM), (shape((1, 256, 128), F32), VM)], 10 ** 6, 6 * 10 ** 5,
    )(arrived, control.T, innov_own, live_own)
    return (gradient_t.T, departures)


def solution(mesh):
    return jax.shard_map(
        per_device,
        mesh=mesh,
        in_specs=(
            P("band", None, "mem"),
            P("band", None, "mem"),
            P(),
            P("mem", None),
            P("mem", None, None),
            P(),
            P("mem", None, None),
            P("mem", None, None),
        ),
        out_specs=(P(None, "band"), P("mem", None, "band")),
        check_vma=False,
    )
```

```python
import math

import jax
import jax.numpy as jnp
from jax import lax
from jax.experimental import pallas as pl
from jax.experimental.pallas import tpu as pltpu
from jax.sharding import PartitionSpec as P

BF = jnp.bfloat16
F32 = jnp.float32
NN = (((1,), (0,)), ((), ()))
NT = (((1,), (1,)), ((), ()))
TN = (((0,), (0,)), ((), ()))
MIB = 1024 * 1024
VM = pl.BlockSpec(memory_space=pltpu.VMEM)
ANY = pl.BlockSpec(memory_space=pl.ANY)
HB = pl.BlockSpec(memory_space=pltpu.HBM)


def dot(a, b, dims=NN):
    return lax.dot_general(a, b, dims, preferred_element_type=F32)


def parts3(x):
    hi = x.astype(BF)
    rest = x - hi.astype(F32)
    mid = rest.astype(BF)
    lo = (rest - mid.astype(F32)).astype(BF)
    return hi, mid, lo


def iota(dims, dim):
    return lax.broadcasted_iota(jnp.int32, dims, dim)


def ones_where(cond):
    return cond.astype(F32).astype(BF)


def shape(dims, dtype):
    return jax.ShapeDtypeStruct(dims, dtype)


def in_hbm(x):
    return pltpu.with_memory_space_constraint(x, pltpu.HBM)


def in_vmem(x):
    return pltpu.with_memory_space_constraint(x, pltpu.VMEM)


def call(body, ins, outs, flops, nbytes, scratch=(), vmem=16):
    return pl.pallas_call(
        body,
        out_shape=tuple(o for o, _ in outs),
        in_specs=list(ins),
        out_specs=tuple(s for _, s in outs),
        scratch_shapes=list(scratch),
        compiler_params=pltpu.CompilerParams(vmem_limit_bytes=vmem * MIB),
        cost_estimate=pl.CostEstimate(flops=flops, bytes_accessed=nbytes, transcendentals=0),
    )


def start_all(copies):
    for c in copies:
        c.start()
    return copies


def wait_all(copies):
    for c in copies:
        c.wait()


def halves_copies(src, mine, mate, sem, at):
    core = lax.axis_index("band") & 1
    lo = pl.multiple_of(core * 8, 8)
    hi = pl.multiple_of(8 - core * 8, 8)
    return [
        pltpu.make_async_copy(src.at[:, pl.ds(hi, 8), :], mate, sem.at[at]),
        pltpu.make_async_copy(src.at[:, pl.ds(lo, 8), :], mine, sem.at[at + 1]),
    ]


def quarter_at(side):
    core = lax.axis_index("band") & 1
    return pl.ds(pl.multiple_of((core + 2 * side) * 128, 128), 128)


def load_body(mem, eig, innovation, obs_weight, m_mine, m_mate, e_mine, e_mate, payload, iv, sem):
    slices = start_all(halves_copies(mem, m_mine, m_mate, sem, 0))
    copies = start_all([
        pltpu.make_async_copy(
            a.at[0, :, quarter_at(side)], iv.at[n, :, side * 128:(side + 1) * 128], sem.at[4 + 2 * n + side])
        for n, a in enumerate((innovation, obs_weight)) for side in range(2)
    ])
    slices += start_all(halves_copies(eig, e_mine, e_mate, sem, 2))
    wait_all(copies)
    for n in range(2):
        payload[:, n * 8:(n + 1) * 8, :] = iv[n].reshape(32, 8, 256).astype(BF)
    wait_all(slices)


def increment_of(scale, kron, ma, mb, ea, eb, cut):
    mixed = dot(kron, jnp.concatenate([ma[:, cut], mb[:, cut]], axis=0))
    total = jnp.sum((mixed[:224] * ea[:, cut].astype(F32)).reshape(28, 8, 256), axis=0)
    total = total + jnp.sum((mixed[224:] * eb[:, cut].astype(F32)).reshape(28, 8, 256), axis=0)
    return scale * total


def increment_own(scale, control_t, ma, mb, ea, eb, out, kron, ct, sem):
    get = pltpu.make_async_copy(control_t, ct, sem)
    get.start()
    band = lax.axis_index("band")
    row = iota((448, 112), 0)
    second = (row >= 224).astype(jnp.int32)
    mode = (band ^ second) * 28 + ((row - 224 * second) >> 3)
    pick_rows = ones_where(mode == iota((448, 112), 1))
    col = iota((64, 512), 1)
    member = (band ^ (col >> 7)) * 16 + ((col & 127) >> 3)
    pick_cols = ones_where(member == iota((64, 512), 0))
    same = (iota((448, 512), 0) & 7) == (iota((448, 512), 1) & 7)
    get.wait()
    rows = dot(pick_rows, ct[...].astype(BF), NT).astype(BF)
    full = jnp.where(same, dot(rows, pick_cols), 0.0).astype(BF)
    kron[...] = full[:, 256:]
    for g in range(0, 1024, 256):
        cut = slice(g, g + 256)
        out[:, cut] = increment_of(scale, full[:, :256], ma, mb, ea, eb, cut)


def increment_other(scale, kron, before, ma, mb, ea, eb, _, out):
    for g in range(0, 1024, 256):
        cut = slice(g, g + 256)
        out[:, cut] = before[:, cut] + increment_of(scale, kron[...], ma, mb, ea, eb, cut)


def prep_body(columns_t, owners_in, interpolation, got_in, innovation, obs_weight, _,
              onehot, place, interp, innov, weight, innov_own, live_own,
              cols_s, own_s, got, sem):
    band = lax.axis_index("band")
    tile = lax.axis_index("mem")
    quarter = pl.ds(pl.multiple_of(band * 128, 128), 128)
    small = [(columns_t, cols_s), (owners_in, own_s), (got_in, got)]
    mid = [(innovation.at[0, :, quarter], innov_own), (obs_weight.at[0, :, quarter], live_own)]
    big = [(interpolation.at[:, :, quarter_at(side)], interp.at[:, :, side * 128:(side + 1) * 128]) for side in range(2)]
    copies = start_all([pltpu.make_async_copy(a, b, sem.at[n]) for n, (a, b) in enumerate(small + mid + big)])
    wait_all(copies[:3])
    t = iota((64, 1024), 1)
    cols = cols_s[...].astype(F32).T.astype(jnp.int32)
    for c in range(16):
        onehot[c * 64:(c + 1) * 64, :] = ones_where(cols[:, c:c + 1] == t)
    pair = own_s[pl.ds(tile >> 1, 1), :].astype(F32)
    own = jnp.where((tile & 1) == 1, pair[:, 64:], pair[:, :64])
    own_row = jnp.broadcast_to(own, (64, 64))
    own_col = own_row.T
    earlier = iota((64, 64), 1) < iota((64, 64), 0)
    rank = jnp.sum(jnp.where((own_row == own_col) & earlier, 1.0, 0.0), axis=1, keepdims=True)
    target = (own_col[:, :1] * 8.0 + rank).astype(jnp.int32)
    sel = ones_where(target == iota((64, 256), 1))
    place[...] = sel
    x = got[...].astype(F32)
    innov[...] = dot(sel, x[:, :8].reshape(256, 256).astype(BF))
    weight[...] = dot(sel, x[:, 8:].reshape(256, 256).astype(BF))
    hit = ones_where(own_s[...] == tile)
    pair = ones_where((iota((256, 16), 0) >> 4) == iota((256, 16), 1))
    odd = (iota((256, 128), 0) >> 3) & 1
    side = jnp.where((iota((256, 128), 1) >> 6) == odd, dot(pair, hit), 0.0)
    count = jnp.sum(side, axis=1, keepdims=True)
    live = jnp.where((iota((256, 1), 0) & 7).astype(F32) < count, 1.0, 0.0)
    wait_all(copies[3:5])
    live_own[...] = live * live_own[...]
    wait_all(copies[5:])


def add_body(a, b, _, out):
    out[...] = (a[...] + b[...]).astype(BF)


def obs_body(inc_my, inc_mt, onehot, place, innov, weight, interp, adj_my, adj_mt, slots, picked, depb, spread):
    band = lax.axis_index("band")
    first = (band & 1) == 0
    mine = inc_my[...].astype(F32)
    mate = inc_mt[...].astype(F32)
    inc = jnp.concatenate([jnp.where(first, mine, mate), jnp.where(first, mate, mine)], axis=0).astype(BF)
    picks = dot(onehot[...], inc, NT)
    by_col = jnp.concatenate([picks[c * 64:(c + 1) * 64] for c in range(16)], axis=1).astype(BF)
    r0 = iota((256, 256), 0)
    r1 = iota((256, 256), 1)
    swap = ones_where(((r0 & 15) * 16 + (r0 >> 4)) == r1)
    picked[...] = dot(by_col, swap).astype(BF)
    rows = iota((16, 256), 0)
    image = []
    for b in range(4):
        lhs = picked[b * 16:(b + 1) * 16, :]
        acc = jnp.zeros((16, 256), F32)
        for i in range(16):
            acc = jnp.where(rows == i, dot(lhs, interp[b * 16 + i]), acc)
        image.append(acc)
    image = jnp.concatenate(image, axis=0)
    depb[...] = (weight[...] * (innov[...] - image)).astype(BF)
    for b in range(4):
        lhs = depb[b * 16:(b + 1) * 16, :]
        acc = jnp.zeros((16, 256), F32)
        for i in range(16):
            acc = jnp.where(rows == i, dot(lhs, interp[b * 16 + i], NT), acc)
        spread[b * 16:(b + 1) * 16, :] = acc
    x = spread[...]
    hi = x.astype(BF)
    lo = (x - hi.astype(F32)).astype(BF)
    terms = []
    for part in (hi, lo):
        turned = dot(swap, part, NT)
        terms.append(jnp.concatenate([turned[c * 16:(c + 1) * 16] for c in range(16)], axis=1))
    both = dot(jnp.concatenate(terms, axis=0).astype(BF), onehot[...])
    adj = both[:16] + both[16:]
    adj_my[...] = jnp.where(first, adj[:8], adj[8:])
    adj_mt[...] = jnp.where(first, adj[8:], adj[:8])
    sel = place[...]
    hi, mid, lo = parts3(jnp.where((band >> 1) == 0, image[:, :128], image[:, 128:]))
    slots[...] = dot(sel, hi, TN) + dot(sel, mid, TN) + dot(sel, lo, TN)


def gradient_body(a0, a1, m0, m1, m2, m3, e0, e1, mate, mine):
    first = (lax.axis_index("band") & 1) == 0
    adj = a0[...] + a1[...]
    wide = jnp.broadcast_to(adj[None], (16, 8, 1024)).reshape(128, 1024)
    same = (iota((448, 256), 0) & 7) == (iota((448, 256), 1) & 7)
    sel = ones_where((iota((32, 256), 1) >> 3) == iota((32, 256), 0))
    eig = jnp.concatenate([e0[...], e1[...]], axis=0)
    for ma, mb, g in ((m1, m3, mate), (m0, m2, mine)):
        weighted = jnp.concatenate(
            [(m[...].astype(F32) * wide).astype(BF) for m in (ma, mb)], axis=0)
        full = jnp.where(same, dot(eig, weighted, NT), 0.0)
        own = jnp.sum(full.reshape(56, 8, 256), axis=1)
        own = jnp.where(first, own, jnp.concatenate([own[28:], own[:28]], axis=0))
        hi, mid, lo = parts3(own)
        g[...] = dot(sel, hi, NT) + dot(sel, mid, NT) + dot(sel, lo, NT)


def pack_body(mine, came, slots, out):
    total = mine[...] + came[...]
    gap = jnp.zeros((8, 8), F32)
    flat = [
        jnp.concatenate([total[r:r + 8], gap, total[r + 8:r + 16], gap], axis=1) for r in (0, 16)
    ]
    high = (lax.axis_index("band") >> 1) == 1
    image = slots[...].reshape(32, 8, 128)
    for side in range(2):
        here = high if side else jnp.logical_not(high)
        rows = slice(side * 32, side * 32 + 32)
        out[rows, :8, :] = image
        out[rows, 8:, :] = jnp.broadcast_to(jnp.where(here, flat[0], flat[1])[None], (32, 8, 128))


def final_body(scale, got, control_t, innov, live, gradient_t, departures):
    band = lax.axis_index("band")
    image = got[pl.ds((band >> 1) * 32, 32), :8, :].reshape(256, 128)
    departures[...] = (live[...] * (innov[...] - image)).reshape(1, 256, 128)
    low = jnp.sum(got[:32, 8:, :], axis=0)
    top = jnp.sum(got[32:, 8:, :], axis=0)
    total = jnp.concatenate([
        jnp.concatenate([low[:, :56], top[:, :56]], axis=1),
        jnp.concatenate([low[:, 64:120], top[:, 64:120]], axis=1),
    ], axis=0)
    own = ones_where(iota((16, 64), 1) == band * 16 + iota((16, 64), 0))
    hi, mid, lo = parts3(control_t[...])
    gradient_t[...] = dot(own, hi) + dot(own, mid) + dot(own, lo) - scale * total


def per_device(members, eigvecs, control, columns, interpolation, owners, innovation, obs_weight):
    scale = 1.0 / math.sqrt(112 * 64)
    owners = owners.reshape(16, 128)

    def over(x, bit):
        return lax.ppermute(x, "band", [(i, i ^ bit) for i in range(4)])

    dma = pltpu.SemaphoreType.DMA
    m_my, m_mt, e_my, e_mt, payload = call(
        load_body,
        [HB] * 4,
        [(pltpu.VMEM((16, 8, 1024), BF), VM)] * 2 + [(pltpu.VMEM((28, 8, 1024), BF), VM)] * 2
        + [(pltpu.HBM((32, 16, 256), BF), VM)],
        10 ** 6, 5 * 10 ** 6,
        [pltpu.VMEM((2, 256, 256), F32), dma((8,))],
    )(in_hbm(members), in_hbm(eigvecs), in_hbm(innovation), in_hbm(obs_weight))
    m_my, m_mt, e0, e_mt = [in_vmem(a.reshape(-1, 1024)) for a in (m_my, m_mt, e_my, e_mt)]
    m3 = over(m_mt, 3)
    m2 = over(m_my, 2)
    m1 = over(m_mt, 1)
    got = lax.all_to_all(payload, "mem", split_axis=0, concat_axis=0, tiled=True)
    e1 = over(e_mt, 1)
    m1, m2, m3, e1 = [in_vmem(a) for a in (m1, m2, m3, e1)]

    part, kron = call(
        lambda *refs: increment_own(scale, *refs), [HB] + [VM] * 4,
        [(pltpu.VMEM((8, 1024), F32), VM), (pltpu.VMEM((448, 256), BF), VM)],
        25 * 10 ** 7, 2 * 10 ** 6, [pltpu.VMEM((64, 112), F32), dma(())],
    )(in_hbm(control.T), m_my, m1, e0, e1)
    (part,) = call(
        lambda *refs: increment_other(scale, *refs), [VM] * 6 + [ANY], [(shape((8, 1024), F32), VM)],
        25 * 10 ** 7, 2 * 10 ** 6,
    )(in_vmem(kron), in_vmem(part), m2, m3, e0, e1, got)

    kept = call(
        prep_body,
        [HB] * 3 + [ANY] + [HB] * 2 + [ANY],
        [(pltpu.VMEM(d, t), VM) for d, t in (
            ((1024, 1024), BF), ((64, 256), BF), ((64, 256, 256), BF), ((64, 256), F32), ((64, 256), F32),
            ((256, 128), F32), ((256, 128), F32))],
        10 ** 8, 12 * 10 ** 6,
        [pltpu.VMEM((16, 64), jnp.int32), pltpu.VMEM((16, 128), jnp.int32), pltpu.VMEM((32, 16, 256), BF), dma((7,))],
    )(in_hbm(columns.T), in_hbm(owners), in_hbm(interpolation), got, in_hbm(innovation), in_hbm(obs_weight), part)
    onehot, place, interp, innov, weight, innov_own, live_own = [in_vmem(a) for a in kept]

    (inc_my,) = call(
        add_body, [VM, VM, ANY], [(shape((8, 1024), BF), VM)], 10 ** 4, 10 ** 5
    )(part, over(part, 2), place)
    inc_mt = over(inc_my, 1)
    adj_my, adj_mt, slots = call(
        obs_body, [VM] * 7,
        [(shape((8, 1024), F32), VM)] * 2 + [(pltpu.VMEM((256, 128), F32), VM)],
        10 ** 9, 12 * 10 ** 6,
        [pltpu.VMEM((64, 256), BF), pltpu.VMEM((64, 256), BF), pltpu.VMEM((64, 256), F32)],
    )(inc_my, inc_mt, onehot, place, innov, weight, interp)

    g_mt, g_my = call(
        gradient_body, [VM] * 8, [(shape((32, 56), F32), VM)] * 2, 5 * 10 ** 8, 2 * 10 ** 6
    )(adj_my, over(adj_mt, 1), m_my, m1, m2, m3, e0, e1)

    (sent,) = call(
        pack_body, [VM] * 3, [(shape((64, 16, 128), F32), VM)], 10 ** 5, 6 * 10 ** 5
    )(g_my, over(g_mt, 1), in_vmem(slots))
    groups = [[(2 * z + core) * 32 + t for z in range(2) for t in range(32)] for core in range(2)]
    arrived = lax.all_to_all(
        sent, ("band", "mem"), split_axis=0, concat_axis=0, axis_index_groups=groups, tiled=True)
    gradient_t, departures = call(
        lambda *refs: final_body(scale, *refs), [VM] * 4,
        [(shape((16, 112), F32), VM), (shape((1, 256, 128), F32), VM)], 10 ** 6, 6 * 10 ** 5,
    )(arrived, control.T, innov_own, live_own)
    return (gradient_t.T, departures)


def solution(mesh):
    return jax.shard_map(
        per_device,
        mesh=mesh,
        in_specs=(
            P("band", None, "mem"),
            P("band", None, "mem"),
            P(),
            P("mem", None),
            P("mem", None, None),
            P(),
            P("mem", None, None),
            P("mem", None, None),
        ),
        out_specs=(P(None, "band"), P("mem", None, "band")),
        check_vma=False,
    )
```

```python
import math

import jax
import jax.numpy as jnp
from jax import lax
from jax.experimental import pallas as pl
from jax.experimental.pallas import tpu as pltpu
from jax.sharding import PartitionSpec as P

BF = jnp.bfloat16
F32 = jnp.float32
NN = (((1,), (0,)), ((), ()))
NT = (((1,), (1,)), ((), ()))
TN = (((0,), (0,)), ((), ()))
MIB = 1024 * 1024
VM = pl.BlockSpec(memory_space=pltpu.VMEM)
ANY = pl.BlockSpec(memory_space=pl.ANY)
HB = pl.BlockSpec(memory_space=pltpu.HBM)


def dot(a, b, dims=NN):
    return lax.dot_general(a, b, dims, preferred_element_type=F32)


def parts3(x):
    hi = x.astype(BF)
    rest = x - hi.astype(F32)
    mid = rest.astype(BF)
    lo = (rest - mid.astype(F32)).astype(BF)
    return hi, mid, lo


def iota(dims, dim):
    return lax.broadcasted_iota(jnp.int32, dims, dim)


def ones_where(cond):
    return cond.astype(F32).astype(BF)


def shape(dims, dtype):
    return jax.ShapeDtypeStruct(dims, dtype)


def in_hbm(x):
    return pltpu.with_memory_space_constraint(x, pltpu.HBM)


def in_vmem(x):
    return pltpu.with_memory_space_constraint(x, pltpu.VMEM)


def call(body, ins, outs, flops, nbytes, scratch=(), vmem=16):
    return pl.pallas_call(
        body,
        out_shape=tuple(o for o, _ in outs),
        in_specs=list(ins),
        out_specs=tuple(s for _, s in outs),
        scratch_shapes=list(scratch),
        compiler_params=pltpu.CompilerParams(vmem_limit_bytes=vmem * MIB),
        cost_estimate=pl.CostEstimate(flops=flops, bytes_accessed=nbytes, transcendentals=0),
    )


def start_all(copies):
    for c in copies:
        c.start()
    return copies


def wait_all(copies):
    for c in copies:
        c.wait()


def halves_copies(src, mine, mate, sem, at):
    core = lax.axis_index("band") & 1
    lo = pl.multiple_of(core * 8, 8)
    hi = pl.multiple_of(8 - core * 8, 8)
    return [
        pltpu.make_async_copy(src.at[:, pl.ds(hi, 8), :], mate, sem.at[at]),
        pltpu.make_async_copy(src.at[:, pl.ds(lo, 8), :], mine, sem.at[at + 1]),
    ]


def quarter_at(side):
    core = lax.axis_index("band") & 1
    return pl.ds(pl.multiple_of((core + 2 * side) * 128, 128), 128)


def load_body(mem, eig, innovation, obs_weight, m_mine, m_mate, e_mine, e_mate, payload, iv, sem):
    slices = start_all(halves_copies(mem, m_mine, m_mate, sem, 0))
    copies = start_all([
        pltpu.make_async_copy(
            a.at[0, :, quarter_at(side)], iv.at[n, :, side * 128:(side + 1) * 128], sem.at[4 + 2 * n + side])
        for n, a in enumerate((innovation, obs_weight)) for side in range(2)
    ])
    slices += start_all(halves_copies(eig, e_mine, e_mate, sem, 2))
    wait_all(copies)
    for n in range(2):
        payload[:, n * 8:(n + 1) * 8, :] = iv[n].reshape(32, 8, 256).astype(BF)
    wait_all(slices)


def increment_of(scale, kron, ma, mb, ea, eb, cut):
    mixed = dot(kron, jnp.concatenate([ma[:, cut], mb[:, cut]], axis=0))
    total = jnp.sum((mixed[:224] * ea[:, cut].astype(F32)).reshape(28, 8, 256), axis=0)
    total = total + jnp.sum((mixed[224:] * eb[:, cut].astype(F32)).reshape(28, 8, 256), axis=0)
    return scale * total


def increment_own(scale, control_t, ma, mb, ea, eb, out, kron, ct, sem):
    get = pltpu.make_async_copy(control_t, ct, sem)
    get.start()
    band = lax.axis_index("band")
    row = iota((448, 112), 0)
    second = (row >= 224).astype(jnp.int32)
    mode = (band ^ second) * 28 + ((row - 224 * second) >> 3)
    pick_rows = ones_where(mode == iota((448, 112), 1))
    col = iota((64, 512), 1)
    member = (band ^ (col >> 7)) * 16 + ((col & 127) >> 3)
    pick_cols = ones_where(member == iota((64, 512), 0))
    same = (iota((448, 512), 0) & 7) == (iota((448, 512), 1) & 7)
    get.wait()
    rows = dot(pick_rows, ct[...].astype(BF), NT).astype(BF)
    full = jnp.where(same, dot(rows, pick_cols), 0.0).astype(BF)
    kron[...] = full[:, 256:]
    for g in range(0, 1024, 256):
        cut = slice(g, g + 256)
        out[:, cut] = increment_of(scale, full[:, :256], ma, mb, ea, eb, cut)


def increment_other(scale, kron, before, ma, mb, ea, eb, _, out):
    for g in range(0, 1024, 256):
        cut = slice(g, g + 256)
        out[:, cut] = before[:, cut] + increment_of(scale, kron[...], ma, mb, ea, eb, cut)


def prep_body(columns_t, owners_in, interpolation, got_in, innovation, obs_weight, _,
              onehot, onehot_t, place, interp, innov, weight, innov_own, live_own,
              cols_s, own_s, got, sem):
    band = lax.axis_index("band")
    tile = lax.axis_index("mem")
    quarter = pl.ds(pl.multiple_of(band * 128, 128), 128)
    small = [(columns_t, cols_s), (owners_in, own_s), (got_in, got)]
    mid = [(innovation.at[0, :, quarter], innov_own), (obs_weight.at[0, :, quarter], live_own)]
    big = [(interpolation.at[:32, :, quarter_at(side)], interp.at[:, :, side * 128:(side + 1) * 128]) for side in range(2)]
    copies = start_all([pltpu.make_async_copy(a, b, sem.at[n]) for n, (a, b) in enumerate(small + mid + big)])
    wait_all(copies[:3])
    t = iota((64, 1024), 1)
    cols = cols_s[...].astype(F32).T.astype(jnp.int32)
    for c in range(16):
        onehot[c * 64:(c + 1) * 64, :] = ones_where(cols[:, c:c + 1] == t)
    flat = jnp.concatenate([cols_s[c:c + 1, :] for c in range(16)], axis=1)
    for r in range(0, 1024, 128):
        onehot_t[r:r + 128, :] = ones_where(flat == iota((128, 1024), 0) + r)
    pair = own_s[pl.ds(tile >> 1, 1), :].astype(F32)
    own = jnp.where((tile & 1) == 1, pair[:, 64:], pair[:, :64])
    own_row = jnp.broadcast_to(own, (64, 64))
    own_col = own_row.T
    earlier = iota((64, 64), 1) < iota((64, 64), 0)
    rank = jnp.sum(jnp.where((own_row == own_col) & earlier, 1.0, 0.0), axis=1, keepdims=True)
    target = (own_col[:, :1] * 8.0 + rank).astype(jnp.int32)
    sel = ones_where(target == iota((64, 256), 1))
    place[...] = sel
    x = got[...].astype(F32)
    innov[...] = dot(sel, x[:, :8].reshape(256, 256).astype(BF))
    weight[...] = dot(sel, x[:, 8:].reshape(256, 256).astype(BF))
    hit = ones_where(own_s[...] == tile)
    pair = ones_where((iota((256, 16), 0) >> 4) == iota((256, 16), 1))
    odd = (iota((256, 128), 0) >> 3) & 1
    side = jnp.where((iota((256, 128), 1) >> 6) == odd, dot(pair, hit), 0.0)
    count = jnp.sum(side, axis=1, keepdims=True)
    live = jnp.where((iota((256, 1), 0) & 7).astype(F32) < count, 1.0, 0.0)
    wait_all(copies[3:5])
    live_own[...] = live * live_own[...]
    wait_all(copies[5:])


def add_body(a, b, _, out):
    out[...] = (a[...] + b[...]).astype(BF)


def obs_body(inc_my, inc_mt, onehot, onehot_t, place, innov, weight, near, interpolation,
             adj_my, adj_mt, slots, picked, depb, spread, far, sem):
    fetch = [
        start_all([
            pltpu.make_async_copy(
                interpolation.at[32 + j:40 + j, :, quarter_at(side)],
                far.at[j:j + 8, :, side * 128:(side + 1) * 128], sem.at[j // 4 + side])
            for side in range(2)
        ]) for j in range(0, 32, 8)
    ]

    def block(j):
        return near[j] if j < 32 else far[j - 32]

    band = lax.axis_index("band")
    first = (band & 1) == 0
    mine = inc_my[...].astype(F32)
    mate = inc_mt[...].astype(F32)
    inc = jnp.concatenate([jnp.where(first, mine, mate), jnp.where(first, mate, mine)], axis=0).astype(BF)
    r0 = iota((256, 256), 0)
    r1 = iota((256, 256), 1)
    swap = ones_where(((r0 & 15) * 16 + (r0 >> 4)) == r1)
    picks = dot(inc, onehot_t[...])
    by_col = jnp.concatenate([picks[:, c * 64:(c + 1) * 64] for c in range(16)], axis=0).astype(BF)
    picked[...] = dot(by_col, swap, TN).astype(BF)
    rows = iota((16, 256), 0)
    image = []
    for b in range(4):
        lhs = picked[b * 16:(b + 1) * 16, :]
        acc = jnp.zeros((16, 256), F32)
        for i in range(16):
            j = b * 16 + i
            if j >= 32 and j % 8 == 0:
                wait_all(fetch[(j - 32) // 8])
            acc = jnp.where(rows == i, dot(lhs, block(j)), acc)
        image.append(acc)
    image = jnp.concatenate(image, axis=0)
    depb[...] = (weight[...] * (innov[...] - image)).astype(BF)
    for b in range(4):
        lhs = depb[b * 16:(b + 1) * 16, :]
        acc = jnp.zeros((16, 256), F32)
        for i in range(16):
            acc = jnp.where(rows == i, dot(lhs, block(b * 16 + i), NT), acc)
        spread[b * 16:(b + 1) * 16, :] = acc
    x = spread[...]
    hi = x.astype(BF)
    lo = (x - hi.astype(F32)).astype(BF)
    terms = []
    for part in (hi, lo):
        turned = dot(swap, part, NT)
        terms.append(jnp.concatenate([turned[c * 16:(c + 1) * 16] for c in range(16)], axis=1))
    both = dot(jnp.concatenate(terms, axis=0).astype(BF), onehot[...])
    adj = both[:16] + both[16:]
    adj_my[...] = jnp.where(first, adj[:8], adj[8:])
    adj_mt[...] = jnp.where(first, adj[8:], adj[:8])
    sel = place[...]
    hi, mid, lo = parts3(jnp.where((band >> 1) == 0, image[:, :128], image[:, 128:]))
    slots[...] = dot(sel, hi, TN) + dot(sel, mid, TN) + dot(sel, lo, TN)


def gradient_body(a0, a1, m0, m1, m2, m3, e0, e1, mate, mine):
    first = (lax.axis_index("band") & 1) == 0
    adj = a0[...] + a1[...]
    wide = jnp.broadcast_to(adj[None], (16, 8, 1024)).reshape(128, 1024)
    same = (iota((448, 256), 0) & 7) == (iota((448, 256), 1) & 7)
    sel = ones_where((iota((32, 256), 1) >> 3) == iota((32, 256), 0))
    eig = jnp.concatenate([e0[...], e1[...]], axis=0)
    for ma, mb, g in ((m1, m3, mate), (m0, m2, mine)):
        weighted = jnp.concatenate(
            [(m[...].astype(F32) * wide).astype(BF) for m in (ma, mb)], axis=0)
        full = jnp.where(same, dot(eig, weighted, NT), 0.0)
        own = jnp.sum(full.reshape(56, 8, 256), axis=1)
        own = jnp.where(first, own, jnp.concatenate([own[28:], own[:28]], axis=0))
        hi, mid, lo = parts3(own)
        g[...] = dot(sel, hi, NT) + dot(sel, mid, NT) + dot(sel, lo, NT)


def pack_body(mine, came, slots, out):
    total = mine[...] + came[...]
    gap = jnp.zeros((8, 8), F32)
    flat = [
        jnp.concatenate([total[r:r + 8], gap, total[r + 8:r + 16], gap], axis=1) for r in (0, 16)
    ]
    high = (lax.axis_index("band") >> 1) == 1
    image = slots[...].reshape(32, 8, 128)
    for side in range(2):
        here = high if side else jnp.logical_not(high)
        rows = slice(side * 32, side * 32 + 32)
        out[rows, :8, :] = image
        out[rows, 8:, :] = jnp.broadcast_to(jnp.where(here, flat[0], flat[1])[None], (32, 8, 128))


def final_body(scale, got, control_t, innov, live, gradient_t, departures):
    band = lax.axis_index("band")
    image = got[pl.ds((band >> 1) * 32, 32), :8, :].reshape(256, 128)
    departures[...] = (live[...] * (innov[...] - image)).reshape(1, 256, 128)
    low = jnp.sum(got[:32, 8:, :], axis=0)
    top = jnp.sum(got[32:, 8:, :], axis=0)
    total = jnp.concatenate([
        jnp.concatenate([low[:, :56], top[:, :56]], axis=1),
        jnp.concatenate([low[:, 64:120], top[:, 64:120]], axis=1),
    ], axis=0)
    own = ones_where(iota((16, 64), 1) == band * 16 + iota((16, 64), 0))
    hi, mid, lo = parts3(control_t[...])
    gradient_t[...] = dot(own, hi) + dot(own, mid) + dot(own, lo) - scale * total


def per_device(members, eigvecs, control, columns, interpolation, owners, innovation, obs_weight):
    scale = 1.0 / math.sqrt(112 * 64)
    owners = owners.reshape(16, 128)

    def over(x, bit):
        return lax.ppermute(x, "band", [(i, i ^ bit) for i in range(4)])

    dma = pltpu.SemaphoreType.DMA
    m_my, m_mt, e_my, e_mt, payload = call(
        load_body,
        [HB] * 4,
        [(pltpu.VMEM((16, 8, 1024), BF), VM)] * 2 + [(pltpu.VMEM((28, 8, 1024), BF), VM)] * 2
        + [(pltpu.HBM((32, 16, 256), BF), VM)],
        10 ** 6, 5 * 10 ** 6,
        [pltpu.VMEM((2, 256, 256), F32), dma((8,))],
    )(in_hbm(members), in_hbm(eigvecs), in_hbm(innovation), in_hbm(obs_weight))
    m_my, m_mt, e0, e_mt = [in_vmem(a.reshape(-1, 1024)) for a in (m_my, m_mt, e_my, e_mt)]
    m3 = over(m_mt, 3)
    m2 = over(m_my, 2)
    m1 = over(m_mt, 1)
    got = lax.all_to_all(payload, "mem", split_axis=0, concat_axis=0, tiled=True)
    e1 = over(e_mt, 1)
    m1, m2, m3, e1 = [in_vmem(a) for a in (m1, m2, m3, e1)]

    part, kron = call(
        lambda *refs: increment_own(scale, *refs), [HB] + [VM] * 4,
        [(pltpu.VMEM((8, 1024), F32), VM), (pltpu.VMEM((448, 256), BF), VM)],
        25 * 10 ** 7, 2 * 10 ** 6, [pltpu.VMEM((64, 112), F32), dma(())],
    )(in_hbm(control.T), m_my, m1, e0, e1)
    (part,) = call(
        lambda *refs: increment_other(scale, *refs), [VM] * 6 + [ANY], [(shape((8, 1024), F32), VM)],
        25 * 10 ** 7, 2 * 10 ** 6,
    )(in_vmem(kron), in_vmem(part), m2, m3, e0, e1, m3)

    kept = call(
        prep_body,
        [HB] * 3 + [ANY] + [HB] * 2 + [ANY],
        [(pltpu.VMEM(d, t), VM) for d, t in (
            ((1024, 1024), BF), ((1024, 1024), BF), ((64, 256), BF), ((32, 256, 256), BF), ((64, 256), F32), ((64, 256), F32),
            ((256, 128), F32), ((256, 128), F32))],
        10 ** 8, 12 * 10 ** 6,
        [pltpu.VMEM((16, 64), jnp.int32), pltpu.VMEM((16, 128), jnp.int32), pltpu.VMEM((32, 16, 256), BF), dma((7,))],
    )(in_hbm(columns.T), in_hbm(owners), in_hbm(interpolation), got, in_hbm(innovation), in_hbm(obs_weight), part)
    onehot, onehot_t, place, interp, innov, weight, innov_own, live_own = [in_vmem(a) for a in kept]

    (inc_my,) = call(
        add_body, [VM, VM, ANY], [(shape((8, 1024), BF), VM)], 10 ** 4, 10 ** 5
    )(part, over(part, 2), place)
    inc_mt = over(inc_my, 1)
    adj_my, adj_mt, slots = call(
        obs_body, [VM] * 8 + [HB],
        [(shape((8, 1024), F32), VM)] * 2 + [(pltpu.VMEM((256, 128), F32), VM)],
        10 ** 9, 12 * 10 ** 6,
        [pltpu.VMEM((64, 256), BF), pltpu.VMEM((64, 256), BF), pltpu.VMEM((64, 256), F32),
         pltpu.VMEM((32, 256, 256), BF), dma((8,))],
    )(inc_my, inc_mt, onehot, onehot_t, place, innov, weight, interp, in_hbm(interpolation))

    g_mt, g_my = call(
        gradient_body, [VM] * 8, [(shape((32, 56), F32), VM)] * 2, 5 * 10 ** 8, 2 * 10 ** 6
    )(adj_my, over(adj_mt, 1), m_my, m1, m2, m3, e0, e1)

    (sent,) = call(
        pack_body, [VM] * 3, [(shape((64, 16, 128), F32), VM)], 10 ** 5, 6 * 10 ** 5
    )(g_my, over(g_mt, 1), in_vmem(slots))
    groups = [[(2 * z + core) * 32 + t for z in range(2) for t in range(32)] for core in range(2)]
    arrived = lax.all_to_all(
        sent, ("band", "mem"), split_axis=0, concat_axis=0, axis_index_groups=groups, tiled=True)
    gradient_t, departures = call(
        lambda *refs: final_body(scale, *refs), [VM] * 4,
        [(shape((16, 112), F32), VM), (shape((1, 256, 128), F32), VM)], 10 ** 6, 6 * 10 ** 5,
    )(arrived, control.T, innov_own, live_own)
    return (gradient_t.T, departures)


def solution(mesh):
    return jax.shard_map(
        per_device,
        mesh=mesh,
        in_specs=(
            P("band", None, "mem"),
            P("band", None, "mem"),
            P(),
            P("mem", None),
            P("mem", None, None),
            P(),
            P("mem", None, None),
            P("mem", None, None),
        ),
        out_specs=(P(None, "band"), P("mem", None, "band")),
        check_vma=False,
    )
```

```python
import math

import jax
import jax.numpy as jnp
from jax import lax
from jax.experimental import pallas as pl
from jax.experimental.pallas import tpu as pltpu
from jax.sharding import PartitionSpec as P

BF = jnp.bfloat16
F32 = jnp.float32
NN = (((1,), (0,)), ((), ()))
NT = (((1,), (1,)), ((), ()))
TN = (((0,), (0,)), ((), ()))
MIB = 1024 * 1024
VM = pl.BlockSpec(memory_space=pltpu.VMEM)
ANY = pl.BlockSpec(memory_space=pl.ANY)
HB = pl.BlockSpec(memory_space=pltpu.HBM)


def dot(a, b, dims=NN):
    return lax.dot_general(a, b, dims, preferred_element_type=F32)


def parts3(x):
    hi = x.astype(BF)
    rest = x - hi.astype(F32)
    mid = rest.astype(BF)
    lo = (rest - mid.astype(F32)).astype(BF)
    return hi, mid, lo


def iota(dims, dim):
    return lax.broadcasted_iota(jnp.int32, dims, dim)


def ones_where(cond):
    return cond.astype(F32).astype(BF)


def shape(dims, dtype):
    return jax.ShapeDtypeStruct(dims, dtype)


def in_hbm(x):
    return pltpu.with_memory_space_constraint(x, pltpu.HBM)


def in_vmem(x):
    return pltpu.with_memory_space_constraint(x, pltpu.VMEM)


def call(body, ins, outs, flops, nbytes, scratch=(), vmem=16):
    return pl.pallas_call(
        body,
        out_shape=tuple(o for o, _ in outs),
        in_specs=list(ins),
        out_specs=tuple(s for _, s in outs),
        scratch_shapes=list(scratch),
        compiler_params=pltpu.CompilerParams(vmem_limit_bytes=vmem * MIB),
        cost_estimate=pl.CostEstimate(flops=flops, bytes_accessed=nbytes, transcendentals=0),
    )


def start_all(copies):
    for c in copies:
        c.start()
    return copies


def wait_all(copies):
    for c in copies:
        c.wait()


def halves_copies(src, mine, mate, sem, at):
    core = lax.axis_index("band") & 1
    lo = pl.multiple_of(core * 8, 8)
    hi = pl.multiple_of(8 - core * 8, 8)
    return [
        pltpu.make_async_copy(src.at[:, pl.ds(hi, 8), :], mate, sem.at[at]),
        pltpu.make_async_copy(src.at[:, pl.ds(lo, 8), :], mine, sem.at[at + 1]),
    ]


def quarter_at(side):
    core = lax.axis_index("band") & 1
    return pl.ds(pl.multiple_of((core + 2 * side) * 128, 128), 128)


def load_body(mem, eig, innovation, obs_weight, m_mine, m_mate, e_mine, e_mate, payload, iv, sem):
    slices = start_all(halves_copies(mem, m_mine, m_mate, sem, 0))
    copies = start_all([
        pltpu.make_async_copy(
            a.at[0, :, quarter_at(side)], iv.at[n, :, side * 128:(side + 1) * 128], sem.at[4 + 2 * n + side])
        for n, a in enumerate((innovation, obs_weight)) for side in range(2)
    ])
    slices += start_all(halves_copies(eig, e_mine, e_mate, sem, 2))
    wait_all(copies)
    for n in range(2):
        payload[:, n * 8:(n + 1) * 8, :] = iv[n].reshape(32, 8, 256).astype(BF)
    wait_all(slices)


def increment_of(scale, kron, ma, mb, ea, eb, cut):
    mixed = dot(kron, jnp.concatenate([ma[:, cut], mb[:, cut]], axis=0))
    total = jnp.sum((mixed[:224] * ea[:, cut].astype(F32)).reshape(28, 8, 256), axis=0)
    total = total + jnp.sum((mixed[224:] * eb[:, cut].astype(F32)).reshape(28, 8, 256), axis=0)
    return scale * total


def increment_own(scale, control_t, ma, mb, ea, eb, out, kron, ct, sem):
    get = pltpu.make_async_copy(control_t, ct, sem)
    get.start()
    band = lax.axis_index("band")
    row = iota((448, 112), 0)
    second = (row >= 224).astype(jnp.int32)
    mode = (band ^ second) * 28 + ((row - 224 * second) >> 3)
    pick_rows = ones_where(mode == iota((448, 112), 1))
    col = iota((64, 512), 1)
    member = (band ^ (col >> 7)) * 16 + ((col & 127) >> 3)
    pick_cols = ones_where(member == iota((64, 512), 0))
    same = (iota((448, 512), 0) & 7) == (iota((448, 512), 1) & 7)
    get.wait()
    rows = dot(pick_rows, ct[...].astype(BF), NT).astype(BF)
    full = jnp.where(same, dot(rows, pick_cols), 0.0).astype(BF)
    kron[...] = full[:, 256:]
    for g in range(0, 1024, 256):
        cut = slice(g, g + 256)
        out[:, cut] = increment_of(scale, full[:, :256], ma, mb, ea, eb, cut)


def increment_other(scale, kron, before, ma, mb, ea, eb, _, out):
    for g in range(0, 1024, 256):
        cut = slice(g, g + 256)
        out[:, cut] = before[:, cut] + increment_of(scale, kron[...], ma, mb, ea, eb, cut)


def prep_body(columns_t, owners_in, interpolation, got_in, innovation, obs_weight, _,
              onehot, onehot_t, place_hi, place_lo, interp, innov, weight, innov_own, live_own,
              cols_s, own_s, got, sem):
    band = lax.axis_index("band")
    tile = lax.axis_index("mem")
    quarter = pl.ds(pl.multiple_of(band * 128, 128), 128)
    small = [(columns_t, cols_s), (owners_in, own_s), (got_in, got)]
    mid = [(innovation.at[0, :, quarter], innov_own), (obs_weight.at[0, :, quarter], live_own)]
    big = [(interpolation.at[:32, :, quarter_at(side)], interp.at[:, :, side * 128:(side + 1) * 128]) for side in range(2)]
    copies = start_all([pltpu.make_async_copy(a, b, sem.at[n]) for n, (a, b) in enumerate(small + mid + big)])
    wait_all(copies[:3])
    t = iota((64, 1024), 1)
    cols = cols_s[...].astype(F32).T.astype(jnp.int32)
    for c in range(16):
        onehot[c * 64:(c + 1) * 64, :] = ones_where(cols[:, c:c + 1] == t)
    flat = jnp.concatenate([cols_s[c:c + 1, :] for c in range(16)], axis=1)
    for r in range(0, 1024, 128):
        onehot_t[r:r + 128, :] = ones_where(flat == iota((128, 1024), 0) + r)
    pair = own_s[pl.ds(tile >> 1, 1), :].astype(F32)
    own = jnp.where((tile & 1) == 1, pair[:, 64:], pair[:, :64])
    own_row = jnp.broadcast_to(own, (64, 64))
    own_col = own_row.T
    earlier = iota((64, 64), 1) < iota((64, 64), 0)
    rank = jnp.sum(jnp.where((own_row == own_col) & earlier, 1.0, 0.0), axis=1, keepdims=True)
    target = (own_col[:, :1] * 8.0 + rank).astype(jnp.int32)
    sel = ones_where(target == iota((64, 256), 1))
    slot = iota((64, 256), 1)
    half = 4 * (band >> 1)
    place_hi[...] = ones_where((target == slot + half) & ((slot & 7) < 4))
    place_lo[...] = ones_where((target == slot + half - 4) & ((slot & 7) >= 4))
    x = got[...].astype(F32)
    innov[...] = dot(sel, x[:, :8].reshape(256, 256).astype(BF))
    weight[...] = dot(sel, x[:, 8:].reshape(256, 256).astype(BF))
    hit = ones_where(own_s[...] == tile)
    pair = ones_where((iota((256, 16), 0) >> 4) == iota((256, 16), 1))
    odd = (iota((256, 128), 0) >> 3) & 1
    side = jnp.where((iota((256, 128), 1) >> 6) == odd, dot(pair, hit), 0.0)
    count = jnp.sum(side, axis=1, keepdims=True)
    live = jnp.where((iota((256, 1), 0) & 7).astype(F32) < count, 1.0, 0.0)
    wait_all(copies[3:5])
    live_own[...] = live * live_own[...]
    wait_all(copies[5:])


def add_body(a, b, _, out):
    out[...] = (a[...] + b[...]).astype(BF)


def obs_body(inc_my, inc_mt, onehot, onehot_t, innov, weight, near, interpolation,
             adj_my, adj_mt, image_out, picked, depb, spread, far, sem):
    fetch = [
        start_all([
            pltpu.make_async_copy(
                interpolation.at[32 + j:40 + j, :, quarter_at(side)],
                far.at[j:j + 8, :, side * 128:(side + 1) * 128], sem.at[j // 4 + side])
            for side in range(2)
        ]) for j in range(0, 32, 8)
    ]

    def block(j):
        return near[j] if j < 32 else far[j - 32]

    band = lax.axis_index("band")
    first = (band & 1) == 0
    mine = inc_my[...].astype(F32)
    mate = inc_mt[...].astype(F32)
    inc = jnp.concatenate([jnp.where(first, mine, mate), jnp.where(first, mate, mine)], axis=0).astype(BF)
    r0 = iota((256, 256), 0)
    r1 = iota((256, 256), 1)
    swap = ones_where(((r0 & 15) * 16 + (r0 >> 4)) == r1)
    picks = dot(inc, onehot_t[...])
    by_col = jnp.concatenate([picks[:, c * 64:(c + 1) * 64] for c in range(16)], axis=0).astype(BF)
    picked[...] = dot(by_col, swap, TN).astype(BF)
    rows = iota((16, 256), 0)
    image = []
    for b in range(4):
        lhs = picked[b * 16:(b + 1) * 16, :]
        acc = jnp.zeros((16, 256), F32)
        for i in range(16):
            j = b * 16 + i
            if j >= 32 and j % 8 == 0:
                wait_all(fetch[(j - 32) // 8])
            acc = jnp.where(rows == i, dot(lhs, block(j)), acc)
        image.append(acc)
    image = jnp.concatenate(image, axis=0)
    image_out[...] = image
    depb[...] = (weight[...] * (innov[...] - image)).astype(BF)
    for b in range(4):
        lhs = depb[b * 16:(b + 1) * 16, :]
        acc = jnp.zeros((16, 256), F32)
        for i in range(16):
            acc = jnp.where(rows == i, dot(lhs, block(b * 16 + i), NT), acc)
        spread[b * 16:(b + 1) * 16, :] = acc
    x = spread[...]
    hi = x.astype(BF)
    lo = (x - hi.astype(F32)).astype(BF)
    terms = []
    for part in (hi, lo):
        turned = dot(swap, part, NT)
        terms.append(jnp.concatenate([turned[c * 16:(c + 1) * 16] for c in range(16)], axis=1))
    both = dot(jnp.concatenate(terms, axis=0).astype(BF), onehot[...])
    adj = both[:16] + both[16:]
    adj_my[...] = jnp.where(first, adj[:8], adj[8:])
    adj_mt[...] = jnp.where(first, adj[8:], adj[:8])


def slots_body(place_hi, place_lo, image, out):
    hi, lo, _ = parts3(image[...])
    out[...] = dot(place_hi[...], hi, TN) + dot(place_lo[...], lo, TN)


def gradient_body(a0, a1, m0, m1, m2, m3, e0, e1, mate, mine):
    first = (lax.axis_index("band") & 1) == 0
    adj = a0[...] + a1[...]
    wide = jnp.broadcast_to(adj[None], (16, 8, 1024)).reshape(128, 1024)
    same = (iota((448, 256), 0) & 7) == (iota((448, 256), 1) & 7)
    sel = ones_where((iota((32, 256), 1) >> 3) == iota((32, 256), 0))
    eig = jnp.concatenate([e0[...], e1[...]], axis=0)
    for ma, mb, g in ((m1, m3, mate), (m0, m2, mine)):
        weighted = jnp.concatenate(
            [(m[...].astype(F32) * wide).astype(BF) for m in (ma, mb)], axis=0)
        full = jnp.where(same, dot(eig, weighted, NT), 0.0)
        own = jnp.sum(full.reshape(56, 8, 256), axis=1)
        own = jnp.where(first, own, jnp.concatenate([own[28:], own[:28]], axis=0))
        hi, mid, lo = parts3(own)
        g[...] = dot(sel, hi, NT) + dot(sel, mid, NT) + dot(sel, lo, NT)


def pack_body(mine, came, slots, out):
    total = mine[...] + came[...]
    gap = jnp.zeros((8, 8), F32)
    flat = [
        jnp.concatenate([total[r:r + 8], gap, total[r + 8:r + 16], gap], axis=1) for r in (0, 16)
    ]
    high = (lax.axis_index("band") >> 1) == 1
    for side in range(2):
        here = high if side else jnp.logical_not(high)
        term = jnp.broadcast_to(jnp.where(here, flat[0], flat[1])[None], (32, 8, 128))
        image = slots[:, side * 128:(side + 1) * 128].reshape(32, 8, 128)
        out[side * 32:(side + 1) * 32] = jnp.concatenate([term, image], axis=1).astype(BF)


def final_body(scale, got, control_t, innov, live, gradient_t, departures):
    band = lax.axis_index("band")
    sums, halves = [], []
    for side in range(2):
        x = got[side * 32:(side + 1) * 32].astype(F32)
        sums.append(jnp.sum(x[:, :8], axis=0))
        halves.append(x[:, 8:12] + x[:, 12:])
    image = jnp.concatenate(halves, axis=1).reshape(256, 128)
    departures[...] = (live[...] * (innov[...] - image)).reshape(1, 256, 128)
    low, top = sums
    total = jnp.concatenate([
        jnp.concatenate([low[:, :56], top[:, :56]], axis=1),
        jnp.concatenate([low[:, 64:120], top[:, 64:120]], axis=1),
    ], axis=0)
    own = ones_where(iota((16, 64), 1) == band * 16 + iota((16, 64), 0))
    hi, mid, lo = parts3(control_t[...])
    gradient_t[...] = dot(own, hi) + dot(own, mid) + dot(own, lo) - scale * total


def per_device(members, eigvecs, control, columns, interpolation, owners, innovation, obs_weight):
    scale = 1.0 / math.sqrt(112 * 64)
    owners = owners.reshape(16, 128)

    def over(x, bit):
        return lax.ppermute(x, "band", [(i, i ^ bit) for i in range(4)])

    dma = pltpu.SemaphoreType.DMA
    m_my, m_mt, e_my, e_mt, payload = call(
        load_body,
        [HB] * 4,
        [(pltpu.VMEM((16, 8, 1024), BF), VM)] * 2 + [(pltpu.VMEM((28, 8, 1024), BF), VM)] * 2
        + [(pltpu.HBM((32, 16, 256), BF), VM)],
        10 ** 6, 5 * 10 ** 6,
        [pltpu.VMEM((2, 256, 256), F32), dma((8,))],
    )(in_hbm(members), in_hbm(eigvecs), in_hbm(innovation), in_hbm(obs_weight))
    m_my, m_mt, e0, e_mt = [in_vmem(a.reshape(-1, 1024)) for a in (m_my, m_mt, e_my, e_mt)]
    m3 = over(m_mt, 3)
    m2 = over(m_my, 2)
    m1 = over(m_mt, 1)
    got = lax.all_to_all(payload, "mem", split_axis=0, concat_axis=0, tiled=True)
    e1 = over(e_mt, 1)
    m1, m2, m3, e1 = [in_vmem(a) for a in (m1, m2, m3, e1)]

    part, kron = call(
        lambda *refs: increment_own(scale, *refs), [HB] + [VM] * 4,
        [(pltpu.VMEM((8, 1024), F32), VM), (pltpu.VMEM((448, 256), BF), VM)],
        25 * 10 ** 7, 2 * 10 ** 6, [pltpu.VMEM((64, 112), F32), dma(())],
    )(in_hbm(control.T), m_my, m1, e0, e1)
    (part,) = call(
        lambda *refs: increment_other(scale, *refs), [VM] * 6 + [ANY], [(shape((8, 1024), F32), VM)],
        25 * 10 ** 7, 2 * 10 ** 6,
    )(in_vmem(kron), in_vmem(part), m2, m3, e0, e1, m3)

    kept = call(
        prep_body,
        [HB] * 3 + [ANY] + [HB] * 2 + [ANY],
        [(pltpu.VMEM(d, t), VM) for d, t in (
            ((1024, 1024), BF), ((1024, 1024), BF), ((64, 256), BF), ((64, 256), BF), ((32, 256, 256), BF), ((64, 256), F32), ((64, 256), F32),
            ((256, 128), F32), ((256, 128), F32))],
        10 ** 8, 12 * 10 ** 6,
        [pltpu.VMEM((16, 64), jnp.int32), pltpu.VMEM((16, 128), jnp.int32), pltpu.VMEM((32, 16, 256), BF), dma((7,))],
    )(in_hbm(columns.T), in_hbm(owners), in_hbm(interpolation), got, in_hbm(innovation), in_hbm(obs_weight), part)
    onehot, onehot_t, place_hi, place_lo, interp, innov, weight, innov_own, live_own = [in_vmem(a) for a in kept]

    (inc_my,) = call(
        add_body, [VM, VM, ANY], [(shape((8, 1024), BF), VM)], 10 ** 4, 10 ** 5
    )(part, over(part, 2), place_hi)
    inc_mt = over(inc_my, 1)
    adj_my, adj_mt, image = call(
        obs_body, [VM] * 7 + [HB],
        [(shape((8, 1024), F32), VM)] * 2 + [(pltpu.VMEM((64, 256), F32), VM)],
        10 ** 9, 12 * 10 ** 6,
        [pltpu.VMEM((64, 256), BF), pltpu.VMEM((64, 256), BF), pltpu.VMEM((64, 256), F32),
         pltpu.VMEM((32, 256, 256), BF), dma((8,))],
    )(inc_my, inc_mt, onehot, onehot_t, innov, weight, interp, in_hbm(interpolation))

    (slots,) = call(
        slots_body, [VM] * 3, [(pltpu.VMEM((256, 256), F32), VM)], 10 ** 7, 5 * 10 ** 5
    )(place_hi, place_lo, in_vmem(image))
    g_mt, g_my = call(
        gradient_body, [VM] * 8, [(shape((32, 56), F32), VM)] * 2, 5 * 10 ** 8, 2 * 10 ** 6
    )(adj_my, over(adj_mt, 1), m_my, m1, m2, m3, e0, e1)

    (sent,) = call(
        pack_body, [VM] * 3, [(shape((64, 16, 128), BF), VM)], 10 ** 5, 6 * 10 ** 5
    )(g_my, over(g_mt, 1), in_vmem(slots))
    groups = [[(2 * z + core) * 32 + t for z in range(2) for t in range(32)] for core in range(2)]
    arrived = lax.all_to_all(
        sent, ("band", "mem"), split_axis=0, concat_axis=0, axis_index_groups=groups, tiled=True)
    gradient_t, departures = call(
        lambda *refs: final_body(scale, *refs), [VM] * 4,
        [(shape((16, 112), F32), VM), (shape((1, 256, 128), F32), VM)], 10 ** 6, 6 * 10 ** 5,
    )(arrived, control.T, innov_own, live_own)
    return (gradient_t.T, departures)


def solution(mesh):
    return jax.shard_map(
        per_device,
        mesh=mesh,
        in_specs=(
            P("band", None, "mem"),
            P("band", None, "mem"),
            P(),
            P("mem", None),
            P("mem", None, None),
            P(),
            P("mem", None, None),
            P("mem", None, None),
        ),
        out_specs=(P(None, "band"), P("mem", None, "band")),
        check_vma=False,
    )
```

```python
import math

import jax
import jax.numpy as jnp
from jax import lax
from jax.experimental import pallas as pl
from jax.experimental.pallas import tpu as pltpu
from jax.sharding import PartitionSpec as P

BF = jnp.bfloat16
F32 = jnp.float32
NN = (((1,), (0,)), ((), ()))
NT = (((1,), (1,)), ((), ()))
TN = (((0,), (0,)), ((), ()))
MIB = 1024 * 1024
VM = pl.BlockSpec(memory_space=pltpu.VMEM)
ANY = pl.BlockSpec(memory_space=pl.ANY)
HB = pl.BlockSpec(memory_space=pltpu.HBM)


def dot(a, b, dims=NN):
    return lax.dot_general(a, b, dims, preferred_element_type=F32)


def parts3(x):
    hi = x.astype(BF)
    rest = x - hi.astype(F32)
    mid = rest.astype(BF)
    lo = (rest - mid.astype(F32)).astype(BF)
    return hi, mid, lo


def iota(dims, dim):
    return lax.broadcasted_iota(jnp.int32, dims, dim)


def ones_where(cond):
    return cond.astype(F32).astype(BF)


def shape(dims, dtype):
    return jax.ShapeDtypeStruct(dims, dtype)


def in_hbm(x):
    return pltpu.with_memory_space_constraint(x, pltpu.HBM)


def in_vmem(x):
    return pltpu.with_memory_space_constraint(x, pltpu.VMEM)


def call(body, ins, outs, flops, nbytes, scratch=(), vmem=16):
    return pl.pallas_call(
        body,
        out_shape=tuple(o for o, _ in outs),
        in_specs=list(ins),
        out_specs=tuple(s for _, s in outs),
        scratch_shapes=list(scratch),
        compiler_params=pltpu.CompilerParams(vmem_limit_bytes=vmem * MIB),
        cost_estimate=pl.CostEstimate(flops=flops, bytes_accessed=nbytes, transcendentals=0),
    )


def start_all(copies):
    for c in copies:
        c.start()
    return copies


def wait_all(copies):
    for c in copies:
        c.wait()


def halves_copies(src, mine, mate, sem, at):
    core = lax.axis_index("band") & 1
    lo = pl.multiple_of(core * 8, 8)
    hi = pl.multiple_of(8 - core * 8, 8)
    return [
        pltpu.make_async_copy(src.at[:, pl.ds(hi, 8), :], mate, sem.at[at]),
        pltpu.make_async_copy(src.at[:, pl.ds(lo, 8), :], mine, sem.at[at + 1]),
    ]


def quarter_at(side):
    core = lax.axis_index("band") & 1
    return pl.ds(pl.multiple_of((core + 2 * side) * 128, 128), 128)


def split_body(mem, eig, m_mine, m_mate, e_mine, e_mate, sem):
    wait_all(start_all(halves_copies(mem, m_mine, m_mate, sem, 0) + halves_copies(eig, e_mine, e_mate, sem, 2)))


def load_body(innovation, obs_weight, _, payload, iv, sem):
    copies = start_all([
        pltpu.make_async_copy(
            a.at[0, :, quarter_at(side)], iv.at[n, :, side * 128:(side + 1) * 128], sem.at[2 * n + side])
        for n, a in enumerate((innovation, obs_weight)) for side in range(2)
    ])
    for n in range(2):
        wait_all(copies[2 * n:2 * n + 2])
        payload[:, n * 8:(n + 1) * 8, :] = iv[n].reshape(32, 8, 256).astype(BF)


def increment_of(scale, kron, ma, mb, ea, eb, cut):
    mixed = dot(kron, jnp.concatenate([ma[:, cut], mb[:, cut]], axis=0))
    total = jnp.sum((mixed[:224] * ea[:, cut].astype(F32)).reshape(28, 8, 256), axis=0)
    total = total + jnp.sum((mixed[224:] * eb[:, cut].astype(F32)).reshape(28, 8, 256), axis=0)
    return scale * total


def increment_own(scale, control_t, ma, mb, ea, eb, out, kron, ct, sem):
    get = pltpu.make_async_copy(control_t, ct, sem)
    get.start()
    band = lax.axis_index("band")
    row = iota((448, 112), 0)
    second = (row >= 224).astype(jnp.int32)
    mode = (band ^ second) * 28 + ((row - 224 * second) >> 3)
    pick_rows = ones_where(mode == iota((448, 112), 1))
    col = iota((64, 512), 1)
    member = (band ^ (col >> 7)) * 16 + ((col & 127) >> 3)
    pick_cols = ones_where(member == iota((64, 512), 0))
    same = (iota((448, 512), 0) & 7) == (iota((448, 512), 1) & 7)
    get.wait()
    rows = dot(pick_rows, ct[...].astype(BF), NT).astype(BF)
    full = jnp.where(same, dot(rows, pick_cols), 0.0).astype(BF)
    kron[...] = full[:, 256:]
    for g in range(0, 1024, 256):
        cut = slice(g, g + 256)
        out[:, cut] = increment_of(scale, full[:, :256], ma, mb, ea, eb, cut)


def increment_other(scale, kron, before, ma, mb, ea, eb, _, out):
    for g in range(0, 1024, 256):
        cut = slice(g, g + 256)
        out[:, cut] = before[:, cut] + increment_of(scale, kron[...], ma, mb, ea, eb, cut)


def prep_body(columns_t, owners_in, interpolation, got_in, innovation, obs_weight, _,
              onehot, onehot_t, place_hi, place_lo, interp, innov, weight, innov_own, live_own,
              cols_s, own_s, got, sem):
    band = lax.axis_index("band")
    tile = lax.axis_index("mem")
    quarter = pl.ds(pl.multiple_of(band * 128, 128), 128)
    small = [(columns_t, cols_s), (owners_in, own_s), (got_in, got)]
    mid = [(innovation.at[0, :, quarter], innov_own), (obs_weight.at[0, :, quarter], live_own)]
    big = [(interpolation.at[:32, :, quarter_at(side)], interp.at[:, :, side * 128:(side + 1) * 128]) for side in range(2)]
    copies = start_all([pltpu.make_async_copy(a, b, sem.at[n]) for n, (a, b) in enumerate(small + mid + big)])
    wait_all(copies[:3])
    t = iota((64, 1024), 1)
    cols = cols_s[...].astype(F32).T.astype(jnp.int32)
    for c in range(16):
        onehot[c * 64:(c + 1) * 64, :] = ones_where(cols[:, c:c + 1] == t)
    flat = jnp.concatenate([cols_s[c:c + 1, :] for c in range(16)], axis=1)
    for r in range(0, 1024, 128):
        onehot_t[r:r + 128, :] = ones_where(flat == iota((128, 1024), 0) + r)
    pair = own_s[pl.ds(tile >> 1, 1), :].astype(F32)
    own = jnp.where((tile & 1) == 1, pair[:, 64:], pair[:, :64])
    own_row = jnp.broadcast_to(own, (64, 64))
    own_col = own_row.T
    earlier = iota((64, 64), 1) < iota((64, 64), 0)
    rank = jnp.sum(jnp.where((own_row == own_col) & earlier, 1.0, 0.0), axis=1, keepdims=True)
    target = (own_col[:, :1] * 8.0 + rank).astype(jnp.int32)
    sel = ones_where(target == iota((64, 256), 1))
    slot = iota((64, 256), 1)
    half = 4 * (band >> 1)
    place_hi[...] = ones_where((target == slot + half) & ((slot & 7) < 4))
    place_lo[...] = ones_where((target == slot + half - 4) & ((slot & 7) >= 4))
    x = got[...].astype(F32)
    innov[...] = dot(sel, x[:, :8].reshape(256, 256).astype(BF))
    weight[...] = dot(sel, x[:, 8:].reshape(256, 256).astype(BF))
    hit = ones_where(own_s[...] == tile)
    pair = ones_where((iota((256, 16), 0) >> 4) == iota((256, 16), 1))
    odd = (iota((256, 128), 0) >> 3) & 1
    side = jnp.where((iota((256, 128), 1) >> 6) == odd, dot(pair, hit), 0.0)
    count = jnp.sum(side, axis=1, keepdims=True)
    live = jnp.where((iota((256, 1), 0) & 7).astype(F32) < count, 1.0, 0.0)
    wait_all(copies[3:5])
    live_own[...] = live * live_own[...]
    wait_all(copies[5:])


def add_body(a, b, _, out):
    out[...] = (a[...] + b[...]).astype(BF)


def obs_body(inc_my, inc_mt, onehot, onehot_t, innov, weight, near, interpolation,
             adj_my, adj_mt, image_out, picked, depb, spread, far, sem):
    fetch = [
        start_all([
            pltpu.make_async_copy(
                interpolation.at[32 + j:40 + j, :, quarter_at(side)],
                far.at[j:j + 8, :, side * 128:(side + 1) * 128], sem.at[j // 4 + side])
            for side in range(2)
        ]) for j in range(0, 32, 8)
    ]

    def block(j):
        return near[j] if j < 32 else far[j - 32]

    band = lax.axis_index("band")
    first = (band & 1) == 0
    mine = inc_my[...].astype(F32)
    mate = inc_mt[...].astype(F32)
    inc = jnp.concatenate([jnp.where(first, mine, mate), jnp.where(first, mate, mine)], axis=0).astype(BF)
    r0 = iota((256, 256), 0)
    r1 = iota((256, 256), 1)
    swap = ones_where(((r0 & 15) * 16 + (r0 >> 4)) == r1)
    picks = dot(inc, onehot_t[...])
    by_col = jnp.concatenate([picks[:, c * 64:(c + 1) * 64] for c in range(16)], axis=0).astype(BF)
    picked[...] = dot(by_col, swap, TN).astype(BF)
    rows = iota((16, 256), 0)
    image = []
    for b in range(4):
        lhs = picked[b * 16:(b + 1) * 16, :]
        acc = jnp.zeros((16, 256), F32)
        for i in range(16):
            j = b * 16 + i
            if j >= 32 and j % 8 == 0:
                wait_all(fetch[(j - 32) // 8])
            acc = jnp.where(rows == i, dot(lhs, block(j)), acc)
        image.append(acc)
    image = jnp.concatenate(image, axis=0)
    image_out[...] = image
    depb[...] = (weight[...] * (innov[...] - image)).astype(BF)
    for b in range(4):
        lhs = depb[b * 16:(b + 1) * 16, :]
        acc = jnp.zeros((16, 256), F32)
        for i in range(16):
            acc = jnp.where(rows == i, dot(lhs, block(b * 16 + i), NT), acc)
        spread[b * 16:(b + 1) * 16, :] = acc
    x = spread[...]
    hi = x.astype(BF)
    lo = (x - hi.astype(F32)).astype(BF)
    terms = []
    for part in (hi, lo):
        turned = dot(swap, part, NT)
        terms.append(jnp.concatenate([turned[c * 16:(c + 1) * 16] for c in range(16)], axis=1))
    both = dot(jnp.concatenate(terms, axis=0).astype(BF), onehot[...])
    adj = both[:16] + both[16:]
    adj_my[...] = jnp.where(first, adj[:8], adj[8:])
    adj_mt[...] = jnp.where(first, adj[8:], adj[:8])


def slots_body(place_hi, place_lo, image, out):
    hi, lo, _ = parts3(image[...])
    out[...] = dot(place_hi[...], hi, TN) + dot(place_lo[...], lo, TN)


def gradient_body(a0, a1, m0, m1, m2, m3, e0, e1, mate, mine):
    first = (lax.axis_index("band") & 1) == 0
    adj = a0[...] + a1[...]
    wide = jnp.broadcast_to(adj[None], (16, 8, 1024)).reshape(128, 1024)
    same = (iota((448, 256), 0) & 7) == (iota((448, 256), 1) & 7)
    sel = ones_where((iota((32, 256), 1) >> 3) == iota((32, 256), 0))
    eig = jnp.concatenate([e0[...], e1[...]], axis=0)
    for ma, mb, g in ((m1, m3, mate), (m0, m2, mine)):
        weighted = jnp.concatenate(
            [(m[...].astype(F32) * wide).astype(BF) for m in (ma, mb)], axis=0)
        full = jnp.where(same, dot(eig, weighted, NT), 0.0)
        own = jnp.sum(full.reshape(56, 8, 256), axis=1)
        own = jnp.where(first, own, jnp.concatenate([own[28:], own[:28]], axis=0))
        hi, mid, _ = parts3(own)
        g[...] = dot(sel, hi, NT) + dot(sel, mid, NT)


def pack_body(mine, came, slots, out):
    total = mine[...] + came[...]
    gap = jnp.zeros((8, 8), F32)
    flat = [
        jnp.concatenate([total[r:r + 8], gap, total[r + 8:r + 16], gap], axis=1) for r in (0, 16)
    ]
    high = (lax.axis_index("band") >> 1) == 1
    for side in range(2):
        here = high if side else jnp.logical_not(high)
        term = jnp.broadcast_to(jnp.where(here, flat[0], flat[1])[None], (32, 8, 128))
        image = slots[:, side * 128:(side + 1) * 128].reshape(32, 8, 128)
        out[side * 32:(side + 1) * 32] = jnp.concatenate([term, image], axis=1).astype(BF)


def final_body(scale, got, control_t, innov, live, gradient_t, departures):
    band = lax.axis_index("band")
    sums, halves = [], []
    for side in range(2):
        x = got[side * 32:(side + 1) * 32].astype(F32)
        sums.append(jnp.sum(x[:, :8], axis=0))
        halves.append(x[:, 8:12] + x[:, 12:])
    image = jnp.concatenate(halves, axis=1).reshape(256, 128)
    departures[...] = (live[...] * (innov[...] - image)).reshape(1, 256, 128)
    low, top = sums
    total = jnp.concatenate([
        jnp.concatenate([low[:, :56], top[:, :56]], axis=1),
        jnp.concatenate([low[:, 64:120], top[:, 64:120]], axis=1),
    ], axis=0)
    own = ones_where(iota((16, 64), 1) == band * 16 + iota((16, 64), 0))
    hi, mid, lo = parts3(control_t[...])
    gradient_t[...] = dot(own, hi) + dot(own, mid) + dot(own, lo) - scale * total


def per_device(members, eigvecs, control, columns, interpolation, owners, innovation, obs_weight):
    scale = 1.0 / math.sqrt(112 * 64)
    owners = owners.reshape(16, 128)

    def over(x, bit):
        return lax.ppermute(x, "band", [(i, i ^ bit) for i in range(4)])

    dma = pltpu.SemaphoreType.DMA
    m_my, m_mt, e_my, e_mt = call(
        split_body, [HB] * 2,
        [(pltpu.VMEM((16, 8, 1024), BF), VM)] * 2 + [(pltpu.VMEM((28, 8, 1024), BF), VM)] * 2, 0, 0, [dma((4,))],
    )(in_hbm(members), in_hbm(eigvecs))
    m_my, m_mt, e0, e_mt = [in_vmem(a.reshape(-1, 1024)) for a in (m_my, m_mt, e_my, e_mt)]
    m3 = over(m_mt, 3)
    m2 = over(m_my, 2)
    m1 = over(m_mt, 1)
    (payload,) = call(
        load_body, [HB] * 2 + [ANY], [(pltpu.HBM((32, 16, 256), BF), VM)],
        0, 0, [pltpu.VMEM((2, 256, 256), F32), dma((4,))],
    )(in_hbm(innovation), in_hbm(obs_weight), m_my)
    got = lax.all_to_all(payload, "mem", split_axis=0, concat_axis=0, tiled=True)
    e1 = over(e_mt, 1)
    m1, m2, m3, e1 = [in_vmem(a) for a in (m1, m2, m3, e1)]

    part, kron = call(
        lambda *refs: increment_own(scale, *refs), [HB] + [VM] * 4,
        [(pltpu.VMEM((8, 1024), F32), VM), (pltpu.VMEM((448, 256), BF), VM)],
        25 * 10 ** 7, 2 * 10 ** 6, [pltpu.VMEM((64, 112), F32), dma(())],
    )(in_hbm(control.T), m_my, m1, e0, e1)
    (part,) = call(
        lambda *refs: increment_other(scale, *refs), [VM] * 6 + [ANY], [(shape((8, 1024), F32), VM)],
        25 * 10 ** 7, 2 * 10 ** 6,
    )(in_vmem(kron), in_vmem(part), m2, m3, e0, e1, m3)

    kept = call(
        prep_body,
        [HB] * 3 + [ANY] + [HB] * 2 + [ANY],
        [(pltpu.VMEM(d, t), VM) for d, t in (
            ((1024, 1024), BF), ((1024, 1024), BF), ((64, 256), BF), ((64, 256), BF), ((32, 256, 256), BF), ((64, 256), F32), ((64, 256), F32),
            ((256, 128), F32), ((256, 128), F32))],
        10 ** 8, 12 * 10 ** 6,
        [pltpu.VMEM((16, 64), jnp.int32), pltpu.VMEM((16, 128), jnp.int32), pltpu.VMEM((32, 16, 256), BF), dma((7,))],
    )(in_hbm(columns.T), in_hbm(owners), in_hbm(interpolation), got, in_hbm(innovation), in_hbm(obs_weight), part)
    onehot, onehot_t, place_hi, place_lo, interp, innov, weight, innov_own, live_own = [in_vmem(a) for a in kept]

    (inc_my,) = call(
        add_body, [VM, VM, ANY], [(shape((8, 1024), BF), VM)], 10 ** 4, 10 ** 5
    )(part, over(part, 2), place_hi)
    inc_mt = over(inc_my, 1)
    adj_my, adj_mt, image = call(
        obs_body, [VM] * 7 + [HB],
        [(shape((8, 1024), F32), VM)] * 2 + [(pltpu.VMEM((64, 256), F32), VM)],
        10 ** 9, 12 * 10 ** 6,
        [pltpu.VMEM((64, 256), BF), pltpu.VMEM((64, 256), BF), pltpu.VMEM((64, 256), F32),
         pltpu.VMEM((32, 256, 256), BF), dma((8,))],
    )(inc_my, inc_mt, onehot, onehot_t, innov, weight, interp, in_hbm(interpolation))

    (slots,) = call(
        slots_body, [VM] * 3, [(pltpu.VMEM((256, 256), F32), VM)], 10 ** 7, 5 * 10 ** 5
    )(place_hi, place_lo, in_vmem(image))
    g_mt, g_my = call(
        gradient_body, [VM] * 8, [(shape((32, 56), F32), VM)] * 2, 5 * 10 ** 8, 2 * 10 ** 6
    )(adj_my, over(adj_mt, 1), m_my, m1, m2, m3, e0, e1)

    (sent,) = call(
        pack_body, [VM] * 3, [(shape((64, 16, 128), BF), VM)], 10 ** 5, 6 * 10 ** 5
    )(g_my, over(g_mt, 1), in_vmem(slots))
    groups = [[(2 * z + core) * 32 + t for z in range(2) for t in range(32)] for core in range(2)]
    arrived = lax.all_to_all(
        sent, ("band", "mem"), split_axis=0, concat_axis=0, axis_index_groups=groups, tiled=True)
    gradient_t, departures = call(
        lambda *refs: final_body(scale, *refs), [VM] * 4,
        [(shape((16, 112), F32), VM), (shape((1, 256, 128), F32), VM)], 10 ** 6, 6 * 10 ** 5,
    )(arrived, control.T, innov_own, live_own)
    return (gradient_t.T, departures)


def solution(mesh):
    return jax.shard_map(
        per_device,
        mesh=mesh,
        in_specs=(
            P("band", None, "mem"),
            P("band", None, "mem"),
            P(),
            P("mem", None),
            P("mem", None, None),
            P(),
            P("mem", None, None),
            P("mem", None, None),
        ),
        out_specs=(P(None, "band"), P("mem", None, "band")),
        check_vma=False,
    )
```

```python
import math

import jax
import jax.numpy as jnp
from jax import lax
from jax.experimental import pallas as pl
from jax.experimental.pallas import tpu as pltpu
from jax.sharding import PartitionSpec as P

BF = jnp.bfloat16
F32 = jnp.float32
NN = (((1,), (0,)), ((), ()))
NT = (((1,), (1,)), ((), ()))
TN = (((0,), (0,)), ((), ()))
MIB = 1024 * 1024
VM = pl.BlockSpec(memory_space=pltpu.VMEM)
ANY = pl.BlockSpec(memory_space=pl.ANY)
HB = pl.BlockSpec(memory_space=pltpu.HBM)


def dot(a, b, dims=NN):
    return lax.dot_general(a, b, dims, preferred_element_type=F32)


def parts3(x):
    hi = x.astype(BF)
    rest = x - hi.astype(F32)
    mid = rest.astype(BF)
    lo = (rest - mid.astype(F32)).astype(BF)
    return hi, mid, lo


def iota(dims, dim):
    return lax.broadcasted_iota(jnp.int32, dims, dim)


def ones_where(cond):
    return cond.astype(F32).astype(BF)


def shape(dims, dtype):
    return jax.ShapeDtypeStruct(dims, dtype)


def in_hbm(x):
    return pltpu.with_memory_space_constraint(x, pltpu.HBM)


def in_vmem(x):
    return pltpu.with_memory_space_constraint(x, pltpu.VMEM)


def call(body, ins, outs, flops, nbytes, scratch=(), vmem=16, aliases=None):
    return pl.pallas_call(
        body,
        out_shape=tuple(o for o, _ in outs),
        in_specs=list(ins),
        out_specs=tuple(s for _, s in outs),
        scratch_shapes=list(scratch),
        input_output_aliases=aliases or {},
        compiler_params=pltpu.CompilerParams(vmem_limit_bytes=vmem * MIB),
        cost_estimate=pl.CostEstimate(flops=flops, bytes_accessed=nbytes, transcendentals=0),
    )


def start_all(copies):
    for c in copies:
        c.start()
    return copies


def wait_all(copies):
    for c in copies:
        c.wait()


def halves_copies(src, mine, mate, sem, at):
    core = lax.axis_index("band") & 1
    lo = pl.multiple_of(core * 8, 8)
    hi = pl.multiple_of(8 - core * 8, 8)
    return [
        pltpu.make_async_copy(src.at[:, pl.ds(hi, 8), :], mate, sem.at[at]),
        pltpu.make_async_copy(src.at[:, pl.ds(lo, 8), :], mine, sem.at[at + 1]),
    ]


def quarter_at(side):
    core = lax.axis_index("band") & 1
    return pl.ds(pl.multiple_of((core + 2 * side) * 128, 128), 128)


def split_body(mem, eig, innovation, obs_weight, m_mine, m_mate, e_mine, e_mate, iv, sem):
    copies = halves_copies(mem, m_mine, m_mate, sem, 0) + halves_copies(eig, e_mine, e_mate, sem, 2) + [
        pltpu.make_async_copy(
            a.at[0, :, quarter_at(side)], iv.at[n, :, side * 128:(side + 1) * 128], sem.at[4 + 2 * n + side])
        for n, a in enumerate((innovation, obs_weight)) for side in range(2)
    ]
    wait_all(start_all(copies))


def load_body(iv, _, payload):
    for n in range(2):
        payload[:, n * 8:(n + 1) * 8, :] = iv[n].reshape(32, 8, 256).astype(BF)


def increment_of(scale, kron, ma, mb, ea, eb, cut):
    mixed = dot(kron, jnp.concatenate([ma[:, cut], mb[:, cut]], axis=0))
    total = jnp.sum((mixed[:224] * ea[:, cut].astype(F32)).reshape(28, 8, 256), axis=0)
    total = total + jnp.sum((mixed[224:] * eb[:, cut].astype(F32)).reshape(28, 8, 256), axis=0)
    return scale * total


def increment_own(scale, control_t, ma, mb, ea, eb, out, kron, ct, sem):
    get = pltpu.make_async_copy(control_t, ct, sem)
    get.start()
    band = lax.axis_index("band")
    row = iota((448, 112), 0)
    second = (row >= 224).astype(jnp.int32)
    mode = (band ^ second) * 28 + ((row - 224 * second) >> 3)
    pick_rows = ones_where(mode == iota((448, 112), 1))
    col = iota((64, 512), 1)
    member = (band ^ (col >> 7)) * 16 + ((col & 127) >> 3)
    pick_cols = ones_where(member == iota((64, 512), 0))
    same = (iota((448, 512), 0) & 7) == (iota((448, 512), 1) & 7)
    get.wait()
    rows = dot(pick_rows, ct[...].astype(BF), NT).astype(BF)
    full = jnp.where(same, dot(rows, pick_cols), 0.0).astype(BF)
    kron[...] = full[:, 256:]
    for g in range(0, 1024, 256):
        cut = slice(g, g + 256)
        out[:, cut] = increment_of(scale, full[:, :256], ma, mb, ea, eb, cut)


def increment_other(scale, kron, before, ma, mb, ea, eb, out):
    for g in range(0, 1024, 256):
        cut = slice(g, g + 256)
        out[:, cut] = before[:, cut] + increment_of(scale, kron[...], ma, mb, ea, eb, cut)


def prep_body(columns_t, owners_in, interpolation, got_in, innovation, obs_weight, _,
              onehot, onehot_t, place_hi, place_lo, interp, innov, weight, innov_own, live_own,
              cols_s, own_s, got, sem):
    band = lax.axis_index("band")
    tile = lax.axis_index("mem")
    quarter = pl.ds(pl.multiple_of(band * 128, 128), 128)
    small = [(columns_t, cols_s), (owners_in, own_s), (got_in, got)]
    mid = [(innovation.at[0, :, quarter], innov_own), (obs_weight.at[0, :, quarter], live_own)]
    big = [(interpolation.at[:32, :, quarter_at(side)], interp.at[:, :, side * 128:(side + 1) * 128]) for side in range(2)]
    copies = start_all([pltpu.make_async_copy(a, b, sem.at[n]) for n, (a, b) in enumerate(small + mid + big)])
    wait_all(copies[:3])
    t = iota((64, 1024), 1)
    cols = cols_s[...].astype(F32).T.astype(jnp.int32)
    for c in range(16):
        onehot[c * 64:(c + 1) * 64, :] = ones_where(cols[:, c:c + 1] == t)
    flat = jnp.concatenate([cols_s[c:c + 1, :] for c in range(16)], axis=1)
    for r in range(0, 1024, 128):
        onehot_t[r:r + 128, :] = ones_where(flat == iota((128, 1024), 0) + r)
    pair = own_s[pl.ds(tile >> 1, 1), :].astype(F32)
    own = jnp.where((tile & 1) == 1, pair[:, 64:], pair[:, :64])
    own_row = jnp.broadcast_to(own, (64, 64))
    own_col = own_row.T
    earlier = iota((64, 64), 1) < iota((64, 64), 0)
    rank = jnp.sum(jnp.where((own_row == own_col) & earlier, 1.0, 0.0), axis=1, keepdims=True)
    target = (own_col[:, :1] * 8.0 + rank).astype(jnp.int32)
    sel = ones_where(target == iota((64, 256), 1))
    slot = iota((64, 256), 1)
    half = 4 * (band >> 1)
    place_hi[...] = ones_where((target == slot + half) & ((slot & 7) < 4))
    place_lo[...] = ones_where((target == slot + half - 4) & ((slot & 7) >= 4))
    x = got[...].astype(F32)
    innov[...] = dot(sel, x[:, :8].reshape(256, 256).astype(BF))
    weight[...] = dot(sel, x[:, 8:].reshape(256, 256).astype(BF))
    hit = ones_where(own_s[...] == tile)
    pair = ones_where((iota((256, 16), 0) >> 4) == iota((256, 16), 1))
    odd = (iota((256, 128), 0) >> 3) & 1
    side = jnp.where((iota((256, 128), 1) >> 6) == odd, dot(pair, hit), 0.0)
    count = jnp.sum(side, axis=1, keepdims=True)
    live = jnp.where((iota((256, 1), 0) & 7).astype(F32) < count, 1.0, 0.0)
    wait_all(copies[3:5])
    live_own[...] = live * live_own[...]
    wait_all(copies[5:])


def add_body(a, b, _, out):
    out[...] = (a[...] + b[...]).astype(BF)


def pass_body(_, x, same_x):
    del x, same_x


def obs_body(inc_my, inc_mt, onehot, onehot_t, innov, weight, near, interpolation,
             adj_all, image_out, picked, depb, spread, far, sem):
    fetch = [
        start_all([
            pltpu.make_async_copy(
                interpolation.at[32 + j:40 + j, :, quarter_at(side)],
                far.at[j:j + 8, :, side * 128:(side + 1) * 128], sem.at[j // 4 + side])
            for side in range(2)
        ]) for j in range(0, 32, 8)
    ]

    def block(j):
        return near[j] if j < 32 else far[j - 32]

    band = lax.axis_index("band")
    first = (band & 1) == 0
    mine = inc_my[...].astype(F32)
    mate = inc_mt[...].astype(F32)
    inc = jnp.concatenate([jnp.where(first, mine, mate), jnp.where(first, mate, mine)], axis=0).astype(BF)
    r0 = iota((256, 256), 0)
    r1 = iota((256, 256), 1)
    swap = ones_where(((r0 & 15) * 16 + (r0 >> 4)) == r1)
    picks = dot(inc, onehot_t[...])
    by_col = jnp.concatenate([picks[:, c * 64:(c + 1) * 64] for c in range(16)], axis=0).astype(BF)
    picked[...] = dot(by_col, swap, TN).astype(BF)
    rows = iota((16, 256), 0)
    image = []
    for b in range(4):
        lhs = picked[b * 16:(b + 1) * 16, :]
        acc = jnp.zeros((16, 256), F32)
        for i in range(16):
            j = b * 16 + i
            if j >= 32 and j % 8 == 0:
                wait_all(fetch[(j - 32) // 8])
            acc = jnp.where(rows == i, dot(lhs, block(j)), acc)
        image.append(acc)
    image = jnp.concatenate(image, axis=0)
    image_out[...] = image
    depb[...] = (weight[...] * (innov[...] - image)).astype(BF)
    for b in range(4):
        lhs = depb[b * 16:(b + 1) * 16, :]
        acc = jnp.zeros((16, 256), F32)
        for i in range(16):
            acc = jnp.where(rows == i, dot(lhs, block(b * 16 + i), NT), acc)
        spread[b * 16:(b + 1) * 16, :] = acc
    x = spread[...]
    hi = x.astype(BF)
    lo = (x - hi.astype(F32)).astype(BF)
    terms = []
    for part in (hi, lo):
        turned = dot(swap, part, NT)
        terms.append(jnp.concatenate([turned[c * 16:(c + 1) * 16] for c in range(16)], axis=1))
    both = dot(jnp.concatenate(terms, axis=0).astype(BF), onehot[...])
    adj = both[:16] + both[16:]
    adj_all[:8] = jnp.where(first, adj[8:], adj[:8])
    adj_all[8:] = jnp.where(first, adj[:8], adj[8:])


def slots_body(place_hi, place_lo, image, out):
    hi, lo, _ = parts3(image[...])
    out[...] = dot(place_hi[...], hi, TN) + dot(place_lo[...], lo, TN)


def gradient_body(adj, came, m_my, m_mt, o_my, o_mt, e_my, e_mt, f_my, f_mt, out):
    first = (lax.axis_index("band") & 1) == 0
    same = (iota((448, 256), 0) & 7) == (iota((448, 256), 1) & 7)
    sel = ones_where((iota((32, 256), 1) >> 3) == iota((32, 256), 0))
    total = None
    for here, there, members, eigs in (
            (adj[8:], came[:8], (m_my, o_my), (e_my, f_my)), (adj[:8], came[8:], (m_mt, o_mt), (e_mt, f_mt))):
        wide = jnp.broadcast_to((here + there)[None], (16, 8, 1024)).reshape(128, 1024)
        weighted = jnp.concatenate([(m[...].astype(F32) * wide).astype(BF) for m in members], axis=0)
        term = dot(jnp.concatenate([e[...] for e in eigs], axis=0), weighted, NT)
        total = term if total is None else total + term
    own = jnp.sum(jnp.where(same, total, 0.0).reshape(56, 8, 256), axis=1)
    own = jnp.where(first, own, jnp.concatenate([own[28:], own[:28]], axis=0))
    hi, mid, _ = parts3(own)
    out[...] = dot(sel, hi, NT) + dot(sel, mid, NT)


def pack_body(mine, slots, out):
    total = mine[...]
    gap = jnp.zeros((8, 8), F32)
    flat = [
        jnp.concatenate([total[r:r + 8], gap, total[r + 8:r + 16], gap], axis=1) for r in (0, 16)
    ]
    high = (lax.axis_index("band") >> 1) == 1
    for side in range(2):
        here = high if side else jnp.logical_not(high)
        term = jnp.broadcast_to(jnp.where(here, flat[0], flat[1])[None], (32, 8, 128))
        image = slots[:, side * 128:(side + 1) * 128].reshape(32, 8, 128)
        out[side * 32:(side + 1) * 32] = jnp.concatenate([term, image], axis=1).astype(BF)


def final_body(scale, got, control_t, innov, live, gradient_t, departures):
    band = lax.axis_index("band")
    sums, halves = [], []
    for side in range(2):
        x = got[side * 32:(side + 1) * 32].astype(F32)
        sums.append(jnp.sum(x[:, :8], axis=0))
        halves.append(x[:, 8:12] + x[:, 12:])
    image = jnp.concatenate(halves, axis=1).reshape(256, 128)
    departures[...] = (live[...] * (innov[...] - image)).reshape(1, 256, 128)
    low, top = sums
    total = jnp.concatenate([
        jnp.concatenate([low[:, :56], top[:, :56]], axis=1),
        jnp.concatenate([low[:, 64:120], top[:, 64:120]], axis=1),
    ], axis=0)
    own = ones_where(iota((16, 64), 1) == band * 16 + iota((16, 64), 0))
    hi, mid, lo = parts3(control_t[...])
    gradient_t[...] = dot(own, hi) + dot(own, mid) + dot(own, lo) - scale * total


def per_device(members, eigvecs, control, columns, interpolation, owners, innovation, obs_weight):
    scale = 1.0 / math.sqrt(112 * 64)
    owners = owners.reshape(16, 128)

    def over(x, bit):
        return lax.ppermute(x, "band", [(i, i ^ bit) for i in range(4)])

    dma = pltpu.SemaphoreType.DMA
    m_my, m_mt, e_my, e_mt, iv = call(
        split_body, [HB] * 4,
        [(pltpu.VMEM((16, 8, 1024), BF), VM)] * 2 + [(pltpu.VMEM((28, 8, 1024), BF), VM)] * 2
        + [(pltpu.VMEM((2, 256, 256), F32), VM)], 0, 0, [dma((8,))],
    )(in_hbm(members), in_hbm(eigvecs), in_hbm(innovation), in_hbm(obs_weight))
    m_my, m_mt, e0, e_mt = [in_vmem(a.reshape(-1, 1024)) for a in (m_my, m_mt, e_my, e_mt)]
    m3 = over(m_mt, 3)
    m2 = over(m_my, 2)
    m1 = over(m_mt, 1)
    (payload,) = call(
        load_body, [VM, ANY], [(pltpu.VMEM((32, 16, 256), BF), VM)], 0, 0,
    )(in_vmem(iv), m_my)
    got = lax.all_to_all(payload, "mem", split_axis=0, concat_axis=0, tiled=True)
    e1 = over(e_mt, 1)
    m1, m2, m3, e1 = [in_vmem(a) for a in (m1, m2, m3, e1)]

    part, kron = call(
        lambda *refs: increment_own(scale, *refs), [HB] + [VM] * 4,
        [(pltpu.VMEM((8, 1024), F32), VM), (pltpu.VMEM((448, 256), BF), VM)],
        25 * 10 ** 7, 2 * 10 ** 6, [pltpu.VMEM((64, 112), F32), dma(())],
    )(in_hbm(control.T), m_my, m1, e0, e1)
    (part,) = call(
        lambda *refs: increment_other(scale, *refs), [VM] * 6, [(shape((8, 1024), F32), VM)],
        25 * 10 ** 7, 2 * 10 ** 6,
    )(in_vmem(kron), in_vmem(part), m2, m3, e0, e1)

    kept = call(
        prep_body,
        [HB] * 3 + [ANY] + [HB] * 2 + [ANY],
        [(pltpu.VMEM(d, t), VM) for d, t in (
            ((1024, 1024), BF), ((1024, 1024), BF), ((64, 256), BF), ((64, 256), BF), ((32, 256, 256), BF), ((64, 256), F32), ((64, 256), F32),
            ((256, 128), F32), ((256, 128), F32))],
        10 ** 8, 12 * 10 ** 6,
        [pltpu.VMEM((16, 64), jnp.int32), pltpu.VMEM((16, 128), jnp.int32), pltpu.VMEM((32, 16, 256), BF), dma((7,))],
    )(in_hbm(columns.T), in_hbm(owners), in_hbm(interpolation), got, in_hbm(innovation), in_hbm(obs_weight), part)
    onehot, onehot_t, place_hi, place_lo, interp, innov, weight, innov_own, live_own = [in_vmem(a) for a in kept]

    (inc_my,) = call(
        add_body, [VM, VM, ANY], [(shape((8, 1024), BF), VM)], 10 ** 4, 10 ** 5,
    )(part, over(part, 2), place_hi)
    inc_mt = over(inc_my, 1)
    (m3,) = call(
        pass_body, [ANY, VM], [(pltpu.VMEM((128, 1024), BF), VM)], 0, 0, aliases={1: 0}
    )(inc_mt, m3)
    adj, image = call(
        obs_body, [VM] * 7 + [HB],
        [(shape((16, 1024), F32), VM), (pltpu.VMEM((64, 256), F32), VM)],
        10 ** 9, 12 * 10 ** 6,
        [pltpu.VMEM((64, 256), BF), pltpu.VMEM((64, 256), BF), pltpu.VMEM((64, 256), F32),
         pltpu.VMEM((32, 256, 256), BF), dma((8,))],
    )(inc_my, inc_mt, onehot, onehot_t, innov, weight, interp, in_hbm(interpolation))

    (slots,) = call(
        slots_body, [VM] * 3, [(pltpu.VMEM((256, 256), F32), VM)], 10 ** 7, 5 * 10 ** 5
    )(place_hi, place_lo, in_vmem(image))
    f_mt = over(e0, 1)
    o_mt = over(in_vmem(m3), 1)
    (terms,) = call(
        gradient_body, [VM] * 10, [(shape((32, 56), F32), VM)], 5 * 10 ** 8, 2 * 10 ** 6
    )(adj, over(adj, 1), m_my, m_mt, m2, o_mt, e0, e_mt, e1, f_mt)

    (sent,) = call(
        pack_body, [VM] * 2, [(shape((64, 16, 128), BF), VM)], 10 ** 5, 6 * 10 ** 5
    )(terms, in_vmem(slots))
    groups = [[(2 * z + core) * 32 + t for z in range(2) for t in range(32)] for core in range(2)]
    arrived = lax.all_to_all(
        sent, ("band", "mem"), split_axis=0, concat_axis=0, axis_index_groups=groups, tiled=True)
    gradient_t, departures = call(
        lambda *refs: final_body(scale, *refs), [VM] * 4,
        [(shape((16, 112), F32), VM), (shape((1, 256, 128), F32), VM)], 10 ** 6, 6 * 10 ** 5,
    )(arrived, control.T, innov_own, live_own)
    return (gradient_t.T, departures)


def solution(mesh):
    return jax.shard_map(
        per_device,
        mesh=mesh,
        in_specs=(
            P("band", None, "mem"),
            P("band", None, "mem"),
            P(),
            P("mem", None),
            P("mem", None, None),
            P(),
            P("mem", None, None),
            P("mem", None, None),
        ),
        out_specs=(P(None, "band"), P("mem", None, "band")),
        check_vma=False,
    )
```

```python
import math

import jax
import jax.numpy as jnp
from jax import lax
from jax.experimental import pallas as pl
from jax.experimental.pallas import tpu as pltpu
from jax.sharding import PartitionSpec as P

BF = jnp.bfloat16
F32 = jnp.float32
NN = (((1,), (0,)), ((), ()))
NT = (((1,), (1,)), ((), ()))
TN = (((0,), (0,)), ((), ()))
MIB = 1024 * 1024
VM = pl.BlockSpec(memory_space=pltpu.VMEM)
ANY = pl.BlockSpec(memory_space=pl.ANY)
HB = pl.BlockSpec(memory_space=pltpu.HBM)


def dot(a, b, dims=NN):
    return lax.dot_general(a, b, dims, preferred_element_type=F32)


def parts3(x):
    hi = x.astype(BF)
    rest = x - hi.astype(F32)
    mid = rest.astype(BF)
    lo = (rest - mid.astype(F32)).astype(BF)
    return hi, mid, lo


def iota(dims, dim):
    return lax.broadcasted_iota(jnp.int32, dims, dim)


def ones_where(cond):
    return cond.astype(F32).astype(BF)


def shape(dims, dtype):
    return jax.ShapeDtypeStruct(dims, dtype)


def in_hbm(x):
    return pltpu.with_memory_space_constraint(x, pltpu.HBM)


def in_vmem(x):
    return pltpu.with_memory_space_constraint(x, pltpu.VMEM)


def call(body, ins, outs, flops, nbytes, scratch=(), vmem=16, aliases=None):
    return pl.pallas_call(
        body,
        out_shape=tuple(o for o, _ in outs),
        in_specs=list(ins),
        out_specs=tuple(s for _, s in outs),
        scratch_shapes=list(scratch),
        input_output_aliases=aliases or {},
        compiler_params=pltpu.CompilerParams(vmem_limit_bytes=vmem * MIB),
        cost_estimate=pl.CostEstimate(flops=flops, bytes_accessed=nbytes, transcendentals=0),
    )


def start_all(copies):
    for c in copies:
        c.start()
    return copies


def wait_all(copies):
    for c in copies:
        c.wait()


def halves_copies(src, mine, mate, sem, at):
    core = lax.axis_index("band") & 1
    lo = pl.multiple_of(core * 8, 8)
    hi = pl.multiple_of(8 - core * 8, 8)
    return [
        pltpu.make_async_copy(src.at[:, pl.ds(hi, 8), :], mate, sem.at[at]),
        pltpu.make_async_copy(src.at[:, pl.ds(lo, 8), :], mine, sem.at[at + 1]),
    ]


def quarter_at(side):
    core = lax.axis_index("band") & 1
    return pl.ds(pl.multiple_of((core + 2 * side) * 128, 128), 128)


def split_body(mem, eig, innovation, obs_weight, m_mine, m_mate, e_mine, e_mate, iv, sem):
    copies = halves_copies(mem, m_mine, m_mate, sem, 0) + halves_copies(eig, e_mine, e_mate, sem, 2) + [
        pltpu.make_async_copy(
            a.at[0, :, quarter_at(side)], iv.at[n, :, side * 128:(side + 1) * 128], sem.at[4 + 2 * n + side])
        for n, a in enumerate((innovation, obs_weight)) for side in range(2)
    ]
    wait_all(start_all(copies))


def load_body(iv, _, payload):
    for n in range(2):
        payload[:, n * 8:(n + 1) * 8, :] = iv[n].reshape(32, 8, 256).astype(BF)


def increment_of(scale, kron, ma, mb, ea, eb, cut):
    mixed = dot(kron, jnp.concatenate([ma[:, cut], mb[:, cut]], axis=0))
    total = jnp.sum((mixed[:224] * ea[:, cut].astype(F32)).reshape(28, 8, 256), axis=0)
    total = total + jnp.sum((mixed[224:] * eb[:, cut].astype(F32)).reshape(28, 8, 256), axis=0)
    return scale * total


def increment_own(scale, control_t, ma, mb, ea, eb, out, kron, ct, sem):
    get = pltpu.make_async_copy(control_t, ct, sem)
    get.start()
    band = lax.axis_index("band")
    row = iota((448, 112), 0)
    second = (row >= 224).astype(jnp.int32)
    mode = (band ^ second) * 28 + ((row - 224 * second) >> 3)
    pick_rows = ones_where(mode == iota((448, 112), 1))
    col = iota((64, 512), 1)
    member = (band ^ (col >> 7)) * 16 + ((col & 127) >> 3)
    pick_cols = ones_where(member == iota((64, 512), 0))
    same = (iota((448, 512), 0) & 7) == (iota((448, 512), 1) & 7)
    get.wait()
    rows = dot(pick_rows, ct[...].astype(BF), NT).astype(BF)
    full = jnp.where(same, dot(rows, pick_cols), 0.0).astype(BF)
    kron[...] = full[:, 256:]
    for g in range(0, 1024, 256):
        cut = slice(g, g + 256)
        out[:, cut] = increment_of(scale, full[:, :256], ma, mb, ea, eb, cut)


def increment_other(scale, kron, before, ma, mb, ea, eb, out):
    for g in range(0, 1024, 256):
        cut = slice(g, g + 256)
        out[:, cut] = before[:, cut] + increment_of(scale, kron[...], ma, mb, ea, eb, cut)


def prep_body(columns_t, owners_in, interpolation, got_in, innovation, obs_weight, _,
              onehot, onehot_t, place_hi, place_lo, interp, innov, weight, innov_own, live_own,
              cols_s, own_s, got, sem):
    band = lax.axis_index("band")
    tile = lax.axis_index("mem")
    quarter = pl.ds(pl.multiple_of(band * 128, 128), 128)
    small = [(columns_t, cols_s), (owners_in, own_s), (got_in, got)]
    mid = [(innovation.at[0, :, quarter], innov_own), (obs_weight.at[0, :, quarter], live_own)]
    big = [(interpolation.at[:32, :, quarter_at(side)], interp.at[:, :, side * 128:(side + 1) * 128]) for side in range(2)]
    copies = start_all([pltpu.make_async_copy(a, b, sem.at[n]) for n, (a, b) in enumerate(small + mid + big)])
    wait_all(copies[:3])
    t = iota((64, 1024), 1)
    cols = cols_s[...].astype(F32).T.astype(jnp.int32)
    for c in range(16):
        onehot[c * 64:(c + 1) * 64, :] = ones_where(cols[:, c:c + 1] == t)
    flat = jnp.concatenate([cols_s[c:c + 1, :] for c in range(16)], axis=1)
    for r in range(0, 1024, 128):
        onehot_t[r:r + 128, :] = ones_where(flat == iota((128, 1024), 0) + r)
    pair = own_s[pl.ds(tile >> 1, 1), :].astype(F32)
    own = jnp.where((tile & 1) == 1, pair[:, 64:], pair[:, :64])
    own_row = jnp.broadcast_to(own, (64, 64))
    own_col = own_row.T
    earlier = iota((64, 64), 1) < iota((64, 64), 0)
    rank = jnp.sum(jnp.where((own_row == own_col) & earlier, 1.0, 0.0), axis=1, keepdims=True)
    target = (own_col[:, :1] * 8.0 + rank).astype(jnp.int32)
    sel = ones_where(target == iota((64, 256), 1))
    slot = iota((64, 256), 1)
    half = 4 * (band >> 1)
    place_hi[...] = ones_where((target == slot + half) & ((slot & 7) < 4))
    place_lo[...] = ones_where((target == slot + half - 4) & ((slot & 7) >= 4))
    x = got[...].astype(F32)
    innov[...] = dot(sel, x[:, :8].reshape(256, 256).astype(BF))
    weight[...] = dot(sel, x[:, 8:].reshape(256, 256).astype(BF))
    hit = ones_where(own_s[...] == tile)
    pair = ones_where((iota((256, 16), 0) >> 4) == iota((256, 16), 1))
    odd = (iota((256, 128), 0) >> 3) & 1
    side = jnp.where((iota((256, 128), 1) >> 6) == odd, dot(pair, hit), 0.0)
    count = jnp.sum(side, axis=1, keepdims=True)
    live = jnp.where((iota((256, 1), 0) & 7).astype(F32) < count, 1.0, 0.0)
    wait_all(copies[3:5])
    live_own[...] = live * live_own[...]
    wait_all(copies[5:])


def pass_body(*refs):
    del refs


def obs_body(p0, p1, p2, p3, onehot, onehot_t, innov, weight, near, interpolation,
             adj_all, image_out, picked, depb, spread, far, sem):
    fetch = [
        start_all([
            pltpu.make_async_copy(
                interpolation.at[32 + j:40 + j, :, quarter_at(side)],
                far.at[j:j + 8, :, side * 128:(side + 1) * 128], sem.at[j // 4 + side])
            for side in range(2)
        ]) for j in range(0, 32, 8)
    ]

    def block(j):
        return near[j] if j < 32 else far[j - 32]

    band = lax.axis_index("band")
    first = (band & 1) == 0
    mine = p0[...] + p2[...]
    mate = p1[...] + p3[...]
    inc = jnp.concatenate([jnp.where(first, mine, mate), jnp.where(first, mate, mine)], axis=0).astype(BF)
    r0 = iota((256, 256), 0)
    r1 = iota((256, 256), 1)
    swap = ones_where(((r0 & 15) * 16 + (r0 >> 4)) == r1)
    picks = dot(inc, onehot_t[...])
    by_col = jnp.concatenate([picks[:, c * 64:(c + 1) * 64] for c in range(16)], axis=0).astype(BF)
    picked[...] = dot(by_col, swap, TN).astype(BF)
    rows = iota((16, 256), 0)
    image = []
    for b in range(4):
        lhs = picked[b * 16:(b + 1) * 16, :]
        acc = jnp.zeros((16, 256), F32)
        for i in range(16):
            j = b * 16 + i
            if j >= 32 and j % 8 == 0:
                wait_all(fetch[(j - 32) // 8])
            acc = jnp.where(rows == i, dot(lhs, block(j)), acc)
        image.append(acc)
    image = jnp.concatenate(image, axis=0)
    image_out[...] = image
    depb[...] = (weight[...] * (innov[...] - image)).astype(BF)
    for b in range(4):
        lhs = depb[b * 16:(b + 1) * 16, :]
        acc = jnp.zeros((16, 256), F32)
        for i in range(16):
            acc = jnp.where(rows == i, dot(lhs, block(b * 16 + i), NT), acc)
        spread[b * 16:(b + 1) * 16, :] = acc
    x = spread[...]
    hi = x.astype(BF)
    lo = (x - hi.astype(F32)).astype(BF)
    terms = []
    for part in (hi, lo):
        turned = dot(swap, part, NT)
        terms.append(jnp.concatenate([turned[c * 16:(c + 1) * 16] for c in range(16)], axis=1))
    both = dot(jnp.concatenate(terms, axis=0).astype(BF), onehot[...])
    adj = both[:16] + both[16:]
    adj_all[:8] = jnp.where(first, adj[8:], adj[:8])
    adj_all[8:] = jnp.where(first, adj[:8], adj[8:])


def slots_body(place_hi, place_lo, image, out):
    hi, lo, _ = parts3(image[...])
    out[...] = dot(place_hi[...], hi, TN) + dot(place_lo[...], lo, TN)


def gradient_body(adj, came, m_my, m_mt, o_my, o_mt, e_my, e_mt, f_my, f_mt, out):
    first = (lax.axis_index("band") & 1) == 0
    same = (iota((448, 256), 0) & 7) == (iota((448, 256), 1) & 7)
    sel = ones_where((iota((32, 256), 1) >> 3) == iota((32, 256), 0))
    total = None
    for here, there, members, eigs in (
            (adj[8:], came[:8], (m_my, o_my), (e_my, f_my)), (adj[:8], came[8:], (m_mt, o_mt), (e_mt, f_mt))):
        wide = jnp.broadcast_to((here + there)[None], (16, 8, 1024)).reshape(128, 1024)
        weighted = jnp.concatenate([(m[...].astype(F32) * wide).astype(BF) for m in members], axis=0)
        term = dot(jnp.concatenate([e[...] for e in eigs], axis=0), weighted, NT)
        total = term if total is None else total + term
    own = jnp.sum(jnp.where(same, total, 0.0).reshape(56, 8, 256), axis=1)
    own = jnp.where(first, own, jnp.concatenate([own[28:], own[:28]], axis=0))
    hi, mid, _ = parts3(own)
    out[...] = dot(sel, hi, NT) + dot(sel, mid, NT)


def pack_body(mine, slots, out):
    total = mine[...]
    gap = jnp.zeros((8, 8), F32)
    flat = [
        jnp.concatenate([total[r:r + 8], gap, total[r + 8:r + 16], gap], axis=1) for r in (0, 16)
    ]
    high = (lax.axis_index("band") >> 1) == 1
    for side in range(2):
        here = high if side else jnp.logical_not(high)
        term = jnp.broadcast_to(jnp.where(here, flat[0], flat[1])[None], (32, 8, 128))
        image = slots[:, side * 128:(side + 1) * 128].reshape(32, 8, 128)
        out[side * 32:(side + 1) * 32] = jnp.concatenate([term, image], axis=1).astype(BF)


def final_body(scale, got, control_t, innov, live, gradient_t, departures):
    band = lax.axis_index("band")
    sums, halves = [], []
    for side in range(2):
        x = got[side * 32:(side + 1) * 32].astype(F32)
        sums.append(jnp.sum(x[:, :8], axis=0))
        halves.append(x[:, 8:12] + x[:, 12:])
    image = jnp.concatenate(halves, axis=1).reshape(256, 128)
    departures[...] = (live[...] * (innov[...] - image)).reshape(1, 256, 128)
    low, top = sums
    total = jnp.concatenate([
        jnp.concatenate([low[:, :56], top[:, :56]], axis=1),
        jnp.concatenate([low[:, 64:120], top[:, 64:120]], axis=1),
    ], axis=0)
    own = ones_where(iota((16, 64), 1) == band * 16 + iota((16, 64), 0))
    hi, mid, lo = parts3(control_t[...])
    gradient_t[...] = dot(own, hi) + dot(own, mid) + dot(own, lo) - scale * total


def per_device(members, eigvecs, control, columns, interpolation, owners, innovation, obs_weight):
    scale = 1.0 / math.sqrt(112 * 64)
    owners = owners.reshape(16, 128)

    def over(x, bit):
        return lax.ppermute(x, "band", [(i, i ^ bit) for i in range(4)])

    dma = pltpu.SemaphoreType.DMA
    m_my, m_mt, e_my, e_mt, iv = call(
        split_body, [HB] * 4,
        [(pltpu.VMEM((16, 8, 1024), BF), VM)] * 2 + [(pltpu.VMEM((28, 8, 1024), BF), VM)] * 2
        + [(pltpu.VMEM((2, 256, 256), F32), VM)], 0, 0, [dma((8,))],
    )(in_hbm(members), in_hbm(eigvecs), in_hbm(innovation), in_hbm(obs_weight))
    m_my, m_mt, e0, e_mt = [in_vmem(a.reshape(-1, 1024)) for a in (m_my, m_mt, e_my, e_mt)]
    m3 = over(m_mt, 3)
    m2 = over(m_my, 2)
    m1 = over(m_mt, 1)
    (payload,) = call(
        load_body, [VM, ANY], [(pltpu.VMEM((32, 16, 256), BF), VM)], 0, 0,
    )(in_vmem(iv), m_my)
    got = lax.all_to_all(payload, "mem", split_axis=0, concat_axis=0, tiled=True)
    e1 = over(e_mt, 1)
    m1, m2, m3, e1 = [in_vmem(a) for a in (m1, m2, m3, e1)]

    part, kron = call(
        lambda *refs: increment_own(scale, *refs), [HB] + [VM] * 4,
        [(pltpu.VMEM((8, 1024), F32), VM), (pltpu.VMEM((448, 256), BF), VM)],
        25 * 10 ** 7, 2 * 10 ** 6, [pltpu.VMEM((64, 112), F32), dma(())],
    )(in_hbm(control.T), m_my, m1, e0, e1)
    (part,) = call(
        lambda *refs: increment_other(scale, *refs), [VM] * 6, [(shape((8, 1024), F32), VM)],
        25 * 10 ** 7, 2 * 10 ** 6,
    )(in_vmem(kron), in_vmem(part), m2, m3, e0, e1)

    kept = call(
        prep_body,
        [HB] * 3 + [ANY] + [HB] * 2 + [ANY],
        [(pltpu.VMEM(d, t), VM) for d, t in (
            ((1024, 1024), BF), ((1024, 1024), BF), ((64, 256), BF), ((64, 256), BF), ((32, 256, 256), BF), ((64, 256), F32), ((64, 256), F32),
            ((256, 128), F32), ((256, 128), F32))],
        10 ** 8, 12 * 10 ** 6,
        [pltpu.VMEM((16, 64), jnp.int32), pltpu.VMEM((16, 128), jnp.int32), pltpu.VMEM((32, 16, 256), BF), dma((7,))],
    )(in_hbm(columns.T), in_hbm(owners), in_hbm(interpolation), got, in_hbm(innovation), in_hbm(obs_weight), part)
    onehot, onehot_t, place_hi, place_lo, interp, innov, weight, innov_own, live_own = [in_vmem(a) for a in kept]

    p3 = over(part, 3)
    p2 = over(part, 2)
    p1 = over(part, 1)
    (m3,) = call(
        pass_body, [ANY] * 4 + [VM], [(pltpu.VMEM((128, 1024), BF), VM)], 0, 0, aliases={4: 0}
    )(p1, p2, p3, place_hi, m3)
    adj, image = call(
        obs_body, [VM] * 9 + [HB],
        [(shape((16, 1024), F32), VM), (pltpu.VMEM((64, 256), F32), VM)],
        10 ** 9, 12 * 10 ** 6,
        [pltpu.VMEM((64, 256), BF), pltpu.VMEM((64, 256), BF), pltpu.VMEM((64, 256), F32),
         pltpu.VMEM((32, 256, 256), BF), dma((8,))],
    )(part, p1, p2, p3, onehot, onehot_t, innov, weight, interp, in_hbm(interpolation))

    (slots,) = call(
        slots_body, [VM] * 3, [(pltpu.VMEM((256, 256), F32), VM)], 10 ** 7, 5 * 10 ** 5
    )(place_hi, place_lo, in_vmem(image))
    f_mt = over(e0, 1)
    o_mt = over(in_vmem(m3), 1)
    (terms,) = call(
        gradient_body, [VM] * 10, [(shape((32, 56), F32), VM)], 5 * 10 ** 8, 2 * 10 ** 6
    )(adj, over(adj, 1), m_my, m_mt, m2, o_mt, e0, e_mt, e1, f_mt)

    (sent,) = call(
        pack_body, [VM] * 2, [(shape((64, 16, 128), BF), VM)], 10 ** 5, 6 * 10 ** 5
    )(terms, in_vmem(slots))
    groups = [[(2 * z + core) * 32 + t for z in range(2) for t in range(32)] for core in range(2)]
    arrived = lax.all_to_all(
        sent, ("band", "mem"), split_axis=0, concat_axis=0, axis_index_groups=groups, tiled=True)
    gradient_t, departures = call(
        lambda *refs: final_body(scale, *refs), [VM] * 4,
        [(shape((16, 112), F32), VM), (shape((1, 256, 128), F32), VM)], 10 ** 6, 6 * 10 ** 5,
    )(arrived, control.T, innov_own, live_own)
    return (gradient_t.T, departures)


def solution(mesh):
    return jax.shard_map(
        per_device,
        mesh=mesh,
        in_specs=(
            P("band", None, "mem"),
            P("band", None, "mem"),
            P(),
            P("mem", None),
            P("mem", None, None),
            P(),
            P("mem", None, None),
            P("mem", None, None),
        ),
        out_specs=(P(None, "band"), P("mem", None, "band")),
        check_vma=False,
    )
```

```python
import math

import jax
import jax.numpy as jnp
from jax import lax
from jax.experimental import pallas as pl
from jax.experimental.pallas import tpu as pltpu
from jax.sharding import PartitionSpec as P

BF = jnp.bfloat16
F32 = jnp.float32
NN = (((1,), (0,)), ((), ()))
NT = (((1,), (1,)), ((), ()))
TN = (((0,), (0,)), ((), ()))
MIB = 1024 * 1024
VM = pl.BlockSpec(memory_space=pltpu.VMEM)
ANY = pl.BlockSpec(memory_space=pl.ANY)
HB = pl.BlockSpec(memory_space=pltpu.HBM)


def dot(a, b, dims=NN):
    return lax.dot_general(a, b, dims, preferred_element_type=F32)


def parts3(x):
    hi = x.astype(BF)
    rest = x - hi.astype(F32)
    mid = rest.astype(BF)
    lo = (rest - mid.astype(F32)).astype(BF)
    return hi, mid, lo


def iota(dims, dim):
    return lax.broadcasted_iota(jnp.int32, dims, dim)


def ones_where(cond):
    return cond.astype(F32).astype(BF)


def shape(dims, dtype):
    return jax.ShapeDtypeStruct(dims, dtype)


def in_hbm(x):
    return pltpu.with_memory_space_constraint(x, pltpu.HBM)


def in_vmem(x):
    return pltpu.with_memory_space_constraint(x, pltpu.VMEM)


def call(body, ins, outs, flops, nbytes, scratch=(), vmem=16, aliases=None):
    return pl.pallas_call(
        body,
        out_shape=tuple(o for o, _ in outs),
        in_specs=list(ins),
        out_specs=tuple(s for _, s in outs),
        scratch_shapes=list(scratch),
        input_output_aliases=aliases or {},
        compiler_params=pltpu.CompilerParams(vmem_limit_bytes=vmem * MIB),
        cost_estimate=pl.CostEstimate(flops=flops, bytes_accessed=nbytes, transcendentals=0),
    )


def start_all(copies):
    for c in copies:
        c.start()
    return copies


def wait_all(copies):
    for c in copies:
        c.wait()


def halves_copies(src, mine, mate, sem, at):
    core = lax.axis_index("band") & 1
    lo = pl.multiple_of(core * 8, 8)
    hi = pl.multiple_of(8 - core * 8, 8)
    return [
        pltpu.make_async_copy(src.at[:, pl.ds(hi, 8), :], mate, sem.at[at]),
        pltpu.make_async_copy(src.at[:, pl.ds(lo, 8), :], mine, sem.at[at + 1]),
    ]


def quarter_at(side):
    core = lax.axis_index("band") & 1
    return pl.ds(pl.multiple_of((core + 2 * side) * 128, 128), 128)


def split_body(mem, eig, m_mine, m_mate, e_mine, e_mate, sem):
    wait_all(start_all(halves_copies(mem, m_mine, m_mate, sem, 0) + halves_copies(eig, e_mine, e_mate, sem, 2)))


def load_body(innovation, obs_weight, _, payload, iv, sem):
    copies = start_all([
        pltpu.make_async_copy(
            a.at[0, :, quarter_at(side)], iv.at[n, :, side * 128:(side + 1) * 128], sem.at[2 * n + side])
        for n, a in enumerate((innovation, obs_weight)) for side in range(2)
    ])
    for n in range(2):
        wait_all(copies[2 * n:2 * n + 2])
        payload[:, n * 8:(n + 1) * 8, :] = iv[n].reshape(32, 8, 256).astype(BF)


def increment_of(scale, kron, ma, mb, ea, eb, cut):
    mixed = dot(kron, jnp.concatenate([ma[:, cut], mb[:, cut]], axis=0))
    total = jnp.sum((mixed[:224] * ea[:, cut].astype(F32)).reshape(28, 8, 256), axis=0)
    total = total + jnp.sum((mixed[224:] * eb[:, cut].astype(F32)).reshape(28, 8, 256), axis=0)
    return scale * total


def increment_own(scale, control_t, ma, mb, ea, eb, out, kron, ct, sem):
    get = pltpu.make_async_copy(control_t, ct, sem)
    get.start()
    band = lax.axis_index("band")
    row = iota((448, 112), 0)
    second = (row >= 224).astype(jnp.int32)
    mode = (band ^ second) * 28 + ((row - 224 * second) >> 3)
    pick_rows = ones_where(mode == iota((448, 112), 1))
    col = iota((64, 512), 1)
    member = (band ^ (col >> 7)) * 16 + ((col & 127) >> 3)
    pick_cols = ones_where(member == iota((64, 512), 0))
    same = (iota((448, 512), 0) & 7) == (iota((448, 512), 1) & 7)
    get.wait()
    rows = dot(pick_rows, ct[...].astype(BF), NT).astype(BF)
    full = jnp.where(same, dot(rows, pick_cols), 0.0).astype(BF)
    kron[...] = full[:, 256:]
    for g in range(0, 1024, 256):
        cut = slice(g, g + 256)
        out[:, cut] = increment_of(scale, full[:, :256], ma, mb, ea, eb, cut)


def increment_other(scale, kron, before, ma, mb, ea, eb, out):
    for g in range(0, 1024, 256):
        cut = slice(g, g + 256)
        out[:, cut] = before[:, cut] + increment_of(scale, kron[...], ma, mb, ea, eb, cut)


def prep_body(columns_t, owners_in, interpolation, got_in, innovation, obs_weight, _,
              onehot, onehot_t, place_hi, place_lo, interp, innov, weight, innov_own, live_own,
              cols_s, own_s, got, sem):
    band = lax.axis_index("band")
    tile = lax.axis_index("mem")
    quarter = pl.ds(pl.multiple_of(band * 128, 128), 128)
    small = [(columns_t, cols_s), (owners_in, own_s), (got_in, got)]
    mid = [(innovation.at[0, :, quarter], innov_own), (obs_weight.at[0, :, quarter], live_own)]
    big = [(interpolation.at[:32, :, quarter_at(side)], interp.at[:, :, side * 128:(side + 1) * 128]) for side in range(2)]
    copies = start_all([pltpu.make_async_copy(a, b, sem.at[n]) for n, (a, b) in enumerate(small + mid + big)])
    wait_all(copies[:3])
    t = iota((64, 1024), 1)
    cols = cols_s[...].astype(F32).T.astype(jnp.int32)
    for c in range(16):
        onehot[c * 64:(c + 1) * 64, :] = ones_where(cols[:, c:c + 1] == t)
    flat = jnp.concatenate([cols_s[c:c + 1, :] for c in range(16)], axis=1)
    for r in range(0, 1024, 128):
        onehot_t[r:r + 128, :] = ones_where(flat == iota((128, 1024), 0) + r)
    pair = own_s[pl.ds(tile >> 1, 1), :].astype(F32)
    own = jnp.where((tile & 1) == 1, pair[:, 64:], pair[:, :64])
    own_row = jnp.broadcast_to(own, (64, 64))
    own_col = own_row.T
    earlier = iota((64, 64), 1) < iota((64, 64), 0)
    rank = jnp.sum(jnp.where((own_row == own_col) & earlier, 1.0, 0.0), axis=1, keepdims=True)
    target = (own_col[:, :1] * 8.0 + rank).astype(jnp.int32)
    sel = ones_where(target == iota((64, 256), 1))
    slot = iota((64, 256), 1)
    half = 4 * (band >> 1)
    place_hi[...] = ones_where((target == slot + half) & ((slot & 7) < 4))
    place_lo[...] = ones_where((target == slot + half - 4) & ((slot & 7) >= 4))
    x = got[...].astype(F32)
    innov[...] = dot(sel, x[:, :8].reshape(256, 256).astype(BF))
    weight[...] = dot(sel, x[:, 8:].reshape(256, 256).astype(BF))
    hit = ones_where(own_s[...] == tile)
    pair = ones_where((iota((256, 16), 0) >> 4) == iota((256, 16), 1))
    odd = (iota((256, 128), 0) >> 3) & 1
    side = jnp.where((iota((256, 128), 1) >> 6) == odd, dot(pair, hit), 0.0)
    count = jnp.sum(side, axis=1, keepdims=True)
    live = jnp.where((iota((256, 1), 0) & 7).astype(F32) < count, 1.0, 0.0)
    wait_all(copies[3:5])
    live_own[...] = live * live_own[...]
    wait_all(copies[5:])


def add_body(a, b, _, out):
    out[...] = (a[...] + b[...]).astype(BF)


def pass_body(_, x, same_x):
    del x, same_x


def obs_body(inc_my, inc_mt, onehot, onehot_t, innov, weight, near, interpolation,
             adj_all, image_out, picked, depb, spread, far, sem):
    fetch = [
        start_all([
            pltpu.make_async_copy(
                interpolation.at[32 + j:40 + j, :, quarter_at(side)],
                far.at[j:j + 8, :, side * 128:(side + 1) * 128], sem.at[j // 4 + side])
            for side in range(2)
        ]) for j in range(0, 32, 8)
    ]

    def block(j):
        return near[j] if j < 32 else far[j - 32]

    band = lax.axis_index("band")
    first = (band & 1) == 0
    mine = inc_my[...].astype(F32)
    mate = inc_mt[...].astype(F32)
    inc = jnp.concatenate([jnp.where(first, mine, mate), jnp.where(first, mate, mine)], axis=0).astype(BF)
    r0 = iota((256, 256), 0)
    r1 = iota((256, 256), 1)
    swap = ones_where(((r0 & 15) * 16 + (r0 >> 4)) == r1)
    picks = dot(inc, onehot_t[...])
    by_col = jnp.concatenate([picks[:, c * 64:(c + 1) * 64] for c in range(16)], axis=0).astype(BF)
    picked[...] = dot(by_col, swap, TN).astype(BF)
    rows = iota((16, 256), 0)
    image = []
    for b in range(4):
        lhs = picked[b * 16:(b + 1) * 16, :]
        acc = jnp.zeros((16, 256), F32)
        for i in range(16):
            j = b * 16 + i
            if j >= 32 and j % 8 == 0:
                wait_all(fetch[(j - 32) // 8])
            acc = jnp.where(rows == i, dot(lhs, block(j)), acc)
        image.append(acc)
    image = jnp.concatenate(image, axis=0)
    image_out[...] = image
    dep = weight[...] * (innov[...] - image)
    depb[...] = dep.astype(BF)
    dep_t = dep.T.astype(BF)
    column = iota((256, 64), 1)
    odd = jnp.zeros((256, 64), F32)
    for b in range(4):
        lhs = depb[b * 16:(b + 1) * 16, :]
        acc = jnp.zeros((16, 256), F32)
        for i in range(16):
            j = b * 16 + i
            if j % 2:
                odd = jnp.where(column == j, dot(block(j), dep_t), odd)
            else:
                acc = jnp.where(rows == i, dot(lhs, block(j), NT), acc)
        spread[b * 16:(b + 1) * 16, :] = acc
    x = spread[...]
    hi, lo, _ = parts3(x)
    odd_hi, odd_lo, _ = parts3(odd)
    terms = []
    for part, odd_part in ((hi, odd_hi), (lo, odd_lo)):
        turned = dot(swap, part, NT) + dot(swap, odd_part)
        terms.append(jnp.concatenate([turned[c * 16:(c + 1) * 16] for c in range(16)], axis=1))
    both = dot(jnp.concatenate(terms, axis=0).astype(BF), onehot[...])
    adj = both[:16] + both[16:]
    adj_all[:8] = jnp.where(first, adj[8:], adj[:8])
    adj_all[8:] = jnp.where(first, adj[:8], adj[8:])


def slots_body(place_hi, place_lo, image, out):
    hi, lo, _ = parts3(image[...])
    out[...] = dot(place_hi[...], hi, TN) + dot(place_lo[...], lo, TN)


def gradient_body(adj, came, m_my, m_mt, o_my, o_mt, e_my, e_mt, f_my, f_mt, out):
    first = (lax.axis_index("band") & 1) == 0
    same = (iota((448, 256), 0) & 7) == (iota((448, 256), 1) & 7)
    sel = ones_where((iota((32, 256), 1) >> 3) == iota((32, 256), 0))
    total = None
    for here, there, members, eigs in (
            (adj[8:], came[:8], (m_my, o_my), (e_my, f_my)), (adj[:8], came[8:], (m_mt, o_mt), (e_mt, f_mt))):
        wide = jnp.broadcast_to((here + there)[None], (16, 8, 1024)).reshape(128, 1024)
        weighted = jnp.concatenate([(m[...].astype(F32) * wide).astype(BF) for m in members], axis=0)
        term = dot(jnp.concatenate([e[...] for e in eigs], axis=0), weighted, NT)
        total = term if total is None else total + term
    own = jnp.sum(jnp.where(same, total, 0.0).reshape(56, 8, 256), axis=1)
    own = jnp.where(first, own, jnp.concatenate([own[28:], own[:28]], axis=0))
    hi, mid, _ = parts3(own)
    out[...] = dot(sel, hi, NT) + dot(sel, mid, NT)


def pack_body(mine, slots, out):
    total = mine[...]
    gap = jnp.zeros((8, 8), F32)
    flat = [
        jnp.concatenate([total[r:r + 8], gap, total[r + 8:r + 16], gap], axis=1) for r in (0, 16)
    ]
    high = (lax.axis_index("band") >> 1) == 1
    for side in range(2):
        here = high if side else jnp.logical_not(high)
        term = jnp.broadcast_to(jnp.where(here, flat[0], flat[1])[None], (32, 8, 128))
        image = slots[:, side * 128:(side + 1) * 128].reshape(32, 8, 128)
        out[side * 32:(side + 1) * 32] = jnp.concatenate([term, image], axis=1).astype(BF)


def final_body(scale, got, control_t, innov, live, gradient_t, departures):
    band = lax.axis_index("band")
    sums, halves = [], []
    for side in range(2):
        x = got[side * 32:(side + 1) * 32].astype(F32)
        sums.append(jnp.sum(x[:, :8], axis=0))
        halves.append(x[:, 8:12] + x[:, 12:])
    image = jnp.concatenate(halves, axis=1).reshape(256, 128)
    departures[...] = (live[...] * (innov[...] - image)).reshape(1, 256, 128)
    low, top = sums
    total = jnp.concatenate([
        jnp.concatenate([low[:, :56], top[:, :56]], axis=1),
        jnp.concatenate([low[:, 64:120], top[:, 64:120]], axis=1),
    ], axis=0)
    own = ones_where(iota((16, 64), 1) == band * 16 + iota((16, 64), 0))
    hi, mid, lo = parts3(control_t[...])
    gradient_t[...] = dot(own, hi) + dot(own, mid) + dot(own, lo) - scale * total


def per_device(members, eigvecs, control, columns, interpolation, owners, innovation, obs_weight):
    scale = 1.0 / math.sqrt(112 * 64)
    owners = owners.reshape(16, 128)

    def over(x, bit):
        return lax.ppermute(x, "band", [(i, i ^ bit) for i in range(4)])

    dma = pltpu.SemaphoreType.DMA
    m_my, m_mt, e_my, e_mt = call(
        split_body, [HB] * 2,
        [(pltpu.VMEM((16, 8, 1024), BF), VM)] * 2 + [(pltpu.VMEM((28, 8, 1024), BF), VM)] * 2, 0, 0, [dma((4,))],
    )(in_hbm(members), in_hbm(eigvecs))
    m_my, m_mt, e0, e_mt = [in_vmem(a.reshape(-1, 1024)) for a in (m_my, m_mt, e_my, e_mt)]
    m3 = over(m_mt, 3)
    m2 = over(m_my, 2)
    m1 = over(m_mt, 1)
    (payload,) = call(
        load_body, [HB] * 2 + [ANY], [(pltpu.HBM((32, 16, 256), BF), VM)],
        0, 0, [pltpu.VMEM((2, 256, 256), F32), dma((4,))],
    )(in_hbm(innovation), in_hbm(obs_weight), m_my)
    got = lax.all_to_all(payload, "mem", split_axis=0, concat_axis=0, tiled=True)
    e1 = over(e_mt, 1)
    m1, m2, m3, e1 = [in_vmem(a) for a in (m1, m2, m3, e1)]

    part, kron = call(
        lambda *refs: increment_own(scale, *refs), [HB] + [VM] * 4,
        [(pltpu.VMEM((8, 1024), F32), VM), (pltpu.VMEM((448, 256), BF), VM)],
        25 * 10 ** 7, 2 * 10 ** 6, [pltpu.VMEM((64, 112), F32), dma(())],
    )(in_hbm(control.T), m_my, m1, e0, e1)
    (part,) = call(
        lambda *refs: increment_other(scale, *refs), [VM] * 6, [(shape((8, 1024), F32), VM)],
        25 * 10 ** 7, 2 * 10 ** 6,
    )(in_vmem(kron), in_vmem(part), m2, m3, e0, e1)

    kept = call(
        prep_body,
        [HB] * 3 + [ANY] + [HB] * 2 + [ANY],
        [(pltpu.VMEM(d, t), VM) for d, t in (
            ((1024, 1024), BF), ((1024, 1024), BF), ((64, 256), BF), ((64, 256), BF), ((32, 256, 256), BF), ((64, 256), F32), ((64, 256), F32),
            ((256, 128), F32), ((256, 128), F32))],
        10 ** 8, 12 * 10 ** 6,
        [pltpu.VMEM((16, 64), jnp.int32), pltpu.VMEM((16, 128), jnp.int32), pltpu.VMEM((32, 16, 256), BF), dma((7,))],
    )(in_hbm(columns.T), in_hbm(owners), in_hbm(interpolation), got, in_hbm(innovation), in_hbm(obs_weight), part)
    onehot, onehot_t, place_hi, place_lo, interp, innov, weight, innov_own, live_own = [in_vmem(a) for a in kept]

    (inc_my,) = call(
        add_body, [VM, VM, ANY], [(shape((8, 1024), BF), VM)], 10 ** 4, 10 ** 5,
    )(part, over(part, 2), place_hi)
    inc_mt = over(inc_my, 1)
    (m3,) = call(
        pass_body, [ANY, VM], [(pltpu.VMEM((128, 1024), BF), VM)], 0, 0, aliases={1: 0}
    )(inc_mt, m3)
    adj, image = call(
        obs_body, [VM] * 7 + [HB],
        [(shape((16, 1024), F32), VM), (pltpu.VMEM((64, 256), F32), VM)],
        10 ** 9, 12 * 10 ** 6,
        [pltpu.VMEM((64, 256), BF), pltpu.VMEM((64, 256), BF), pltpu.VMEM((64, 256), F32),
         pltpu.VMEM((32, 256, 256), BF), dma((8,))],
    )(inc_my, inc_mt, onehot, onehot_t, innov, weight, interp, in_hbm(interpolation))

    (slots,) = call(
        slots_body, [VM] * 3, [(pltpu.VMEM((256, 256), F32), VM)], 10 ** 7, 5 * 10 ** 5
    )(place_hi, place_lo, in_vmem(image))
    f_mt = over(e0, 1)
    o_mt = over(in_vmem(m3), 1)
    (terms,) = call(
        gradient_body, [VM] * 10, [(shape((32, 56), F32), VM)], 5 * 10 ** 8, 2 * 10 ** 6
    )(adj, over(adj, 1), m_my, m_mt, m2, o_mt, e0, e_mt, e1, f_mt)

    (sent,) = call(
        pack_body, [VM] * 2, [(shape((64, 16, 128), BF), VM)], 10 ** 5, 6 * 10 ** 5
    )(terms, in_vmem(slots))
    groups = [[(2 * z + core) * 32 + t for z in range(2) for t in range(32)] for core in range(2)]
    arrived = lax.all_to_all(
        sent, ("band", "mem"), split_axis=0, concat_axis=0, axis_index_groups=groups, tiled=True)
    gradient_t, departures = call(
        lambda *refs: final_body(scale, *refs), [VM] * 4,
        [(shape((16, 112), F32), VM), (shape((1, 256, 128), F32), VM)], 10 ** 6, 6 * 10 ** 5,
    )(arrived, control.T, innov_own, live_own)
    return (gradient_t.T, departures)


def solution(mesh):
    return jax.shard_map(
        per_device,
        mesh=mesh,
        in_specs=(
            P("band", None, "mem"),
            P("band", None, "mem"),
            P(),
            P("mem", None),
            P("mem", None, None),
            P(),
            P("mem", None, None),
            P("mem", None, None),
        ),
        out_specs=(P(None, "band"), P("mem", None, "band")),
        check_vma=False,
    )
```

```python
import math

import jax
import jax.numpy as jnp
from jax import lax
from jax.experimental import pallas as pl
from jax.experimental.pallas import tpu as pltpu
from jax.sharding import PartitionSpec as P

BF = jnp.bfloat16
F32 = jnp.float32
NN = (((1,), (0,)), ((), ()))
NT = (((1,), (1,)), ((), ()))
TN = (((0,), (0,)), ((), ()))
MIB = 1024 * 1024
VM = pl.BlockSpec(memory_space=pltpu.VMEM)
ANY = pl.BlockSpec(memory_space=pl.ANY)
HB = pl.BlockSpec(memory_space=pltpu.HBM)


def dot(a, b, dims=NN):
    return lax.dot_general(a, b, dims, preferred_element_type=F32)


def parts3(x):
    hi = x.astype(BF)
    rest = x - hi.astype(F32)
    mid = rest.astype(BF)
    lo = (rest - mid.astype(F32)).astype(BF)
    return hi, mid, lo


def iota(dims, dim):
    return lax.broadcasted_iota(jnp.int32, dims, dim)


def ones_where(cond):
    return cond.astype(F32).astype(BF)


def shape(dims, dtype):
    return jax.ShapeDtypeStruct(dims, dtype)


def in_hbm(x):
    return pltpu.with_memory_space_constraint(x, pltpu.HBM)


def in_vmem(x):
    return pltpu.with_memory_space_constraint(x, pltpu.VMEM)


def call(body, ins, outs, flops, nbytes, scratch=(), vmem=16, aliases=None):
    return pl.pallas_call(
        body,
        out_shape=tuple(o for o, _ in outs),
        in_specs=list(ins),
        out_specs=tuple(s for _, s in outs),
        scratch_shapes=list(scratch),
        input_output_aliases=aliases or {},
        compiler_params=pltpu.CompilerParams(vmem_limit_bytes=vmem * MIB),
        cost_estimate=pl.CostEstimate(flops=flops, bytes_accessed=nbytes, transcendentals=0),
    )


def start_all(copies):
    for c in copies:
        c.start()
    return copies


def wait_all(copies):
    for c in copies:
        c.wait()


def halves_copies(src, mine, mate, sem, at):
    core = lax.axis_index("band") & 1
    lo = pl.multiple_of(core * 8, 8)
    hi = pl.multiple_of(8 - core * 8, 8)
    return [
        pltpu.make_async_copy(src.at[:, pl.ds(hi, 8), :], mate, sem.at[at]),
        pltpu.make_async_copy(src.at[:, pl.ds(lo, 8), :], mine, sem.at[at + 1]),
    ]


def quarter_at(side):
    core = lax.axis_index("band") & 1
    return pl.ds(pl.multiple_of((core + 2 * side) * 128, 128), 128)


def split_body(mem, eig, m_mine, m_mate, e_mine, e_mate, sem):
    wait_all(start_all(halves_copies(mem, m_mine, m_mate, sem, 0) + halves_copies(eig, e_mine, e_mate, sem, 2)))


def load_body(innovation, obs_weight, _, payload, iv, sem):
    copies = start_all([
        pltpu.make_async_copy(
            a.at[0, :, quarter_at(side)], iv.at[n, :, side * 128:(side + 1) * 128], sem.at[2 * n + side])
        for n, a in enumerate((innovation, obs_weight)) for side in range(2)
    ])
    for n in range(2):
        wait_all(copies[2 * n:2 * n + 2])
        payload[:, n * 8:(n + 1) * 8, :] = iv[n].reshape(32, 8, 256).astype(BF)


def increment_of(scale, kron, ma, mb, ea, eb, cut):
    mixed = dot(kron, jnp.concatenate([ma[:, cut], mb[:, cut]], axis=0))
    total = jnp.sum((mixed[:224] * ea[:, cut].astype(F32)).reshape(28, 8, 256), axis=0)
    total = total + jnp.sum((mixed[224:] * eb[:, cut].astype(F32)).reshape(28, 8, 256), axis=0)
    return scale * total


def increment_own(scale, control_t, columns_t, owners, ma, mb, ea, eb, out, kron, columns_out, owners_out, ct, sem):
    get, *small = start_all([
        pltpu.make_async_copy(a, b, sem.at[n])
        for n, (a, b) in enumerate(((control_t, ct), (columns_t, columns_out), (owners, owners_out)))
    ])
    band = lax.axis_index("band")
    row = iota((448, 112), 0)
    second = (row >= 224).astype(jnp.int32)
    mode = (band ^ second) * 28 + ((row - 224 * second) >> 3)
    pick_rows = ones_where(mode == iota((448, 112), 1))
    col = iota((64, 512), 1)
    member = (band ^ (col >> 7)) * 16 + ((col & 127) >> 3)
    pick_cols = ones_where(member == iota((64, 512), 0))
    same = (iota((448, 512), 0) & 7) == (iota((448, 512), 1) & 7)
    get.wait()
    rows = dot(pick_rows, ct[...].astype(BF), NT).astype(BF)
    full = jnp.where(same, dot(rows, pick_cols), 0.0).astype(BF)
    kron[...] = full[:, 256:]
    for g in range(0, 1024, 256):
        cut = slice(g, g + 256)
        out[:, cut] = increment_of(scale, full[:, :256], ma, mb, ea, eb, cut)
    wait_all(small)


def increment_other(scale, kron, before, ma, mb, ea, eb, out):
    for g in range(0, 1024, 256):
        cut = slice(g, g + 256)
        out[:, cut] = before[:, cut] + increment_of(scale, kron[...], ma, mb, ea, eb, cut)


def prep_body(cols_s, own_s, interpolation, got, innovation, obs_weight, _,
              onehot, onehot_t, place_hi, place_lo, interp, innov, weight, innov_own, live_own, sem):
    band = lax.axis_index("band")
    tile = lax.axis_index("mem")
    quarter = pl.ds(pl.multiple_of(band * 128, 128), 128)
    mid = [(innovation.at[0, :, quarter], innov_own), (obs_weight.at[0, :, quarter], live_own)]
    big = [(interpolation.at[:32, :, quarter_at(side)], interp.at[:, :, side * 128:(side + 1) * 128]) for side in range(2)]
    copies = start_all([pltpu.make_async_copy(a, b, sem.at[n]) for n, (a, b) in enumerate(mid + big)])
    t = iota((64, 1024), 1)
    cols = cols_s[...].astype(F32).T.astype(jnp.int32)
    for c in range(16):
        onehot[c * 64:(c + 1) * 64, :] = ones_where(cols[:, c:c + 1] == t)
    flat = jnp.concatenate([cols_s[c:c + 1, :] for c in range(16)], axis=1)
    for r in range(0, 1024, 128):
        onehot_t[r:r + 128, :] = ones_where(flat == iota((128, 1024), 0) + r)
    pair = own_s[pl.ds(tile >> 1, 1), :].astype(F32)
    own = jnp.where((tile & 1) == 1, pair[:, 64:], pair[:, :64])
    own_row = jnp.broadcast_to(own, (64, 64))
    own_col = own_row.T
    earlier = iota((64, 64), 1) < iota((64, 64), 0)
    rank = jnp.sum(jnp.where((own_row == own_col) & earlier, 1.0, 0.0), axis=1, keepdims=True)
    target = (own_col[:, :1] * 8.0 + rank).astype(jnp.int32)
    sel = ones_where(target == iota((64, 256), 1))
    slot = iota((64, 256), 1)
    half = 4 * (band >> 1)
    place_hi[...] = ones_where((target == slot + half) & ((slot & 7) < 4))
    place_lo[...] = ones_where((target == slot + half - 4) & ((slot & 7) >= 4))
    x = got[...].astype(F32)
    innov[...] = dot(sel, x[:, :8].reshape(256, 256).astype(BF))
    weight[...] = dot(sel, x[:, 8:].reshape(256, 256).astype(BF))
    hit = ones_where(own_s[...] == tile)
    pair = ones_where((iota((256, 16), 0) >> 4) == iota((256, 16), 1))
    odd = (iota((256, 128), 0) >> 3) & 1
    side = jnp.where((iota((256, 128), 1) >> 6) == odd, dot(pair, hit), 0.0)
    count = jnp.sum(side, axis=1, keepdims=True)
    live = jnp.where((iota((256, 1), 0) & 7).astype(F32) < count, 1.0, 0.0)
    wait_all(copies[:2])
    live_own[...] = live * live_own[...]
    wait_all(copies[2:])


def add_body(a, b, _, out):
    out[...] = (a[...] + b[...]).astype(BF)


def pass_body(_, x, same_x):
    del x, same_x


def obs_body(inc_my, inc_mt, onehot, onehot_t, innov, weight, near, interpolation,
             adj_all, image_out, picked, depb, spread, far, sem):
    fetch = [
        start_all([
            pltpu.make_async_copy(
                interpolation.at[32 + j:40 + j, :, quarter_at(side)],
                far.at[j:j + 8, :, side * 128:(side + 1) * 128], sem.at[j // 4 + side])
            for side in range(2)
        ]) for j in range(0, 32, 8)
    ]

    def block(j):
        return near[j] if j < 32 else far[j - 32]

    band = lax.axis_index("band")
    first = (band & 1) == 0
    mine = inc_my[...].astype(F32)
    mate = inc_mt[...].astype(F32)
    inc = jnp.concatenate([jnp.where(first, mine, mate), jnp.where(first, mate, mine)], axis=0).astype(BF)
    r0 = iota((256, 256), 0)
    r1 = iota((256, 256), 1)
    swap = ones_where(((r0 & 15) * 16 + (r0 >> 4)) == r1)
    picks = dot(inc, onehot_t[...])
    by_col = jnp.concatenate([picks[:, c * 64:(c + 1) * 64] for c in range(16)], axis=0).astype(BF)
    picked[...] = dot(by_col, swap, TN).astype(BF)
    rows = iota((16, 256), 0)
    image = []
    for b in range(4):
        lhs = picked[b * 16:(b + 1) * 16, :]
        acc = jnp.zeros((16, 256), F32)
        for i in range(16):
            j = b * 16 + i
            if j >= 32 and j % 8 == 0:
                wait_all(fetch[(j - 32) // 8])
            acc = jnp.where(rows == i, dot(lhs, block(j)), acc)
        image.append(acc)
    image = jnp.concatenate(image, axis=0)
    image_out[...] = image
    dep = weight[...] * (innov[...] - image)
    depb[...] = dep.astype(BF)
    dep_t = dep.T.astype(BF)
    column = iota((256, 64), 1)
    odd = jnp.zeros((256, 64), F32)
    for b in range(4):
        lhs = depb[b * 16:(b + 1) * 16, :]
        acc = jnp.zeros((16, 256), F32)
        for i in range(16):
            j = b * 16 + i
            if j % 2:
                odd = jnp.where(column == j, dot(block(j), dep_t), odd)
            else:
                acc = jnp.where(rows == i, dot(lhs, block(j), NT), acc)
        spread[b * 16:(b + 1) * 16, :] = acc
    x = spread[...]
    hi, lo, _ = parts3(x)
    odd_hi, odd_lo, _ = parts3(odd)
    terms = []
    for part, odd_part in ((hi, odd_hi), (lo, odd_lo)):
        turned = dot(swap, part, NT) + dot(swap, odd_part)
        terms.append(jnp.concatenate([turned[c * 16:(c + 1) * 16] for c in range(16)], axis=1))
    both = dot(jnp.concatenate(terms, axis=0).astype(BF), onehot[...])
    adj = both[:16] + both[16:]
    adj_all[:8] = jnp.where(first, adj[8:], adj[:8])
    adj_all[8:] = jnp.where(first, adj[:8], adj[8:])


def slots_body(place_hi, place_lo, image, out):
    hi, lo, _ = parts3(image[...])
    out[...] = dot(place_hi[...], hi, TN) + dot(place_lo[...], lo, TN)


def gradient_body(adj, came, m_my, m_mt, o_my, o_mt, e_my, e_mt, f_my, f_mt, out):
    first = (lax.axis_index("band") & 1) == 0
    same = (iota((448, 256), 0) & 7) == (iota((448, 256), 1) & 7)
    sel = ones_where((iota((32, 256), 1) >> 3) == iota((32, 256), 0))
    total = None
    for here, there, members, eigs in (
            (adj[8:], came[:8], (m_my, o_my), (e_my, f_my)), (adj[:8], came[8:], (m_mt, o_mt), (e_mt, f_mt))):
        wide = jnp.broadcast_to((here + there)[None], (16, 8, 1024)).reshape(128, 1024)
        weighted = jnp.concatenate([(m[...].astype(F32) * wide).astype(BF) for m in members], axis=0)
        term = dot(jnp.concatenate([e[...] for e in eigs], axis=0), weighted, NT)
        total = term if total is None else total + term
    own = jnp.sum(jnp.where(same, total, 0.0).reshape(56, 8, 256), axis=1)
    own = jnp.where(first, own, jnp.concatenate([own[28:], own[:28]], axis=0))
    hi, mid, _ = parts3(own)
    out[...] = dot(sel, hi, NT) + dot(sel, mid, NT)


def pack_body(mine, slots, out):
    total = mine[...]
    gap = jnp.zeros((8, 8), F32)
    flat = [
        jnp.concatenate([total[r:r + 8], gap, total[r + 8:r + 16], gap], axis=1) for r in (0, 16)
    ]
    high = (lax.axis_index("band") >> 1) == 1
    for side in range(2):
        here = high if side else jnp.logical_not(high)
        term = jnp.broadcast_to(jnp.where(here, flat[0], flat[1])[None], (32, 8, 128))
        image = slots[:, side * 128:(side + 1) * 128].reshape(32, 8, 128)
        out[side * 32:(side + 1) * 32] = jnp.concatenate([term, image], axis=1).astype(BF)


def final_body(scale, got, control_t, innov, live, gradient_t, departures):
    band = lax.axis_index("band")
    sums, halves = [], []
    for side in range(2):
        x = got[side * 32:(side + 1) * 32].astype(F32)
        sums.append(jnp.sum(x[:, :8], axis=0))
        halves.append(x[:, 8:12] + x[:, 12:])
    image = jnp.concatenate(halves, axis=1).reshape(256, 128)
    departures[...] = (live[...] * (innov[...] - image)).reshape(1, 256, 128)
    low, top = sums
    total = jnp.concatenate([
        jnp.concatenate([low[:, :56], top[:, :56]], axis=1),
        jnp.concatenate([low[:, 64:120], top[:, 64:120]], axis=1),
    ], axis=0)
    own = ones_where(iota((16, 64), 1) == band * 16 + iota((16, 64), 0))
    hi, mid, lo = parts3(control_t[...])
    gradient_t[...] = dot(own, hi) + dot(own, mid) + dot(own, lo) - scale * total


def per_device(members, eigvecs, control, columns, interpolation, owners, innovation, obs_weight):
    scale = 1.0 / math.sqrt(112 * 64)
    owners = owners.reshape(16, 128)

    def over(x, bit):
        return lax.ppermute(x, "band", [(i, i ^ bit) for i in range(4)])

    dma = pltpu.SemaphoreType.DMA
    m_my, m_mt, e_my, e_mt = call(
        split_body, [HB] * 2,
        [(pltpu.VMEM((16, 8, 1024), BF), VM)] * 2 + [(pltpu.VMEM((28, 8, 1024), BF), VM)] * 2, 0, 0, [dma((4,))],
    )(in_hbm(members), in_hbm(eigvecs))
    m_my, m_mt, e0, e_mt = [in_vmem(a.reshape(-1, 1024)) for a in (m_my, m_mt, e_my, e_mt)]
    m3 = over(m_mt, 3)
    m2 = over(m_my, 2)
    m1 = over(m_mt, 1)
    (payload,) = call(
        load_body, [HB] * 2 + [ANY], [(pltpu.HBM((32, 16, 256), BF), VM)],
        0, 0, [pltpu.VMEM((2, 256, 256), F32), dma((4,))],
    )(in_hbm(innovation), in_hbm(obs_weight), m_my)
    got = lax.all_to_all(payload, "mem", split_axis=0, concat_axis=0, tiled=True)
    e1 = over(e_mt, 1)
    m1, m2, m3, e1 = [in_vmem(a) for a in (m1, m2, m3, e1)]

    part, kron, columns_v, owners_v = call(
        lambda *refs: increment_own(scale, *refs), [HB] * 3 + [VM] * 4,
        [(pltpu.VMEM((8, 1024), F32), VM), (pltpu.VMEM((448, 256), BF), VM),
         (pltpu.VMEM((16, 64), jnp.int32), VM), (pltpu.VMEM((16, 128), jnp.int32), VM)],
        25 * 10 ** 7, 2 * 10 ** 6, [pltpu.VMEM((64, 112), F32), dma((3,))],
    )(in_hbm(control.T), in_hbm(columns.T), in_hbm(owners), m_my, m1, e0, e1)
    (part,) = call(
        lambda *refs: increment_other(scale, *refs), [VM] * 6, [(shape((8, 1024), F32), VM)],
        25 * 10 ** 7, 2 * 10 ** 6,
    )(in_vmem(kron), in_vmem(part), m2, m3, e0, e1)

    kept = call(
        prep_body,
        [VM, VM, HB, VM, HB, HB, ANY],
        [(pltpu.VMEM(d, t), VM) for d, t in (
            ((1024, 1024), BF), ((1024, 1024), BF), ((64, 256), BF), ((64, 256), BF), ((32, 256, 256), BF), ((64, 256), F32), ((64, 256), F32),
            ((256, 128), F32), ((256, 128), F32))],
        10 ** 8, 12 * 10 ** 6,
        [dma((4,))],
    )(in_vmem(columns_v), in_vmem(owners_v), in_hbm(interpolation), in_vmem(got), in_hbm(innovation), in_hbm(obs_weight), part)
    onehot, onehot_t, place_hi, place_lo, interp, innov, weight, innov_own, live_own = [in_vmem(a) for a in kept]

    (inc_my,) = call(
        add_body, [VM, VM, ANY], [(shape((8, 1024), BF), VM)], 10 ** 4, 10 ** 5,
    )(part, over(part, 2), place_hi)
    inc_mt = over(inc_my, 1)
    (m3,) = call(
        pass_body, [ANY, VM], [(pltpu.VMEM((128, 1024), BF), VM)], 0, 0, aliases={1: 0}
    )(inc_mt, m3)
    adj, image = call(
        obs_body, [VM] * 7 + [HB],
        [(shape((16, 1024), F32), VM), (pltpu.VMEM((64, 256), F32), VM)],
        10 ** 9, 12 * 10 ** 6,
        [pltpu.VMEM((64, 256), BF), pltpu.VMEM((64, 256), BF), pltpu.VMEM((64, 256), F32),
         pltpu.VMEM((32, 256, 256), BF), dma((8,))],
    )(inc_my, inc_mt, onehot, onehot_t, innov, weight, interp, in_hbm(interpolation))

    (slots,) = call(
        slots_body, [VM] * 3, [(pltpu.VMEM((256, 256), F32), VM)], 10 ** 7, 5 * 10 ** 5
    )(place_hi, place_lo, in_vmem(image))
    f_mt = over(e0, 1)
    o_mt = over(in_vmem(m3), 1)
    (terms,) = call(
        gradient_body, [VM] * 10, [(shape((32, 56), F32), VM)], 5 * 10 ** 8, 2 * 10 ** 6
    )(adj, over(adj, 1), m_my, m_mt, m2, o_mt, e0, e_mt, e1, f_mt)

    (sent,) = call(
        pack_body, [VM] * 2, [(shape((64, 16, 128), BF), VM)], 10 ** 5, 6 * 10 ** 5
    )(terms, in_vmem(slots))
    groups = [[(2 * z + core) * 32 + t for z in range(2) for t in range(32)] for core in range(2)]
    arrived = lax.all_to_all(
        sent, ("band", "mem"), split_axis=0, concat_axis=0, axis_index_groups=groups, tiled=True)
    gradient_t, departures = call(
        lambda *refs: final_body(scale, *refs), [VM] * 4,
        [(shape((16, 112), F32), VM), (shape((1, 256, 128), F32), VM)], 10 ** 6, 6 * 10 ** 5,
    )(arrived, control.T, innov_own, live_own)
    return (gradient_t.T, departures)


def solution(mesh):
    return jax.shard_map(
        per_device,
        mesh=mesh,
        in_specs=(
            P("band", None, "mem"),
            P("band", None, "mem"),
            P(),
            P("mem", None),
            P("mem", None, None),
            P(),
            P("mem", None, None),
            P("mem", None, None),
        ),
        out_specs=(P(None, "band"), P("mem", None, "band")),
        check_vma=False,
    )
```

```python
import math

import jax
import jax.numpy as jnp
from jax import lax
from jax.experimental import pallas as pl
from jax.experimental.pallas import tpu as pltpu
from jax.sharding import PartitionSpec as P

BF = jnp.bfloat16
F32 = jnp.float32
NN = (((1,), (0,)), ((), ()))
NT = (((1,), (1,)), ((), ()))
TN = (((0,), (0,)), ((), ()))
MIB = 1024 * 1024
VM = pl.BlockSpec(memory_space=pltpu.VMEM)
ANY = pl.BlockSpec(memory_space=pl.ANY)
HB = pl.BlockSpec(memory_space=pltpu.HBM)


def dot(a, b, dims=NN):
    return lax.dot_general(a, b, dims, preferred_element_type=F32)


def parts3(x):
    hi = x.astype(BF)
    rest = x - hi.astype(F32)
    mid = rest.astype(BF)
    lo = (rest - mid.astype(F32)).astype(BF)
    return hi, mid, lo


def iota(dims, dim):
    return lax.broadcasted_iota(jnp.int32, dims, dim)


def ones_where(cond):
    return cond.astype(F32).astype(BF)


def shape(dims, dtype):
    return jax.ShapeDtypeStruct(dims, dtype)


def in_hbm(x):
    return pltpu.with_memory_space_constraint(x, pltpu.HBM)


def in_vmem(x):
    return pltpu.with_memory_space_constraint(x, pltpu.VMEM)


def call(body, ins, outs, flops, nbytes, scratch=(), vmem=16, aliases=None):
    return pl.pallas_call(
        body,
        out_shape=tuple(o for o, _ in outs),
        in_specs=list(ins),
        out_specs=tuple(s for _, s in outs),
        scratch_shapes=list(scratch),
        input_output_aliases=aliases or {},
        compiler_params=pltpu.CompilerParams(vmem_limit_bytes=vmem * MIB),
        cost_estimate=pl.CostEstimate(flops=flops, bytes_accessed=nbytes, transcendentals=0),
    )


def start_all(copies):
    for c in copies:
        c.start()
    return copies


def wait_all(copies):
    for c in copies:
        c.wait()


def halves_copies(src, mine, mate, sem, at):
    core = lax.axis_index("band") & 1
    lo = pl.multiple_of(core * 8, 8)
    hi = pl.multiple_of(8 - core * 8, 8)
    return [
        pltpu.make_async_copy(src.at[:, pl.ds(hi, 8), :], mate, sem.at[at]),
        pltpu.make_async_copy(src.at[:, pl.ds(lo, 8), :], mine, sem.at[at + 1]),
    ]


def quarter_at(side):
    core = lax.axis_index("band") & 1
    return pl.ds(pl.multiple_of((core + 2 * side) * 128, 128), 128)


def split_body(mem, eig, m_mine, m_mate, e_mine, e_mate, sem):
    wait_all(start_all(halves_copies(mem, m_mine, m_mate, sem, 0) + halves_copies(eig, e_mine, e_mate, sem, 2)))


def load_body(innovation, obs_weight, _, payload, iv, sem):
    copies = start_all([
        pltpu.make_async_copy(
            a.at[0, :, quarter_at(side)], iv.at[n, :, side * 128:(side + 1) * 128], sem.at[2 * n + side])
        for n, a in enumerate((innovation, obs_weight)) for side in range(2)
    ])
    for n in range(2):
        wait_all(copies[2 * n:2 * n + 2])
        payload[:, n * 8:(n + 1) * 8, :] = iv[n].reshape(32, 8, 256).astype(BF)


def increment_of(scale, kron, ma, mb, ea, eb, cut):
    mixed = dot(kron, jnp.concatenate([ma[:, cut], mb[:, cut]], axis=0))
    total = jnp.sum((mixed[:224] * ea[:, cut].astype(F32)).reshape(28, 8, 256), axis=0)
    total = total + jnp.sum((mixed[224:] * eb[:, cut].astype(F32)).reshape(28, 8, 256), axis=0)
    return scale * total


def increment_own(scale, control_t, columns_t, owners, ma, mb, ea, eb, out, kron, columns_out, owners_out, ct, sem):
    get, *small = start_all([
        pltpu.make_async_copy(a, b, sem.at[n])
        for n, (a, b) in enumerate(((control_t, ct), (columns_t, columns_out), (owners, owners_out)))
    ])
    band = lax.axis_index("band")
    row = iota((448, 112), 0)
    second = (row >= 224).astype(jnp.int32)
    mode = (band ^ second) * 28 + ((row - 224 * second) >> 3)
    pick_rows = ones_where(mode == iota((448, 112), 1))
    col = iota((64, 512), 1)
    member = (band ^ (col >> 7)) * 16 + ((col & 127) >> 3)
    pick_cols = ones_where(member == iota((64, 512), 0))
    same = (iota((448, 512), 0) & 7) == (iota((448, 512), 1) & 7)
    get.wait()
    rows = dot(pick_rows, ct[...].astype(BF), NT).astype(BF)
    full = jnp.where(same, dot(rows, pick_cols), 0.0).astype(BF)
    kron[...] = full[:, 256:]
    for g in range(0, 1024, 256):
        cut = slice(g, g + 256)
        out[:, cut] = increment_of(scale, full[:, :256], ma, mb, ea, eb, cut)
    wait_all(small)


def increment_other(scale, kron, before, ma, mb, ea, eb, out):
    for g in range(0, 1024, 256):
        cut = slice(g, g + 256)
        out[:, cut] = before[:, cut] + increment_of(scale, kron[...], ma, mb, ea, eb, cut)


def prep_body(cols_s, own_s, interpolation, got_in, innovation, obs_weight, _,
              onehot, onehot_t, place_hi, place_lo, interp, innov, weight, innov_own, live_own, got, sem):
    band = lax.axis_index("band")
    tile = lax.axis_index("mem")
    quarter = pl.ds(pl.multiple_of(band * 128, 128), 128)
    mid = [(innovation.at[0, :, quarter], innov_own), (obs_weight.at[0, :, quarter], live_own)]
    big = [(interpolation.at[:32, :, quarter_at(side)], interp.at[:, :, side * 128:(side + 1) * 128]) for side in range(2)]
    copies = start_all([pltpu.make_async_copy(a, b, sem.at[n]) for n, (a, b) in enumerate([(got_in, got)] + mid + big)])
    t = iota((64, 1024), 1)
    cols = cols_s[...].astype(F32).T.astype(jnp.int32)
    for c in range(16):
        onehot[c * 64:(c + 1) * 64, :] = ones_where(cols[:, c:c + 1] == t)
    flat = jnp.concatenate([cols_s[c:c + 1, :] for c in range(16)], axis=1)
    for r in range(0, 1024, 128):
        onehot_t[r:r + 128, :] = ones_where(flat == iota((128, 1024), 0) + r)
    pair = own_s[pl.ds(tile >> 1, 1), :].astype(F32)
    own = jnp.where((tile & 1) == 1, pair[:, 64:], pair[:, :64])
    own_row = jnp.broadcast_to(own, (64, 64))
    own_col = own_row.T
    earlier = iota((64, 64), 1) < iota((64, 64), 0)
    rank = jnp.sum(jnp.where((own_row == own_col) & earlier, 1.0, 0.0), axis=1, keepdims=True)
    target = (own_col[:, :1] * 8.0 + rank).astype(jnp.int32)
    sel = ones_where(target == iota((64, 256), 1))
    slot = iota((64, 256), 1)
    half = 4 * (band >> 1)
    place_hi[...] = ones_where((target == slot + half) & ((slot & 7) < 4))
    place_lo[...] = ones_where((target == slot + half - 4) & ((slot & 7) >= 4))
    copies[0].wait()
    x = got[...].astype(F32)
    innov[...] = dot(sel, x[:, :8].reshape(256, 256).astype(BF))
    weight[...] = dot(sel, x[:, 8:].reshape(256, 256).astype(BF))
    hit = ones_where(own_s[...] == tile)
    pair = ones_where((iota((256, 16), 0) >> 4) == iota((256, 16), 1))
    odd = (iota((256, 128), 0) >> 3) & 1
    side = jnp.where((iota((256, 128), 1) >> 6) == odd, dot(pair, hit), 0.0)
    count = jnp.sum(side, axis=1, keepdims=True)
    live = jnp.where((iota((256, 1), 0) & 7).astype(F32) < count, 1.0, 0.0)
    wait_all(copies[1:3])
    live_own[...] = live * live_own[...]
    wait_all(copies[3:])


def add_body(a, b, _, out):
    out[...] = (a[...] + b[...]).astype(BF)


def pass_body(_, x, same_x):
    del x, same_x


def obs_body(inc_my, inc_mt, onehot, onehot_t, innov, weight, near, interpolation,
             adj_all, image_out, picked, depb, spread, far, sem):
    fetch = [
        start_all([
            pltpu.make_async_copy(
                interpolation.at[32 + j:40 + j, :, quarter_at(side)],
                far.at[j:j + 8, :, side * 128:(side + 1) * 128], sem.at[j // 4 + side])
            for side in range(2)
        ]) for j in range(0, 32, 8)
    ]

    def block(j):
        return near[j] if j < 32 else far[j - 32]

    band = lax.axis_index("band")
    first = (band & 1) == 0
    mine = inc_my[...].astype(F32)
    mate = inc_mt[...].astype(F32)
    inc = jnp.concatenate([jnp.where(first, mine, mate), jnp.where(first, mate, mine)], axis=0).astype(BF)
    r0 = iota((256, 256), 0)
    r1 = iota((256, 256), 1)
    swap = ones_where(((r0 & 15) * 16 + (r0 >> 4)) == r1)
    picks = dot(inc, onehot_t[...])
    by_col = jnp.concatenate([picks[:, c * 64:(c + 1) * 64] for c in range(16)], axis=0).astype(BF)
    picked[...] = dot(by_col, swap, TN).astype(BF)
    rows = iota((16, 256), 0)
    image = []
    for b in range(4):
        lhs = picked[b * 16:(b + 1) * 16, :]
        acc = jnp.zeros((16, 256), F32)
        for i in range(16):
            j = b * 16 + i
            if j >= 32 and j % 8 == 0:
                wait_all(fetch[(j - 32) // 8])
            acc = jnp.where(rows == i, dot(lhs, block(j)), acc)
        image.append(acc)
    image = jnp.concatenate(image, axis=0)
    image_out[...] = image
    dep = weight[...] * (innov[...] - image)
    depb[...] = dep.astype(BF)
    dep_t = dep.T.astype(BF)
    column = iota((256, 64), 1)
    odd = jnp.zeros((256, 64), F32)
    for b in range(4):
        lhs = depb[b * 16:(b + 1) * 16, :]
        acc = jnp.zeros((16, 256), F32)
        for i in range(16):
            j = b * 16 + i
            if j % 2:
                odd = jnp.where(column == j, dot(block(j), dep_t), odd)
            else:
                acc = jnp.where(rows == i, dot(lhs, block(j), NT), acc)
        spread[b * 16:(b + 1) * 16, :] = acc
    x = spread[...]
    hi, lo, _ = parts3(x)
    odd_hi, odd_lo, _ = parts3(odd)
    terms = []
    for part, odd_part in ((hi, odd_hi), (lo, odd_lo)):
        turned = dot(swap, part, NT) + dot(swap, odd_part)
        terms.append(jnp.concatenate([turned[c * 16:(c + 1) * 16] for c in range(16)], axis=1))
    both = dot(jnp.concatenate(terms, axis=0).astype(BF), onehot[...])
    adj = both[:16] + both[16:]
    adj_all[:8] = jnp.where(first, adj[8:], adj[:8])
    adj_all[8:] = jnp.where(first, adj[:8], adj[8:])


def slots_body(place_hi, place_lo, image, out):
    hi, lo, _ = parts3(image[...])
    out[...] = dot(place_hi[...], hi, TN) + dot(place_lo[...], lo, TN)


def gradient_body(adj, came, m_my, m_mt, o_my, o_mt, e_my, e_mt, f_my, f_mt, out):
    first = (lax.axis_index("band") & 1) == 0
    same = (iota((448, 256), 0) & 7) == (iota((448, 256), 1) & 7)
    sel = ones_where((iota((32, 256), 1) >> 3) == iota((32, 256), 0))
    total = None
    for here, there, members, eigs in (
            (adj[8:], came[:8], (m_my, o_my), (e_my, f_my)), (adj[:8], came[8:], (m_mt, o_mt), (e_mt, f_mt))):
        wide = jnp.broadcast_to((here + there)[None], (16, 8, 1024)).reshape(128, 1024)
        weighted = jnp.concatenate([(m[...].astype(F32) * wide).astype(BF) for m in members], axis=0)
        term = dot(jnp.concatenate([e[...] for e in eigs], axis=0), weighted, NT)
        total = term if total is None else total + term
    own = jnp.sum(jnp.where(same, total, 0.0).reshape(56, 8, 256), axis=1)
    own = jnp.where(first, own, jnp.concatenate([own[28:], own[:28]], axis=0))
    hi, mid, _ = parts3(own)
    out[...] = dot(sel, hi, NT) + dot(sel, mid, NT)


def pack_body(mine, slots, out):
    total = mine[...]
    gap = jnp.zeros((8, 8), F32)
    flat = [
        jnp.concatenate([total[r:r + 8], gap, total[r + 8:r + 16], gap], axis=1) for r in (0, 16)
    ]
    high = (lax.axis_index("band") >> 1) == 1
    for side in range(2):
        here = high if side else jnp.logical_not(high)
        term = jnp.broadcast_to(jnp.where(here, flat[0], flat[1])[None], (32, 8, 128))
        image = slots[:, side * 128:(side + 1) * 128].reshape(32, 8, 128)
        out[side * 32:(side + 1) * 32] = jnp.concatenate([term, image], axis=1).astype(BF)


def final_body(scale, got, control_t, innov, live, gradient_t, departures):
    band = lax.axis_index("band")
    sums, halves = [], []
    for side in range(2):
        x = got[side * 32:(side + 1) * 32].astype(F32)
        sums.append(jnp.sum(x[:, :8], axis=0))
        halves.append(x[:, 8:12] + x[:, 12:])
    image = jnp.concatenate(halves, axis=1).reshape(256, 128)
    departures[...] = (live[...] * (innov[...] - image)).reshape(1, 256, 128)
    low, top = sums
    total = jnp.concatenate([
        jnp.concatenate([low[:, :56], top[:, :56]], axis=1),
        jnp.concatenate([low[:, 64:120], top[:, 64:120]], axis=1),
    ], axis=0)
    own = ones_where(iota((16, 64), 1) == band * 16 + iota((16, 64), 0))
    hi, mid, lo = parts3(control_t[...])
    gradient_t[...] = dot(own, hi) + dot(own, mid) + dot(own, lo) - scale * total


def per_device(members, eigvecs, control, columns, interpolation, owners, innovation, obs_weight):
    scale = 1.0 / math.sqrt(112 * 64)
    owners = owners.reshape(16, 128)

    def over(x, bit):
        return lax.ppermute(x, "band", [(i, i ^ bit) for i in range(4)])

    dma = pltpu.SemaphoreType.DMA
    m_my, m_mt, e_my, e_mt = call(
        split_body, [HB] * 2,
        [(pltpu.VMEM((16, 8, 1024), BF), VM)] * 2 + [(pltpu.VMEM((28, 8, 1024), BF), VM)] * 2, 0, 0, [dma((4,))],
    )(in_hbm(members), in_hbm(eigvecs))
    m_my, m_mt, e0, e_mt = [in_vmem(a.reshape(-1, 1024)) for a in (m_my, m_mt, e_my, e_mt)]
    m3 = over(m_mt, 3)
    m2 = over(m_my, 2)
    m1 = over(m_mt, 1)
    (payload,) = call(
        load_body, [HB] * 2 + [ANY], [(pltpu.HBM((32, 16, 256), BF), VM)],
        0, 0, [pltpu.VMEM((2, 256, 256), F32), dma((4,))],
    )(in_hbm(innovation), in_hbm(obs_weight), m_my)
    got = lax.all_to_all(payload, "mem", split_axis=0, concat_axis=0, tiled=True)
    e1 = over(e_mt, 1)
    m1, m2, m3, e1 = [in_vmem(a) for a in (m1, m2, m3, e1)]

    part, kron, columns_v, owners_v = call(
        lambda *refs: increment_own(scale, *refs), [HB] * 3 + [VM] * 4,
        [(pltpu.VMEM((8, 1024), F32), VM), (pltpu.VMEM((448, 256), BF), VM),
         (pltpu.VMEM((16, 64), jnp.int32), VM), (pltpu.VMEM((16, 128), jnp.int32), VM)],
        25 * 10 ** 7, 2 * 10 ** 6, [pltpu.VMEM((64, 112), F32), dma((3,))],
    )(in_hbm(control.T), in_hbm(columns.T), in_hbm(owners), m_my, m1, e0, e1)
    (part,) = call(
        lambda *refs: increment_other(scale, *refs), [VM] * 6, [(shape((8, 1024), F32), VM)],
        25 * 10 ** 7, 2 * 10 ** 6,
    )(in_vmem(kron), in_vmem(part), m2, m3, e0, e1)

    kept = call(
        prep_body,
        [VM, VM, HB, ANY, HB, HB, ANY],
        [(pltpu.VMEM(d, t), VM) for d, t in (
            ((1024, 1024), BF), ((1024, 1024), BF), ((64, 256), BF), ((64, 256), BF), ((32, 256, 256), BF), ((64, 256), F32), ((64, 256), F32),
            ((256, 128), F32), ((256, 128), F32))],
        10 ** 8, 12 * 10 ** 6,
        [pltpu.VMEM((32, 16, 256), BF), dma((5,))],
    )(in_vmem(columns_v), in_vmem(owners_v), in_hbm(interpolation), got, in_hbm(innovation), in_hbm(obs_weight), part)
    onehot, onehot_t, place_hi, place_lo, interp, innov, weight, innov_own, live_own = [in_vmem(a) for a in kept]

    (inc_my,) = call(
        add_body, [VM, VM, ANY], [(shape((8, 1024), BF), VM)], 10 ** 4, 10 ** 5,
    )(part, over(part, 2), place_hi)
    inc_mt = over(inc_my, 1)
    (m3,) = call(
        pass_body, [ANY, VM], [(pltpu.VMEM((128, 1024), BF), VM)], 0, 0, aliases={1: 0}
    )(inc_mt, m3)
    adj, image = call(
        obs_body, [VM] * 7 + [HB],
        [(shape((16, 1024), F32), VM), (pltpu.VMEM((64, 256), F32), VM)],
        10 ** 9, 12 * 10 ** 6,
        [pltpu.VMEM((64, 256), BF), pltpu.VMEM((64, 256), BF), pltpu.VMEM((64, 256), F32),
         pltpu.VMEM((32, 256, 256), BF), dma((8,))],
    )(inc_my, inc_mt, onehot, onehot_t, innov, weight, interp, in_hbm(interpolation))

    (slots,) = call(
        slots_body, [VM] * 3, [(pltpu.VMEM((256, 256), F32), VM)], 10 ** 7, 5 * 10 ** 5
    )(place_hi, place_lo, in_vmem(image))
    f_mt = over(e0, 1)
    o_mt = over(in_vmem(m3), 1)
    (terms,) = call(
        gradient_body, [VM] * 10, [(shape((32, 56), F32), VM)], 5 * 10 ** 8, 2 * 10 ** 6
    )(adj, over(adj, 1), m_my, m_mt, m2, o_mt, e0, e_mt, e1, f_mt)

    (sent,) = call(
        pack_body, [VM] * 2, [(shape((64, 16, 128), BF), VM)], 10 ** 5, 6 * 10 ** 5
    )(terms, in_vmem(slots))
    groups = [[(2 * z + core) * 32 + t for z in range(2) for t in range(32)] for core in range(2)]
    arrived = lax.all_to_all(
        sent, ("band", "mem"), split_axis=0, concat_axis=0, axis_index_groups=groups, tiled=True)
    gradient_t, departures = call(
        lambda *refs: final_body(scale, *refs), [VM] * 4,
        [(shape((16, 112), F32), VM), (shape((1, 256, 128), F32), VM)], 10 ** 6, 6 * 10 ** 5,
    )(arrived, control.T, innov_own, live_own)
    return (gradient_t.T, departures)


def solution(mesh):
    return jax.shard_map(
        per_device,
        mesh=mesh,
        in_specs=(
            P("band", None, "mem"),
            P("band", None, "mem"),
            P(),
            P("mem", None),
            P("mem", None, None),
            P(),
            P("mem", None, None),
            P("mem", None, None),
        ),
        out_specs=(P(None, "band"), P("mem", None, "band")),
        check_vma=False,
    )
```
